128 devices in a mesh: rollout: 8 (over y, z_hi), tensor: 16 (over x, z_lo, core).
Axes of the slice: x: 4, y: 4, z: 4 (z_hi: 2, z_lo: 2; z = z_hi * 2 + z_lo), core: 2. Of those that a mesh axis runs over, the one named last changes fastest.
Arguments:
- hidden_in: bfloat16 [512, 8192], P('rollout'), may hold values from -6 to 6
- norm_gain: float32 [8192], replicated, may hold values from 0.25 to 1.75
- query_weight_base: bfloat16 [8192, 8192], P(None, 'tensor'), may hold values from -0.0625 to 0.0625
- w_key: bfloat16 [8192, 1024], P(None, 'tensor'), may hold values from -0.0625 to 0.0625
- w_value: bfloat16 [8192, 1024], P(None, 'tensor'), may hold values from -0.0625 to 0.0625
- output_weight_base: bfloat16 [8192, 8192], P('tensor'), may hold values from -0.0625 to 0.0625
- kv_cache: bfloat16 [512, 256, 2, 1024], P(('rollout', 'tensor'))
- cache_lengths: int32 [512], P(('rollout', 'tensor')), may hold values from 1 to 254, as said below
- adapter_shards: bfloat16 [128, 16384], P(('rollout', 'tensor')), may hold values from -0.111328125 to 0.111328125
- shard_order: int32 [128], replicated, may hold values from 0 to 127, each once
Outputs:
- decoded: bfloat16 [2, 512, 8192], P(None, 'rollout', 'tensor')
The draws below stay inside these ranges and needn't reach their ends.
Inputs may be any that keep to these rules, and one draw needn't show every extreme that they name: `cache_lengths`: row 0 has exactly 254 valid positions and row 1 has 1.
All inputs are finite; a program needn't handle non-finite values.
Results may differ from the reference program's by a relative error of at most 0.019.
Values may be sent and summed in bfloat16 or wider, within the bound.
A program may use at most 128 MiB of HBM per device.

```python
import jax
import jax.numpy as jnp
from jax import lax

D = 8192
HEADS = 64
KV_HEADS = 8
HEAD_DIM = 128
RANK = 64
STEPS = 2
CAP = 256
ROWS = 512
PIECE = 16384
DEVICES = 128


def draw_kv_cache(key, part):
    key = jax.random.fold_in(key, 11)
    array_shape = (ROWS, CAP, 2, KV_HEADS * HEAD_DIM)
    values = jax.random.normal(key, array_shape, jnp.float32)
    return values.astype(jnp.bfloat16)


def draw_cache_lengths(key, part):
    key = jax.random.fold_in(key, 23)
    drawn = jax.random.randint(key, (ROWS,), 1, CAP - 1)
    drawn = drawn.at[0].set(CAP - 2).at[1].set(1)
    return drawn.astype(jnp.int32)


def shard_levels(own_key, extent, shards, least, high):
    factor_of, own = 1.0, jax.random.fold_in(own_key, 6)
    for dim, blocks in shards:
        steps = jnp.exp(jax.random.uniform(jax.random.fold_in(own, dim), (blocks,), jnp.float32, least / len(shards), high / len(shards)))
        factor_of = factor_of * jnp.repeat(steps, extent[dim] // blocks).reshape([-1 if axis == dim else 1 for axis in range(len(extent))])
    return factor_of


def bell_draw(rng, extent, spread, reach, shards=(), kind=jnp.bfloat16):
    array = spread * jax.random.normal(rng, extent, jnp.float32)
    if shards:
        array = array * shard_levels(rng, extent, shards, -0.22, 0.18)
    return jnp.clip(array, -reach, reach).astype(kind)


def setup_inputs(seed: int = 0) -> dict:
    arg_keys = jax.random.split(jax.random.key(seed), 11)
    hidden_in = bell_draw(arg_keys[0], (ROWS, D), 1.0, 6.0, ((0, 8),))
    norm_gain = jnp.clip(1.0 + 0.15 * jax.random.normal(arg_keys[1], (D,), jnp.float32), 0.25, 1.75)
    query_weight_base = bell_draw(arg_keys[2], (D, D), D ** -0.5, 0.0625, ((1, 16),))
    w_key = bell_draw(arg_keys[3], (D, KV_HEADS * HEAD_DIM), D ** -0.5, 0.0625, ((1, 16),))
    w_value = bell_draw(arg_keys[4], (D, KV_HEADS * HEAD_DIM), D ** -0.5, 0.0625, ((1, 16),))
    output_weight_base = bell_draw(arg_keys[5], (D, D), D ** -0.5, 0.0625, ((0, 16),))
    kv_cache = draw_kv_cache(jax.random.fold_in(arg_keys[10], 71), 0)
    cache_lengths = draw_cache_lengths(jax.random.fold_in(arg_keys[10], 71), 0)
    adapter_shards = bell_draw(arg_keys[8], (DEVICES, PIECE), (0.5 / (D * RANK) ** 0.25), 0.111328125, ((0, 128),))
    shard_order = jax.random.permutation(arg_keys[9], DEVICES).astype(jnp.int32)
    return {"hidden_in": hidden_in, "norm_gain": norm_gain, "query_weight_base": query_weight_base, "w_key": w_key, "w_value": w_value, "output_weight_base": output_weight_base, "kv_cache": kv_cache, "cache_lengths": cache_lengths, "adapter_shards": adapter_shards, "shard_order": shard_order}


low_rank_scale = 2.0
norm_epsilon = 1e-05
rope_theta = 500000.0

def rotate(vectors, positions):
    half_dim = HEAD_DIM // 2
    exponent = jnp.arange(half_dim, dtype=jnp.float32) * (2.0 / HEAD_DIM)
    frequency = jnp.float32(rope_theta) ** (-exponent)
    angles = positions.astype(jnp.float32)[:, None, None] * frequency[None, None, :]
    cosine = jnp.cos(angles)
    sine = jnp.sin(angles)
    front_part = vectors[..., :half_dim]
    back_part = vectors[..., half_dim:]
    return jnp.concatenate([front_part * cosine - back_part * sine, back_part * cosine + front_part * sine], axis=-1)

def attend_row(query_row, cache_row, length_row, keys_new, values_new):
    groups = HEADS // KV_HEADS
    query_f = query_row.astype(jnp.float32).reshape(KV_HEADS, groups, HEAD_DIM)
    past_keys = cache_row[:, 0].astype(jnp.float32).reshape(CAP, KV_HEADS, HEAD_DIM)
    past_values = cache_row[:, 1].astype(jnp.float32).reshape(CAP, KV_HEADS, HEAD_DIM)
    score_scale = 1.0 / jnp.sqrt(jnp.float32(HEAD_DIM))
    past_scores = jnp.einsum('kgd,pkd->kgp', query_f, past_keys) * score_scale
    visible = jnp.arange(CAP) < length_row
    past_scores = jnp.where(visible[None, None, :], past_scores, jnp.float32(-1e+30))
    fresh_scores = jnp.einsum('kgd,skd->kgs', query_f, keys_new.astype(jnp.float32)) * score_scale
    scores = jnp.concatenate([past_scores, fresh_scores], axis=-1)
    largest = lax.optimization_barrier(jnp.max(scores, axis=-1, keepdims=True))
    expo = jnp.exp(scores - largest)
    weights = (expo / lax.optimization_barrier(jnp.sum(expo, axis=-1, keepdims=True))).astype(jnp.bfloat16).astype(jnp.float32)
    attended = jnp.einsum('kgp,pkd->kgd', weights[..., :CAP], past_values)
    attended = attended + jnp.einsum('kgs,skd->kgd', weights[..., CAP:], values_new.astype(jnp.float32))
    return attended.reshape(HEADS * HEAD_DIM).astype(jnp.bfloat16)

def reference(hidden_in, norm_gain, query_weight_base, w_key, w_value, output_weight_base, kv_cache, cache_lengths, adapter_shards, shard_order):
    ordered = jnp.zeros_like(adapter_shards).at[shard_order].set(adapter_shards)
    flattened = ordered.reshape(4, D * RANK)
    query_down_factor = flattened[0].reshape(D, RANK)
    query_up_factor = flattened[1].reshape(RANK, D)
    output_down_factor = flattened[2].reshape(D, RANK)
    output_up_factor = flattened[3].reshape(RANK, D)
    combined_query_weight = (query_weight_base.astype(jnp.float32) + low_rank_scale * jnp.dot(query_down_factor, query_up_factor, preferred_element_type=jnp.float32)).astype(jnp.bfloat16)
    combined_output_weight = (output_weight_base.astype(jnp.float32) + low_rank_scale * jnp.dot(output_down_factor, output_up_factor, preferred_element_type=jnp.float32)).astype(jnp.bfloat16)
    stream = hidden_in
    keys_list = []
    values_list = []
    results = []
    for step_index in range(STEPS):
        stream_f = stream.astype(jnp.float32)
        normed = (stream_f * lax.rsqrt(lax.optimization_barrier(jnp.mean(stream_f * stream_f, axis=-1, keepdims=True)) + norm_epsilon) * norm_gain).astype(jnp.bfloat16)
        query = jnp.dot(normed, combined_query_weight, preferred_element_type=jnp.float32).astype(jnp.bfloat16)
        key_new = jnp.dot(normed, w_key, preferred_element_type=jnp.float32).astype(jnp.bfloat16)
        value_new = jnp.dot(normed, w_value, preferred_element_type=jnp.float32).astype(jnp.bfloat16)
        positions = cache_lengths + step_index
        query_rot = rotate(query.astype(jnp.float32).reshape(ROWS, HEADS, HEAD_DIM), positions).astype(jnp.bfloat16)
        key_rot = rotate(key_new.astype(jnp.float32).reshape(ROWS, KV_HEADS, HEAD_DIM), positions).astype(jnp.bfloat16)
        keys_list.append(key_rot)
        values_list.append(value_new.reshape(ROWS, KV_HEADS, HEAD_DIM))
        keys_all = jnp.stack(keys_list, axis=1)
        values_all = jnp.stack(values_list, axis=1)
        attended = lax.map(lambda packed: attend_row(*packed), (query_rot, kv_cache, cache_lengths, keys_all, values_all))
        projected = jnp.dot(attended, combined_output_weight, preferred_element_type=jnp.float32)
        stream = (stream.astype(jnp.float32) + projected).astype(jnp.bfloat16)
        results.append(stream)
    return jnp.stack(results, axis=0)
```

```python
import jax
import jax.numpy as jnp
from jax import lax
from jax.sharding import PartitionSpec as P

D = 8192
HEADS = 64
KV_HEADS = 8
HEAD_DIM = 128
RANK = 64
STEPS = 2


low_rank_scale = 2.0
norm_epsilon = 1e-05
rope_theta = 500000.0


def rotate(vectors, positions):
    half_dim = HEAD_DIM // 2
    exponent = jnp.arange(half_dim, dtype=jnp.float32) * (2.0 / HEAD_DIM)
    frequency = jnp.float32(rope_theta) ** (-exponent)
    angles = positions.astype(jnp.float32)[:, None, None] * frequency[None, None, :]
    cosine = jnp.cos(angles)
    sine = jnp.sin(angles)
    front_part = vectors[..., :half_dim]
    back_part = vectors[..., half_dim:]
    return jnp.concatenate(
        [front_part * cosine - back_part * sine, back_part * cosine + front_part * sine], axis=-1
    )


def attend_local(query_rot, kv_cache, cache_lengths, keys_all, values_all):
    row_count = query_rot.shape[0]
    capacity = kv_cache.shape[1]
    groups = HEADS // KV_HEADS
    query_heads = query_rot.reshape(row_count, KV_HEADS, groups, HEAD_DIM)
    past_keys = kv_cache[:, :, 0].reshape(row_count, capacity, KV_HEADS, HEAD_DIM)
    past_values = kv_cache[:, :, 1].reshape(row_count, capacity, KV_HEADS, HEAD_DIM)
    score_scale = 1.0 / jnp.sqrt(jnp.float32(HEAD_DIM))
    past_scores = (
        jnp.einsum("rkgd,rpkd->rkgp", query_heads, past_keys, preferred_element_type=jnp.float32)
        * score_scale
    )
    visible = jnp.arange(capacity)[None, :] < cache_lengths[:, None]
    past_scores = jnp.where(visible[:, None, None, :], past_scores, jnp.float32(-1e30))
    fresh_scores = (
        jnp.einsum("rkgd,rskd->rkgs", query_heads, keys_all, preferred_element_type=jnp.float32)
        * score_scale
    )
    scores = jnp.concatenate([past_scores, fresh_scores], axis=-1)
    largest = jnp.max(scores, axis=-1, keepdims=True)
    expo = jnp.exp(scores - largest)
    weights = (expo / jnp.sum(expo, axis=-1, keepdims=True)).astype(jnp.bfloat16)
    attended = jnp.einsum(
        "rkgp,rpkd->rkgd", weights[..., :capacity], past_values, preferred_element_type=jnp.float32
    )
    attended = attended + jnp.einsum(
        "rkgs,rskd->rkgd", weights[..., capacity:], values_all, preferred_element_type=jnp.float32
    )
    return attended.reshape(row_count, HEADS * HEAD_DIM).astype(jnp.bfloat16)


def body(
    hidden_in,
    norm_gain,
    query_weight_base,
    w_key,
    w_value,
    output_weight_base,
    kv_cache,
    cache_lengths,
    adapter_shards,
    shard_order,
):
    tensor_rank = lax.axis_index("tensor")
    me = lax.axis_index("rollout") * 16 + tensor_rank
    piece = adapter_shards.reshape(16384)
    is_up = lax.rem(shard_order[me] // 32, 2) == 1
    chunks = jnp.where(
        is_up,
        piece.reshape(2, 16, 512).transpose(1, 0, 2).reshape(16, 1024),
        piece.reshape(16, 1024),
    )
    outgoing = jnp.broadcast_to(chunks[None], (8, 16, 1024)).reshape(128, 1024)
    everything = lax.all_to_all(
        outgoing, ("rollout", "tensor"), split_axis=0, concat_axis=0, tiled=True
    )
    ordered = jnp.zeros_like(everything).at[shard_order].set(everything).reshape(4, 32, 1024)
    query_up_factor_local = ordered[1].reshape(RANK, 512)
    shared = jnp.stack([ordered[0], ordered[3]])
    shared = jnp.broadcast_to(shared[None], (16, 2, 32, 1024))
    shared = lax.all_to_all(shared, "tensor", split_axis=0, concat_axis=0, tiled=True)
    query_down_factor = shared[:, 0].transpose(1, 0, 2).reshape(D, RANK)
    output_up_factor = shared[:, 1].reshape(16, RANK, 512).transpose(1, 0, 2).reshape(RANK, D)
    down = ordered[2].reshape(16, 2, 1024)
    down = lax.all_to_all(down, "tensor", split_axis=0, concat_axis=0, tiled=True)
    output_down_factor_local = down.transpose(1, 0, 2).reshape(512, RANK)
    combined_query_weight = (
        query_weight_base.astype(jnp.float32)
        + low_rank_scale
        * jnp.dot(query_down_factor, query_up_factor_local, preferred_element_type=jnp.float32)
    ).astype(jnp.bfloat16)
    combined_output_weight = (
        output_weight_base.astype(jnp.float32)
        + low_rank_scale
        * jnp.dot(output_down_factor_local, output_up_factor, preferred_element_type=jnp.float32)
    ).astype(jnp.bfloat16)
    feature_cols = D // lax.axis_size("tensor")
    stream = hidden_in
    own = lax.dynamic_slice_in_dim(stream, tensor_rank * feature_cols, feature_cols, 1)
    keys_list = []
    values_list = []
    results = []
    for step_index in range(STEPS):
        stream_f = stream.astype(jnp.float32)
        normed = (
            stream_f
            * lax.rsqrt(jnp.mean(stream_f * stream_f, axis=-1, keepdims=True) + norm_epsilon)
            * norm_gain
        ).astype(jnp.bfloat16)
        query = jnp.dot(normed, combined_query_weight, preferred_element_type=jnp.float32).astype(
            jnp.bfloat16
        )
        key_new = jnp.dot(normed, w_key, preferred_element_type=jnp.float32).astype(jnp.bfloat16)
        value_new = jnp.dot(normed, w_value, preferred_element_type=jnp.float32).astype(
            jnp.bfloat16
        )
        query_rows, key_rows, value_rows = (
            lax.all_to_all(query, "tensor", split_axis=0, concat_axis=1, tiled=True),
            lax.all_to_all(key_new, "tensor", split_axis=0, concat_axis=1, tiled=True),
            lax.all_to_all(value_new, "tensor", split_axis=0, concat_axis=1, tiled=True),
        )
        row_count = query_rows.shape[0]
        positions = cache_lengths + step_index
        query_rot = rotate(
            query_rows.astype(jnp.float32).reshape(row_count, HEADS, HEAD_DIM), positions
        ).astype(jnp.bfloat16)
        key_rot = rotate(
            key_rows.astype(jnp.float32).reshape(row_count, KV_HEADS, HEAD_DIM), positions
        ).astype(jnp.bfloat16)
        keys_list.append(key_rot)
        values_list.append(value_rows.reshape(row_count, KV_HEADS, HEAD_DIM))
        keys_all = jnp.stack(keys_list, axis=1)
        values_all = jnp.stack(values_list, axis=1)
        attended = attend_local(query_rot, kv_cache, cache_lengths, keys_all, values_all)
        head_block = lax.all_to_all(attended, "tensor", split_axis=1, concat_axis=0, tiled=True)
        projected = jnp.dot(head_block, combined_output_weight, preferred_element_type=jnp.float32)
        parts = projected.reshape(64, 16, 512).transpose(1, 0, 2)
        parts = lax.all_to_all(parts, "tensor", split_axis=0, concat_axis=0, tiled=True)
        own = (own.astype(jnp.float32) + jnp.sum(parts, axis=0)).astype(jnp.bfloat16)
        results.append(own)
        if step_index + 1 < STEPS:
            spread = jnp.broadcast_to(own[None], (16,) + own.shape)
            spread = lax.all_to_all(spread, "tensor", split_axis=0, concat_axis=0, tiled=True)
            stream = spread.transpose(1, 0, 2).reshape(64, D)
    return jnp.stack(results, axis=0)


def solution(mesh):
    return jax.shard_map(
        body,
        mesh=mesh,
        in_specs=(
            P("rollout", None),
            P(),
            P(None, "tensor"),
            P(None, "tensor"),
            P(None, "tensor"),
            P("tensor", None),
            P(("rollout", "tensor"), None, None, None),
            P(("rollout", "tensor")),
            P(("rollout", "tensor"), None),
            P(),
        ),
        out_specs=P(None, "rollout", "tensor"),
        check_vma=False,
    )
```

```python
import jax
import jax.numpy as jnp
import numpy as np
from jax import lax
from jax.experimental import pallas as pl
from jax.experimental.pallas import tpu as pltpu
from jax.sharding import PartitionSpec as P

D = 8192
HEADS = 64
KV_HEADS = 8
HEAD_DIM = 128
RANK = 64
STEPS = 2
CAP = 256
T = 16
R = 8
CHUNK = D // T

low_rank_scale = 2.0
norm_epsilon = 1e-05
rope_theta = 500000.0
score_scale = 1.0 / np.sqrt(np.float32(HEAD_DIM))

f32 = jnp.float32
bf16 = jnp.bfloat16
MESH = pl.DeviceIdType.MESH


def mm(a, b):
    return jnp.dot(a, b, preferred_element_type=f32)


def mm_t(a, b):
    return lax.dot_general(a, b, (((1,), (1,)), ((), ())), preferred_element_type=f32)


def lanes(shape):
    return lax.broadcasted_iota(jnp.int32, shape, len(shape) - 1)


def swap_halves(x):
    return pltpu.roll(x, 64, len(x.shape) - 1)


def spread_pairs(x, ref):
    low = lanes(x.shape) < 64
    rows = x.shape[0]
    ref[pl.ds(0, rows, stride=2), :] = jnp.where(low, x, 0.0)
    ref[pl.ds(1, rows, stride=2), :] = jnp.where(low, swap_halves(x), 0.0)


def pack_rank(t):
    return t[0:32] + swap_halves(t[32:64])


def unpack_split(total):
    high = total.astype(bf16).astype(f32)
    rest = total - high
    low = lanes(total.shape) < 64
    top = jnp.where(low, high, swap_halves(rest))
    bottom = jnp.where(low, swap_halves(high), rest)
    return jnp.concatenate([top, bottom], axis=0).astype(bf16)


def kernel(
    hid, gain, wq, wk_t, wv_t, wo, kv, lens, freq, piece, order,
    out,
    WQ, WKV, WO, KV, HF, ST0, ST1, NB,
    CP, A1R, A2S, A2R, XF, OF, AE, AP, BQ, BO, AOS, AOR, AOE, AO,
    TS, TR, Q32, QS, QR, QX, KN, VN, AF, AM, AR, AT, TOS, TOR, RSS, RB, OUTF,
    lsem, wosem, a1sem, a2sem, aosem, tsem, qsem, asem, tosem, rssem, agdsem, agfsem, agssem,
):
    me = lax.axis_index("tensor")
    ro = lax.axis_index("rollout")
    core = lax.rem(me, 2)
    chip = me // 2
    sib = me + 1 - 2 * core

    def wait(ref, sem):
        pltpu.make_async_copy(ref, ref, sem).wait()

    def tensor_copy(src, dst, send, recv, peer):
        return pltpu.make_async_remote_copy(
            src_ref=src, dst_ref=dst, send_sem=send, recv_sem=recv,
            device_id={"tensor": peer}, device_id_type=MESH,
        )

    def loop(lo, hi, body):
        def step(k, carry):
            body(k)
            return carry
        lax.fori_loop(lo, hi, step, 0)

    barrier = pltpu.get_barrier_semaphore()
    loop(1, T, lambda k: pl.semaphore_signal(
        barrier, inc=1, device_id={"tensor": lax.rem(me + k, T)}, device_id_type=MESH))
    loop(1, R, lambda k: pl.semaphore_signal(
        barrier, inc=1, device_id={"rollout": lax.rem(ro + k, R)}, device_id_type=MESH))

    for j in range(T):
        pltpu.make_async_copy(wq.at[pl.ds(CHUNK * j, CHUNK), :], WQ.at[j], lsem.at[j]).start()
    pltpu.make_async_copy(wk_t, WKV.at[pl.ds(0, 64), :], lsem.at[16]).start()
    pltpu.make_async_copy(wv_t, WKV.at[pl.ds(64, 64), :], lsem.at[17]).start()
    for i in range(4):
        for g in range(KV_HEADS):
            pltpu.make_async_copy(
                kv.at[i, :, :, pl.ds(HEAD_DIM * g, HEAD_DIM)], KV.at[i, g], lsem.at[19]).start()

    def wo_columns(q, parity):
        return wo.at[:, pl.ds(pl.multiple_of((2 * q + parity) * CHUNK, CHUNK), CHUNK)]

    wo_rows = pl.ds(pl.multiple_of(core * CHUNK, CHUNK), CHUNK)
    loop(0, 8, lambda q: pltpu.make_async_copy(
        wo_columns(q, core), WO.at[q, wo_rows, :], lsem.at[18]).start())

    order_row = order[...]
    mine = jnp.sum(
        jnp.where(lanes((1, 128)) == ro * T + me, order_row, 0), axis=1, keepdims=True)
    is_up = jnp.broadcast_to((mine >> 5) & 1, (128, 128))
    row = lax.broadcasted_iota(jnp.int32, (128, 128), 0)
    up_row = 64 * ((row >> 2) & 1) + 4 * (row >> 3) + (row & 3)
    wanted = jnp.where(is_up == 1, up_row, row)
    pick = jnp.where(lanes((128, 128)) == wanted, 1.0, 0.0).astype(bf16)
    CP[...] = mm(pick, piece[...]).astype(bf16)
    A1R[ro] = CP[...]
    place = jnp.where(row == jnp.broadcast_to(order_row, (128, 128)), 1.0, 0.0).astype(bf16)

    pl.semaphore_wait(barrier, T - 1 + R - 1)

    loop(1, R, lambda k: pltpu.make_async_remote_copy(
        src_ref=CP, dst_ref=A1R.at[ro], send_sem=a1sem.at[0], recv_sem=a1sem.at[1],
        device_id={"rollout": lax.rem(ro + k, R)}, device_id_type=MESH).start())
    loop(0, 8, lambda q: tensor_copy(
        wo_columns(q, 1 - core), WO.at[q, wo_rows, :], wosem.at[0], wosem.at[1], sib).start())

    def permute_hidden(j):
        for c in range(4):
            at = pl.multiple_of(CHUNK * j + 128 * c, 128)
            HF[c] = hid[:, pl.ds(at, 128)].astype(f32)
        for c in range(4):
            for i in range(4):
                ST0[j, 16 * i:16 * i + 16, 128 * c:128 * c + 128] = (
                    HF[c, pl.ds(i, 16, stride=4), :].astype(bf16))
    loop(0, T, permute_hidden)

    AP[...] = jnp.zeros_like(AP)
    Q32[320:512, :] = jnp.zeros((192, 128), f32)

    def square_sum(ST, j, total):
        x = ST[j].astype(f32)
        x = x * x
        return total + (x[:, 0:128] + x[:, 128:256]) + (x[:, 256:384] + x[:, 384:512])

    def normalize(ST, total):
        inv = lax.rsqrt(jnp.sum(total, axis=1, keepdims=True) * (1.0 / D) + norm_epsilon)
        def body(j):
            NB[j] = (ST[j].astype(f32) * inv * gain[j]).astype(bf16)
        loop(0, T, body)

    zero_total = jnp.zeros((64, 128), f32)
    normalize(ST0, lax.fori_loop(0, T, lambda j, t: square_sum(ST0, j, t), zero_total))

    wait(A1R.at[pl.ds(0, R - 1)], a1sem.at[1])
    for r in range(R):
        held = A1R[r].astype(f32).reshape(T, 8, 128)
        OF[:, 8 * r:8 * r + 8, :] = held
    A2S[...] = OF[...].astype(bf16)
    loop(1, T, lambda k: tensor_copy(
        A2S.at[lax.rem(me + k, T)], A2R.at[me], a2sem.at[0], a2sem.at[1],
        lax.rem(me + k, T)).start())
    A2R[me] = A2S[me]
    wait(A2R.at[pl.ds(0, T - 1)], a2sem.at[1])

    arrived = A2R[...].astype(f32).reshape(T, R, 8, 128)
    for r in range(R):
        XF[128 * r:128 * r + 128, :] = arrived[:, r].reshape(128, 128)
    FL = AOE
    for s in range(8):
        FL[pl.ds(s, 128, stride=8), :] = mm(place, XF[pl.ds(s, 128, stride=8), :].astype(bf16))
    spread_pairs(FL[0:256, :], AE)
    for b in range(32):
        AP[b, pl.ds(pl.multiple_of(16 * me, 16), 16), :] = AE[16 * b:16 * b + 16, :].astype(bf16)
    for c in range(4):
        up = FL[pl.ds(256 + c, 64, stride=4), :].astype(bf16)
        BQ[0:64, 128 * c:128 * c + 128] = up
        BQ[64:128, 128 * c:128 * c + 128] = up
        up = FL[pl.ds(768 + c, 64, stride=4), :].astype(bf16)
        BO[0:64, 128 * c:128 * c + 128] = up
        BO[64:128, 128 * c:128 * c + 128] = up
    AOS[...] = FL[512:768, :].astype(bf16).reshape(8, 32, 128)

    def send_rank(s):
        def body(j, acc):
            return acc + mm(NB[j], AP[pl.ds(2 * j, 2)].reshape(CHUNK, 128))
        t = lax.fori_loop(0, T, body, zero_total)
        TS[s] = pack_rank(t).astype(bf16)
        loop(1, T, lambda k: tensor_copy(
            TS.at[s], TR.at[s, me], tsem.at[s, 0], tsem.at[s, 1], lax.rem(me + k, T)).start())
        TR[s, me] = TS[s]

    send_rank(0)
    loop(1, T, lambda k: tensor_copy(
        AOS.at[lax.rem(me + k, T) // 2], AOR.at[me], aosem.at[0], aosem.at[1],
        lax.rem(me + k, T)).start())
    AOR[me] = AOS[chip]

    low_half = lanes((8, 128)) < 64
    sub = lax.broadcasted_iota(jnp.int32, (8, 128), 0) & 3
    lengths = jnp.zeros((8, 128), jnp.int32)
    for i in range(4):
        lengths = jnp.where(sub == i, lens[i], lengths)
    wide = lanes((64, 2 * CAP))

    for s in range(STEPS):
        if s == 0:
            wait(WKV.at[pl.ds(0, 64), :], lsem.at[16])
            wait(WKV.at[pl.ds(64, 64), :], lsem.at[17])

        def project(j, carry):
            q, n = carry
            if s == 0:
                wait(WQ.at[j], lsem.at[j])
            x = NB[j]
            q = q + mm(x, WQ[j])
            n = n + mm_t(x, WKV[:, pl.ds(pl.multiple_of(CHUNK * j, CHUNK), CHUNK)])
            return q, n

        q, new = lax.fori_loop(0, T, project, (jnp.zeros((64, CHUNK), f32), zero_total))
        wait(TR.at[s, pl.ds(0, T - 1)], tsem.at[s, 1])
        rank = jnp.sum(TR[s].astype(f32), axis=0)
        q = q + low_rank_scale * mm(unpack_split(rank), BQ[...])
        for h in range(4):
            Q32[64 * h:64 * h + 64, :] = q[:, 128 * h:128 * h + 128]
        Q32[256:320, :] = new
        for t in range(T):
            QS[s, t] = Q32[pl.ds(t, 32, stride=16), :].astype(bf16)
        loop(1, T, lambda k: tensor_copy(
            QS.at[s, lax.rem(me + k, T)], QR.at[s, me], qsem.at[s, 0], qsem.at[s, 1],
            lax.rem(me + k, T)).start())
        QR[s, me] = QS[s, me]

        angles = (lengths + s).astype(f32) * freq[...]
        cosine = jnp.cos(angles)
        sine = jnp.where(low_half, -jnp.sin(angles), jnp.sin(angles))

        if s == 0:
            wait(AOR.at[pl.ds(0, T - 1)], aosem.at[1])
            blocks = AOR[...].astype(f32).reshape(T, 4, 8, 128)
            for b in range(4):
                XF[128 * b:128 * b + 128, :] = blocks[:, b].reshape(128, 128)
            spread_pairs(XF[0:512, :], AOE)
            AO[...] = AOE[...].astype(bf16)

        wait(QR.at[s, pl.ds(0, T - 1)], qsem.at[s, 1])
        got = QR[s].astype(f32)
        heads = got[:, 0:16].reshape(T, 2, 8, 128)
        heads = heads * cosine + swap_halves(heads) * sine
        QX[...] = heads.astype(bf16).astype(f32).reshape(256, 128)
        fresh = got[:, 16:24].reshape(8, 2, 8, 128)
        even, odd = fresh[:, 0], fresh[:, 1]
        low = lanes(even.shape) < 64
        key = jnp.where(low, even, swap_halves(odd))
        key = key * cosine + swap_halves(key) * sine
        KN[s] = key.astype(bf16).astype(f32).reshape(64, 128)
        VN[s] = jnp.where(low, swap_halves(even), odd).reshape(64, 128)

        if s == 0:
            wait(KV, lsem.at[19])

        def attend(i):
            queries = [QX[pl.ds(32 * g + i, 8, stride=4), :] for g in range(KV_HEADS)]
            scores = jnp.concatenate(
                [mm_t(queries[g].astype(bf16), KV[i, g].reshape(2 * CAP, HEAD_DIM))
                 for g in range(KV_HEADS)], axis=0) * score_scale
            seen = ((wide & 1) == 0) & (wide < 2 * lens[i])
            scores = jnp.where(seen, scores, -1e30)
            rows = jnp.concatenate(queries, axis=0)
            largest = jnp.max(scores, axis=1, keepdims=True)
            news, values = [], []
            for n in range(s + 1):
                k = KN[n, pl.ds(i, 8, stride=8), :]
                v = VN[n, pl.ds(i, 8, stride=8), :]
                k = jnp.broadcast_to(k[:, None, :], (8, 8, 128)).reshape(64, 128)
                values.append(jnp.broadcast_to(v[:, None, :], (8, 8, 128)).reshape(64, 128))
                news.append(jnp.sum(rows * k, axis=1, keepdims=True) * score_scale)
                largest = jnp.maximum(largest, news[-1])
            expo = jnp.exp(scores - largest)
            news = [jnp.exp(x - largest) for x in news]
            total = jnp.sum(expo, axis=1, keepdims=True)
            for x in news:
                total = total + x
            weights = pltpu.roll((expo / total).astype(bf16).astype(f32), 1, 1).astype(bf16)
            result = jnp.concatenate(
                [mm(weights[8 * g:8 * g + 8], KV[i, g].reshape(2 * CAP, HEAD_DIM))
                 for g in range(KV_HEADS)], axis=0)
            for x, v in zip(news, values):
                result = result + (x / total).astype(bf16).astype(f32) * v
            AF[pl.ds(i, 64, stride=4), :] = result

        for i in range(4):
            attend(i)
        AM[s] = AF[...].astype(bf16).reshape(8, 32, 128)
        loop(1, T, lambda k: tensor_copy(
            AM.at[s, lax.rem(me + k, T) // 2], AR.at[s, me], asem.at[s, 0], asem.at[s, 1],
            lax.rem(me + k, T)).start())
        AR[s, me] = AM[s, chip]
        wait(AR.at[s, pl.ds(0, T - 1)], asem.at[s, 1])
        XF[0:512, :] = AR[s].astype(f32).reshape(512, 128)
        for h in range(8):
            for i in range(4):
                AT[16 * i:16 * i + 16, 128 * h:128 * h + 128] = (
                    XF[pl.ds(4 * h + i, 16, stride=32), :].astype(bf16))

        attended = AT[...]
        t = mm(attended, AO[...])
        TOS[s] = pack_rank(t).astype(bf16)
        loop(1, 8, lambda k: tensor_copy(
            TOS.at[s], TOR.at[s, chip], tosem.at[s, 0], tosem.at[s, 1],
            lax.rem(me + 2 * k, T)).start())
        TOR[s, chip] = TOS[s]
        if s == 0:
            wait(WO.at[:, pl.ds(0, CHUNK), :], lsem.at[18])
            wait(WO.at[:, pl.ds(0, CHUNK), :], wosem.at[1])

        def part(k):
            q = lax.rem(chip + k, 8)
            RSS[s, q] = mm(AT[...], WO[q]).astype(bf16)
            tensor_copy(
                RSS.at[s, q], RB.at[s, chip], rssem.at[s, 0], rssem.at[s, 1],
                2 * q + core).start()
        loop(1, 8, part)
        RB[s, chip] = jnp.zeros((64, CHUNK), bf16)
        y = mm(attended, WO[chip])
        y = y + (ST0 if s == 0 else ST1)[me].astype(f32)
        wait(TOR.at[s, pl.ds(0, 7)], tosem.at[s, 1])
        rank = jnp.sum(TOR[s].astype(f32), axis=0)
        y = y + low_rank_scale * mm(unpack_split(rank), BO[...])
        wait(RB.at[s, pl.ds(0, 7)], rssem.at[s, 1])
        for q in range(8):
            y = y + RB[s, q].astype(f32)
        y = y.astype(bf16)

        if s + 1 < STEPS:
            ST1[me] = y
            loop(1, 8, lambda k: tensor_copy(
                ST1.at[me], ST1.at[me], agdsem.at[0, k], agdsem.at[1, k],
                lax.rem(me + 2 * k, T)).start())
            tensor_copy(ST1.at[me], ST1.at[me], agssem.at[0], agssem.at[1], sib).start()
        yf = y.astype(f32)
        for c in range(4):
            for i in range(4):
                OUTF[c, pl.ds(i, 16, stride=4), :] = yf[16 * i:16 * i + 16, 128 * c:128 * c + 128]
        for c in range(4):
            out[s, :, 128 * c:128 * c + 128] = OUTF[c].astype(bf16)

        if s + 1 < STEPS:
            total = square_sum(ST1, me, zero_total)

            def pass_on(k, total):
                j = lax.rem(me + T - 2 * k, T)
                wait(ST1.at[j], agdsem.at[1, k])
                tensor_copy(
                    ST1.at[j], ST1.at[j], agfsem.at[0, k], agfsem.at[1, k], sib).start()
                return square_sum(ST1, j, total)
            total = lax.fori_loop(1, 8, pass_on, total)
            wait(ST1.at[sib], agssem.at[1])
            total = square_sum(ST1, sib, total)

            def take(k, total):
                j = lax.rem(sib + T - 2 * k, T)
                wait(ST1.at[j], agfsem.at[1, k])
                return square_sum(ST1, j, total)
            total = lax.fori_loop(1, 8, take, total)
            normalize(ST1, total)
            send_rank(s + 1)

    wait(A1R.at[pl.ds(0, R - 1)], a1sem.at[0])
    wait(WO.at[:, pl.ds(0, CHUNK), :], wosem.at[0])
    wait(A2S.at[pl.ds(0, T - 1)], a2sem.at[0])
    wait(AOR.at[pl.ds(0, T - 1)], aosem.at[0])
    for s in range(STEPS):
        wait(TR.at[s, pl.ds(0, T - 1)], tsem.at[s, 0])
        wait(QR.at[s, pl.ds(0, T - 1)], qsem.at[s, 0])
        wait(AR.at[s, pl.ds(0, T - 1)], asem.at[s, 0])
        wait(TOR.at[s, pl.ds(0, 7)], tosem.at[s, 0])
        wait(RB.at[s, pl.ds(0, 7)], rssem.at[s, 0])
    loop(1, 8, lambda k: wait(ST1.at[me], agdsem.at[0, k]))
    wait(ST1.at[me], agssem.at[0])
    loop(1, 8, lambda k: wait(ST1.at[me], agfsem.at[0, k]))


def body(
    hidden_in,
    norm_gain,
    query_weight_base,
    w_key,
    w_value,
    output_weight_base,
    kv_cache,
    cache_lengths,
    adapter_shards,
    shard_order,
):
    half_dim = HEAD_DIM // 2
    exponent = np.arange(half_dim, dtype=np.float32) * np.float32(2.0 / HEAD_DIM)
    frequency = np.float32(rope_theta) ** (-exponent)
    freq = jnp.asarray(np.concatenate([frequency, frequency]).reshape(1, HEAD_DIM))
    vmem = pl.BlockSpec(memory_space=pltpu.VMEM)
    smem = pl.BlockSpec(memory_space=pltpu.SMEM)
    hbm = pl.BlockSpec(memory_space=pl.ANY)
    V = pltpu.VMEM
    dma = pltpu.SemaphoreType.DMA
    return pl.pallas_call(
        kernel,
        out_shape=jax.ShapeDtypeStruct((STEPS, 64, CHUNK), bf16),
        in_specs=[vmem, vmem, hbm, hbm, hbm, hbm, hbm, smem, vmem, vmem, vmem],
        out_specs=vmem,
        scratch_shapes=[
            V((T, CHUNK, CHUNK), bf16),
            V((128, D), bf16),
            V((8, 2 * CHUNK, CHUNK), bf16),
            V((4, KV_HEADS, CAP, 2, HEAD_DIM), bf16),
            V((4, 64, 128), f32),
            V((T, 64, CHUNK), bf16),
            V((T, 64, CHUNK), bf16),
            V((T, 64, CHUNK), bf16),
            V((128, 128), bf16),
            V((R, 128, 128), bf16),
            V((T, 64, 128), bf16),
            V((T, 64, 128), bf16),
            V((1024, 128), f32),
            V((T, 64, 128), f32),
            V((512, 128), f32),
            V((32, 256, 128), bf16),
            V((128, CHUNK), bf16),
            V((128, CHUNK), bf16),
            V((8, 32, 128), bf16),
            V((T, 32, 128), bf16),
            V((1024, 128), f32),
            V((1024, 128), bf16),
            V((STEPS, 32, 128), bf16),
            V((STEPS, T, 32, 128), bf16),
            V((512, 128), f32),
            V((STEPS, T, 32, 128), bf16),
            V((STEPS, T, 32, 128), bf16),
            V((256, 128), f32),
            V((STEPS, 64, 128), f32),
            V((STEPS, 64, 128), f32),
            V((256, 128), f32),
            V((STEPS, 8, 32, 128), bf16),
            V((STEPS, T, 32, 128), bf16),
            V((64, 2 * CHUNK), bf16),
            V((STEPS, 32, 128), bf16),
            V((STEPS, 8, 32, 128), bf16),
            V((STEPS, 8, 64, CHUNK), bf16),
            V((STEPS, 8, 64, CHUNK), bf16),
            V((4, 64, 128), f32),
            dma((20,)),
            dma((2,)),
            dma((2,)),
            dma((2,)),
            dma((2,)),
            dma((STEPS, 2)),
            dma((STEPS, 2)),
            dma((STEPS, 2)),
            dma((STEPS, 2)),
            dma((STEPS, 2)),
            dma((2, 8)),
            dma((2, 8)),
            dma((2,)),
        ],
        compiler_params=pltpu.CompilerParams(
            collective_id=0, has_side_effects=True, vmem_limit_bytes=56 * 2**20
        ),
        cost_estimate=pl.CostEstimate(
            flops=5 * 10**9, bytes_accessed=25 * 2**20, transcendentals=10**6
        ),
    )(
        hidden_in,
        norm_gain.reshape(T, 1, CHUNK),
        query_weight_base,
        w_key.T,
        w_value.T,
        output_weight_base,
        kv_cache,
        cache_lengths,
        freq,
        adapter_shards.reshape(128, 128),
        shard_order.reshape(1, 128),
    )


def solution(mesh):
    return jax.shard_map(
        body,
        mesh=mesh,
        in_specs=(
            P("rollout", None),
            P(),
            P(None, "tensor"),
            P(None, "tensor"),
            P(None, "tensor"),
            P("tensor", None),
            P(("rollout", "tensor"), None, None, None),
            P(("rollout", "tensor")),
            P(("rollout", "tensor"), None),
            P(),
        ),
        out_specs=P(None, "rollout", "tensor"),
        check_vma=False,
    )
```

```python
import jax
import jax.numpy as jnp
import numpy as np
from jax import lax
from jax.experimental import pallas as pl
from jax.experimental.pallas import tpu as pltpu
from jax.sharding import PartitionSpec as P

D = 8192
HEADS = 64
KV_HEADS = 8
HEAD_DIM = 128
RANK = 64
STEPS = 2
CAP = 256
T = 16
R = 8
CHUNK = D // T

low_rank_scale = 2.0
norm_epsilon = 1e-05
rope_theta = 500000.0
score_scale = 1.0 / np.sqrt(np.float32(HEAD_DIM))

f32 = jnp.float32
bf16 = jnp.bfloat16
MESH = pl.DeviceIdType.MESH


def mm(a, b):
    return jnp.dot(a, b, preferred_element_type=f32)


def mm_t(a, b):
    return lax.dot_general(a, b, (((1,), (1,)), ((), ())), preferred_element_type=f32)


def lanes(shape):
    return lax.broadcasted_iota(jnp.int32, shape, len(shape) - 1)


def swap_halves(x):
    return pltpu.roll(x, 64, len(x.shape) - 1)


def spread_pairs(x, ref):
    low = lanes(x.shape) < 64
    rows = x.shape[0]
    ref[pl.ds(0, rows, stride=2), :] = jnp.where(low, x, 0.0)
    ref[pl.ds(1, rows, stride=2), :] = jnp.where(low, swap_halves(x), 0.0)


def pack_rank(t):
    return t[0:32] + swap_halves(t[32:64])


def unpack_split(total):
    high = total.astype(bf16).astype(f32)
    rest = total - high
    low = lanes(total.shape) < 64
    top = jnp.where(low, high, swap_halves(rest))
    bottom = jnp.where(low, swap_halves(high), rest)
    return jnp.concatenate([top, bottom], axis=0).astype(bf16)


def kernel(
    hid, gain, wq, wk_t, wv_t, wo, kv, lens, freq, piece, order,
    out,
    WQ, WKV, WO, KV, HF, ST, NB,
    PF, CP, A1R, A2S, A2R, XF, OF, AE, AQ, BQ, BO, AOS, AOR, AOE, AO,
    Q32, QS, QR, QX, KN, VN, AF, AM, AR, AT, TOS, TOR, RSS, RB, OUTF,
    lsem, wosem, a1sem, a2sem, a3dsem, a3fsem, aosem, qsem, asem, tosem, rssem, agdsem, agfsem,
):
    me = lax.axis_index("tensor")
    ro = lax.axis_index("rollout")
    core = lax.rem(me, 2)
    chip = me // 2
    sib = me + 1 - 2 * core

    def wait(ref, sem):
        pltpu.make_async_copy(ref, ref, sem).wait()

    def tensor_copy(src, dst, send, recv, peer):
        return pltpu.make_async_remote_copy(
            src_ref=src, dst_ref=dst, send_sem=send, recv_sem=recv,
            device_id={"tensor": peer}, device_id_type=MESH,
        )

    def loop(lo, hi, body):
        def step(k, carry):
            body(k)
            return carry
        lax.fori_loop(lo, hi, step, 0)

    barrier = pltpu.get_barrier_semaphore()
    loop(1, T, lambda k: pl.semaphore_signal(
        barrier, inc=1, device_id={"tensor": lax.rem(me + k, T)}, device_id_type=MESH))
    partner = ro + 1 - 2 * lax.rem(ro, 2)
    loop(1, 4, lambda k: pl.semaphore_signal(
        barrier, inc=1, device_id={"rollout": lax.rem(ro + 2 * k, R)}, device_id_type=MESH))
    pl.semaphore_signal(
        barrier, inc=1, device_id={"rollout": partner}, device_id_type=MESH)

    for j in range(8):
        pltpu.make_async_copy(
            wq.at[pl.ds(4 * j, 4)], WQ.at[pl.ds(4 * j, 4)], lsem.at[0]).start()
    pltpu.make_async_copy(wk_t, WKV.at[pl.ds(0, 64), :], lsem.at[16]).start()
    pltpu.make_async_copy(wv_t, WKV.at[pl.ds(64, 64), :], lsem.at[17]).start()
    for i in range(4):
        for g in range(KV_HEADS):
            pltpu.make_async_copy(
                kv.at[i, :, :, pl.ds(HEAD_DIM * g, HEAD_DIM)], KV.at[i, g], lsem.at[19]).start()

    def wo_columns(q, parity):
        return wo.at[:, pl.ds(pl.multiple_of((2 * q + parity) * CHUNK, CHUNK), CHUNK)]

    wo_rows = pl.ds(pl.multiple_of(core * CHUNK, CHUNK), CHUNK)
    loop(0, 8, lambda q: pltpu.make_async_copy(
        wo_columns(q, core), WO.at[q, wo_rows, :], lsem.at[18]).start())

    order_row = order[...]
    mine = jnp.sum(
        jnp.where(lanes((1, 128)) == ro * T + me, order_row, 0), axis=1, keepdims=True)
    is_up = jnp.broadcast_to((mine >> 5) & 1, (128, 128))
    row = lax.broadcasted_iota(jnp.int32, (128, 128), 0)
    up_row = 64 * ((row >> 2) & 1) + 4 * (row >> 3) + (row & 3)
    wanted = jnp.where(is_up == 1, up_row, row)
    pick = jnp.where(lanes((128, 128)) == wanted, 1.0, 0.0).astype(bf16)
    flat = piece[...].astype(f32)
    for r in range(128):
        PF[r:r + 1, :] = flat[:, 128 * r:128 * r + 128]
    CP[...] = mm(pick, PF[...].astype(bf16)).astype(bf16)
    A1R[ro] = CP[...]
    place = jnp.where(row == jnp.broadcast_to(order_row, (128, 128)), 1.0, 0.0).astype(bf16)

    pl.semaphore_wait(barrier, T - 1 + 4)

    def rollout_copy(src, slot, sem, peer):
        return pltpu.make_async_remote_copy(
            src_ref=src, dst_ref=A1R.at[slot], send_sem=a1sem.at[0, sem],
            recv_sem=a1sem.at[1, sem], device_id={"rollout": peer}, device_id_type=MESH)

    rollout_copy(CP, ro, 0, partner).start()
    loop(1, 4, lambda k: rollout_copy(CP, ro, 1, lax.rem(ro + 2 * k, R)).start())
    loop(0, 8, lambda q: tensor_copy(
        wo_columns(q, 1 - core), WO.at[q, wo_rows, :], wosem.at[0], wosem.at[1], sib).start())

    def permute_hidden(j):
        for c in range(4):
            at = pl.multiple_of(CHUNK * j + 128 * c, 128)
            HF[c] = hid[:, pl.ds(at, 128)].astype(f32)
        for c in range(4):
            for i in range(4):
                ST[0, j, 16 * i:16 * i + 16, 128 * c:128 * c + 128] = (
                    HF[c, pl.ds(i, 16, stride=4), :].astype(bf16))
    loop(0, T, permute_hidden)

    Q32[320:512, :] = jnp.zeros((192, 128), f32)

    def square_sum(s, j, total):
        x = ST[s, j].astype(f32)
        x = x * x
        return total + (x[:, 0:128] + x[:, 128:256]) + (x[:, 256:384] + x[:, 384:512])

    def normalize(s, total):
        inv = lax.rsqrt(jnp.sum(total, axis=1, keepdims=True) * (1.0 / D) + norm_epsilon)
        def body(j):
            NB[j] = (ST[s, j].astype(f32) * inv * gain[j]).astype(bf16)
        loop(0, T, body)

    zero_total = jnp.zeros((64, 128), f32)
    normalize(0, lax.fori_loop(0, T, lambda j, t: square_sum(0, j, t), zero_total))

    def project_kv(j, new):
        columns = pl.ds(pl.multiple_of(CHUNK * j, CHUNK), CHUNK)
        return new + mm_t(NB[j], WKV[:, columns])

    wait(A1R.at[0], a1sem.at[1, 0])
    loop(1, 4, lambda k: rollout_copy(
        A1R.at[partner], partner, 2, lax.rem(ro + 2 * k, R)).start())

    for half in range(2):
        z = lax.rem(ro + half, 2)
        wait(A1R.at[pl.ds(0, 3)], a1sem.at[1, 1 + half])
        for y in range(4):
            held = A1R[2 * y + z].astype(f32).reshape(T, 8, 128)
            OF[:, 8 * y:8 * y + 8, :] = held
        A2S[half] = OF[...].astype(bf16)
        loop(1, T, lambda k: tensor_copy(
            A2S.at[half, lax.rem(me + k, T)], A2R.at[z, me], a2sem.at[half, 0],
            a2sem.at[half, 1], lax.rem(me + k, T)).start())
        A2R[z, me] = A2S[half, me]

    wait(WKV.at[pl.ds(0, 64), :], lsem.at[16])
    wait(WKV.at[pl.ds(64, 64), :], lsem.at[17])
    new = lax.fori_loop(0, T, project_kv, zero_total)
    wait(WQ, lsem.at[0])
    for half in range(2):
        wait(A2R.at[0, pl.ds(0, T - 1)], a2sem.at[half, 1])

    for z in range(2):
        arrived = A2R[z].astype(f32).reshape(T, 4, 8, 128)
        for y in range(4):
            r = 2 * y + z
            XF[128 * r:128 * r + 128, :] = arrived[:, y].reshape(128, 128)
    FL = AOE
    for s in range(8):
        FL[pl.ds(s, 128, stride=8), :] = mm(place, XF[pl.ds(s, 128, stride=8), :].astype(bf16))
    spread_pairs(FL[0:256, :], AE)
    AQ[me] = (AE[0:256, :] + swap_halves(AE[256:512, :])).astype(bf16)
    loop(1, 8, lambda k: tensor_copy(
        AQ.at[me], AQ.at[me], a3dsem.at[0, k], a3dsem.at[1, k], lax.rem(me + 2 * k, T)).start())
    tensor_copy(AQ.at[me], AQ.at[me], a3fsem.at[0, 0], a3fsem.at[1, 0], sib).start()
    for c in range(4):
        up = (low_rank_scale * FL[pl.ds(256 + c, 64, stride=4), :]).astype(bf16)
        none = jnp.zeros_like(up)
        BQ[0, 0:64, 128 * c:128 * c + 128] = up
        BQ[0, 64:128, 128 * c:128 * c + 128] = none
        BQ[1, 0:64, 128 * c:128 * c + 128] = none
        BQ[1, 64:128, 128 * c:128 * c + 128] = up
        up = FL[pl.ds(768 + c, 64, stride=4), :].astype(bf16)
        BO[0:64, 128 * c:128 * c + 128] = up
        BO[64:128, 128 * c:128 * c + 128] = up
    AOS[...] = FL[512:768, :].astype(bf16).reshape(8, 32, 128)

    loop(1, T, lambda k: tensor_copy(
        AOS.at[lax.rem(me + k, T) // 2], AOR.at[me], aosem.at[0], aosem.at[1],
        lax.rem(me + k, T)).start())
    AOR[me] = AOS[chip]

    def merge(j):
        strip = pl.ds(pl.multiple_of(16 * j, 16), 16)
        for half in range(2):
            for m in range(4):
                change = mm(AQ[j, 64 * m:64 * m + 64, :], BQ[half]).reshape(4, 16, CHUNK)
                blocks = pl.ds(16 * half + 4 * m, 4)
                WQ[blocks, strip, :] = (WQ[blocks, strip, :].astype(f32) + change).astype(bf16)

    def merge_direct(k):
        j = lax.rem(me + T - 2 * k, T)

        @pl.when(k > 0)
        def _():
            wait(AQ.at[j], a3dsem.at[1, k])
            tensor_copy(AQ.at[j], AQ.at[j], a3fsem.at[0, k], a3fsem.at[1, k], sib).start()
        merge(j)

    def merge_passed(k):
        j = lax.rem(sib + T - 2 * k, T)
        wait(AQ.at[j], a3fsem.at[1, k])
        merge(j)

    loop(0, 8, merge_direct)
    loop(0, 8, merge_passed)

    low_half = lanes((8, 128)) < 64
    sub = lax.broadcasted_iota(jnp.int32, (8, 128), 0) & 3
    lengths = jnp.zeros((8, 128), jnp.int32)
    for i in range(4):
        lengths = jnp.where(sub == i, lens[i], lengths)
    wide = lanes((64, 2 * CAP))

    for s in range(STEPS):
        def project(j, q):
            return q + mm(NB[j], WQ[pl.ds(2 * j, 2)].reshape(CHUNK, CHUNK))

        if s > 0:
            new = lax.fori_loop(0, T, project_kv, zero_total)
        q = lax.fori_loop(0, T, project, jnp.zeros((64, CHUNK), f32))
        for h in range(4):
            Q32[64 * h:64 * h + 64, :] = q[:, 128 * h:128 * h + 128]
        Q32[256:320, :] = new
        for t in range(T):
            QS[s, t] = Q32[pl.ds(t, 32, stride=16), :].astype(bf16)
        loop(1, T, lambda k: tensor_copy(
            QS.at[s, lax.rem(me + k, T)], QR.at[s, me], qsem.at[s, 0], qsem.at[s, 1],
            lax.rem(me + k, T)).start())
        QR[s, me] = QS[s, me]

        angles = (lengths + s).astype(f32) * freq[...]
        cosine = jnp.cos(angles)
        sine = jnp.where(low_half, -jnp.sin(angles), jnp.sin(angles))

        if s == 0:
            wait(AOR.at[pl.ds(0, T - 1)], aosem.at[1])
            blocks = AOR[...].astype(f32).reshape(T, 4, 8, 128)
            for b in range(4):
                XF[128 * b:128 * b + 128, :] = blocks[:, b].reshape(128, 128)
            spread_pairs(XF[0:512, :], AOE)
            AO[...] = AOE[...].astype(bf16)

        wait(QR.at[s, pl.ds(0, T - 1)], qsem.at[s, 1])
        got = QR[s].astype(f32)
        heads = got[:, 0:16].reshape(T, 2, 8, 128)
        heads = heads * cosine + swap_halves(heads) * sine
        QX[...] = heads.astype(bf16).astype(f32).reshape(256, 128)
        fresh = got[:, 16:24].reshape(8, 2, 8, 128)
        even, odd = fresh[:, 0], fresh[:, 1]
        low = lanes(even.shape) < 64
        key = jnp.where(low, even, swap_halves(odd))
        key = key * cosine + swap_halves(key) * sine
        KN[s] = key.astype(bf16).astype(f32).reshape(64, 128)
        VN[s] = jnp.where(low, swap_halves(even), odd).reshape(64, 128)

        if s == 0:
            wait(KV, lsem.at[19])

        def attend(i):
            queries = [QX[pl.ds(32 * g + i, 8, stride=4), :] for g in range(KV_HEADS)]
            scores = jnp.concatenate(
                [mm_t(queries[g].astype(bf16), KV[i, g].reshape(2 * CAP, HEAD_DIM))
                 for g in range(KV_HEADS)], axis=0) * score_scale
            seen = ((wide & 1) == 0) & (wide < 2 * lens[i])
            scores = jnp.where(seen, scores, -1e30)
            rows = jnp.concatenate(queries, axis=0)
            largest = jnp.max(scores, axis=1, keepdims=True)
            news, values = [], []
            for n in range(s + 1):
                k = KN[n, pl.ds(i, 8, stride=8), :]
                v = VN[n, pl.ds(i, 8, stride=8), :]
                k = jnp.broadcast_to(k[:, None, :], (8, 8, 128)).reshape(64, 128)
                values.append(jnp.broadcast_to(v[:, None, :], (8, 8, 128)).reshape(64, 128))
                news.append(jnp.sum(rows * k, axis=1, keepdims=True) * score_scale)
                largest = jnp.maximum(largest, news[-1])
            expo = jnp.exp(scores - largest)
            news = [jnp.exp(x - largest) for x in news]
            total = jnp.sum(expo, axis=1, keepdims=True)
            for x in news:
                total = total + x
            weights = pltpu.roll((expo / total).astype(bf16).astype(f32), 1, 1).astype(bf16)
            result = jnp.concatenate(
                [mm(weights[8 * g:8 * g + 8], KV[i, g].reshape(2 * CAP, HEAD_DIM))
                 for g in range(KV_HEADS)], axis=0)
            for x, v in zip(news, values):
                result = result + (x / total).astype(bf16).astype(f32) * v
            AF[pl.ds(i, 64, stride=4), :] = result

        for i in range(4):
            attend(i)
        AM[s] = AF[...].astype(bf16).reshape(8, 32, 128)
        loop(1, T, lambda k: tensor_copy(
            AM.at[s, lax.rem(me + k, T) // 2], AR.at[s, me], asem.at[s, 0], asem.at[s, 1],
            lax.rem(me + k, T)).start())
        AR[s, me] = AM[s, chip]
        wait(AR.at[s, pl.ds(0, T - 1)], asem.at[s, 1])
        XF[0:512, :] = AR[s].astype(f32).reshape(512, 128)
        for h in range(8):
            for i in range(4):
                AT[16 * i:16 * i + 16, 128 * h:128 * h + 128] = (
                    XF[pl.ds(4 * h + i, 16, stride=32), :].astype(bf16))

        attended = AT[...]
        t = mm(attended, AO[...])
        TOS[s] = pack_rank(t).astype(bf16)
        loop(1, 8, lambda k: tensor_copy(
            TOS.at[s], TOR.at[s, chip], tosem.at[s, 0], tosem.at[s, 1],
            lax.rem(me + 2 * k, T)).start())
        TOR[s, chip] = TOS[s]
        if s == 0:
            wait(WO.at[:, pl.ds(0, CHUNK), :], lsem.at[18])
            wait(WO.at[:, pl.ds(0, CHUNK), :], wosem.at[1])

        def part(k):
            q = lax.rem(chip + k, 8)
            RSS[s, q] = mm(AT[...], WO[q]).astype(bf16)
            tensor_copy(
                RSS.at[s, q], RB.at[s, chip], rssem.at[s, 0], rssem.at[s, 1],
                2 * q + core).start()
        loop(1, 8, part)
        RB[s, chip] = jnp.zeros((64, CHUNK), bf16)
        y = mm(attended, WO[chip])
        y = y + ST[s, me].astype(f32)
        wait(TOR.at[s, pl.ds(0, 7)], tosem.at[s, 1])
        rank = jnp.sum(TOR[s].astype(f32), axis=0)
        y = y + low_rank_scale * mm(unpack_split(rank), BO[...])
        wait(RB.at[s, pl.ds(0, 7)], rssem.at[s, 1])
        for q in range(8):
            y = y + RB[s, q].astype(f32)
        y = y.astype(bf16)

        if s + 1 < STEPS:
            ST[1, me] = y
            loop(1, 8, lambda k: tensor_copy(
                ST.at[1, me], ST.at[1, me], agdsem.at[0, k], agdsem.at[1, k],
                lax.rem(me + 2 * k, T)).start())
        yf = y.astype(f32)
        for c in range(4):
            for i in range(4):
                OUTF[c, pl.ds(i, 16, stride=4), :] = yf[16 * i:16 * i + 16, 128 * c:128 * c + 128]
        for c in range(4):
            out[s, :, 128 * c:128 * c + 128] = OUTF[c].astype(bf16)

        if s + 1 < STEPS:
            def pass_on(k, total):
                j = lax.rem(me + T - 2 * k, T)

                @pl.when(k > 0)
                def _():
                    wait(ST.at[1, j], agdsem.at[1, k])
                tensor_copy(
                    ST.at[1, j], ST.at[1, j], agfsem.at[0, k], agfsem.at[1, k], sib).start()
                return square_sum(1, j, total)
            total = lax.fori_loop(0, 8, pass_on, zero_total)

            def take(k, total):
                j = lax.rem(sib + T - 2 * k, T)
                wait(ST.at[1, j], agfsem.at[1, k])
                return square_sum(1, j, total)
            total = lax.fori_loop(0, 8, take, total)
            normalize(1, total)

    wait(A1R.at[0], a1sem.at[0, 0])
    wait(A1R.at[pl.ds(0, 3)], a1sem.at[0, 1])
    wait(A1R.at[pl.ds(0, 3)], a1sem.at[0, 2])
    wait(WO.at[:, pl.ds(0, CHUNK), :], wosem.at[0])
    for half in range(2):
        wait(A2R.at[0, pl.ds(0, T - 1)], a2sem.at[half, 0])
    loop(1, 8, lambda k: wait(AQ.at[me], a3dsem.at[0, k]))
    loop(0, 8, lambda k: wait(AQ.at[me], a3fsem.at[0, k]))
    wait(AOR.at[pl.ds(0, T - 1)], aosem.at[0])
    for s in range(STEPS):
        wait(QR.at[s, pl.ds(0, T - 1)], qsem.at[s, 0])
        wait(AR.at[s, pl.ds(0, T - 1)], asem.at[s, 0])
        wait(TOR.at[s, pl.ds(0, 7)], tosem.at[s, 0])
        wait(RB.at[s, pl.ds(0, 7)], rssem.at[s, 0])
    loop(1, 8, lambda k: wait(ST.at[1, me], agdsem.at[0, k]))
    loop(0, 8, lambda k: wait(ST.at[1, me], agfsem.at[0, k]))


def body(
    hidden_in,
    norm_gain,
    query_weight_base,
    w_key,
    w_value,
    output_weight_base,
    kv_cache,
    cache_lengths,
    adapter_shards,
    shard_order,
):
    half_dim = HEAD_DIM // 2
    exponent = np.arange(half_dim, dtype=np.float32) * np.float32(2.0 / HEAD_DIM)
    frequency = np.float32(rope_theta) ** (-exponent)
    freq = jnp.asarray(np.concatenate([frequency, frequency]).reshape(1, HEAD_DIM))
    vmem = pl.BlockSpec(memory_space=pltpu.VMEM)
    smem = pl.BlockSpec(memory_space=pltpu.SMEM)
    hbm = pl.BlockSpec(memory_space=pl.ANY)
    V = pltpu.VMEM
    dma = pltpu.SemaphoreType.DMA
    return pl.pallas_call(
        kernel,
        out_shape=jax.ShapeDtypeStruct((STEPS, 64, CHUNK), bf16),
        in_specs=[vmem, vmem, hbm, hbm, hbm, hbm, hbm, smem, vmem, vmem, vmem],
        out_specs=vmem,
        scratch_shapes=[
            V((32, 256, CHUNK), bf16),
            V((128, D), bf16),
            V((8, 2 * CHUNK, CHUNK), bf16),
            V((4, KV_HEADS, CAP, 2, HEAD_DIM), bf16),
            V((4, 64, 128), f32),
            V((2, T, 64, CHUNK), bf16),
            V((T, 64, CHUNK), bf16),
            V((128, 128), f32),
            V((128, 128), bf16),
            V((R, 128, 128), bf16),
            V((2, T, 32, 128), bf16),
            V((2, T, 32, 128), bf16),
            V((1024, 128), f32),
            V((T, 32, 128), f32),
            V((512, 128), f32),
            V((T, 256, 128), bf16),
            V((2, 128, CHUNK), bf16),
            V((128, CHUNK), bf16),
            V((8, 32, 128), bf16),
            V((T, 32, 128), bf16),
            V((1024, 128), f32),
            V((1024, 128), bf16),
            V((512, 128), f32),
            V((STEPS, T, 32, 128), bf16),
            V((STEPS, T, 32, 128), bf16),
            V((256, 128), f32),
            V((STEPS, 64, 128), f32),
            V((STEPS, 64, 128), f32),
            V((256, 128), f32),
            V((STEPS, 8, 32, 128), bf16),
            V((STEPS, T, 32, 128), bf16),
            V((64, 2 * CHUNK), bf16),
            V((STEPS, 32, 128), bf16),
            V((STEPS, 8, 32, 128), bf16),
            V((STEPS, 8, 64, CHUNK), bf16),
            V((STEPS, 8, 64, CHUNK), bf16),
            V((4, 64, 128), f32),
            dma((20,)),
            dma((2,)),
            dma((2, 3)),
            dma((2, 2)),
            dma((2, 8)),
            dma((2, 8)),
            dma((2,)),
            dma((STEPS, 2)),
            dma((STEPS, 2)),
            dma((STEPS, 2)),
            dma((STEPS, 2)),
            dma((2, 8)),
            dma((2, 8)),
        ],
        compiler_params=pltpu.CompilerParams(
            collective_id=0, has_side_effects=True, vmem_limit_bytes=56 * 2**20
        ),
        cost_estimate=pl.CostEstimate(
            flops=5 * 10**9, bytes_accessed=25 * 2**20, transcendentals=10**6
        ),
    )(
        hidden_in,
        norm_gain.reshape(T, 1, CHUNK),
        query_weight_base.reshape(32, 256, CHUNK),
        w_key.T,
        w_value.T,
        output_weight_base,
        kv_cache,
        cache_lengths,
        freq,
        adapter_shards,
        shard_order.reshape(1, 128),
    )


def solution(mesh):
    return jax.shard_map(
        body,
        mesh=mesh,
        in_specs=(
            P("rollout", None),
            P(),
            P(None, "tensor"),
            P(None, "tensor"),
            P(None, "tensor"),
            P("tensor", None),
            P(("rollout", "tensor"), None, None, None),
            P(("rollout", "tensor")),
            P(("rollout", "tensor"), None),
            P(),
        ),
        out_specs=P(None, "rollout", "tensor"),
        check_vma=False,
    )
```

```python
import jax
import jax.numpy as jnp
import numpy as np
from jax import lax
from jax.experimental import pallas as pl
from jax.experimental.pallas import tpu as pltpu
from jax.sharding import PartitionSpec as P

D = 8192
HEADS = 64
KV_HEADS = 8
HEAD_DIM = 128
RANK = 64
STEPS = 2
CAP = 256
T = 16
R = 8
CHUNK = D // T

low_rank_scale = 2.0
norm_epsilon = 1e-05
rope_theta = 500000.0
score_scale = 1.0 / np.sqrt(np.float32(HEAD_DIM))

f32 = jnp.float32
bf16 = jnp.bfloat16
MESH = pl.DeviceIdType.MESH


def mm(a, b):
    return jnp.dot(a, b, preferred_element_type=f32)


def mm_t(a, b):
    return lax.dot_general(a, b, (((1,), (1,)), ((), ())), preferred_element_type=f32)


def lanes(shape):
    return lax.broadcasted_iota(jnp.int32, shape, len(shape) - 1)


def swap_halves(x):
    return pltpu.roll(x, 64, len(x.shape) - 1)


def spread_pairs(x, ref):
    low = lanes(x.shape) < 64
    rows = x.shape[0]
    ref[pl.ds(0, rows, stride=2), :] = jnp.where(low, x, 0.0)
    ref[pl.ds(1, rows, stride=2), :] = jnp.where(low, swap_halves(x), 0.0)


def pack_rank(t):
    return t[0:32] + swap_halves(t[32:64])


def unpack_split(total):
    high = total.astype(bf16).astype(f32)
    rest = total - high
    low = lanes(total.shape) < 64
    top = jnp.where(low, high, swap_halves(rest))
    bottom = jnp.where(low, swap_halves(high), rest)
    return jnp.concatenate([top, bottom], axis=0).astype(bf16)


def kernel(
    hid, gain, wq, wk_t, wv_t, wo, kv, lens, freq, piece, order,
    out,
    WQ, WKV, WO, KV, HF, ST, NB,
    PF, CP, A1R, A2S, A2R, XF, OF, AE, AQ, BQ, BO, AOS, AOR, AOE, AO,
    Q32, QS, QR, QX, KN, VN, AF, AM, AR, AT, TOS, TOR, RSS, RB, OUTF, SQS, SQR,
    lsem, wosem, a1sem, a2sem, a3dsem, a3fsem, aosem, qsem, asem, tosem, rssem, agdsem, agfsem, sqsem,
):
    me = lax.axis_index("tensor")
    ro = lax.axis_index("rollout")
    core = lax.rem(me, 2)
    chip = me // 2
    sib = me + 1 - 2 * core

    def wait(ref, sem):
        pltpu.make_async_copy(ref, ref, sem).wait()

    def tensor_copy(src, dst, send, recv, peer):
        return pltpu.make_async_remote_copy(
            src_ref=src, dst_ref=dst, send_sem=send, recv_sem=recv,
            device_id={"tensor": peer}, device_id_type=MESH,
        )

    def loop(lo, hi, body):
        def step(k, carry):
            body(k)
            return carry
        lax.fori_loop(lo, hi, step, 0)

    barrier = pltpu.get_barrier_semaphore()
    loop(1, T, lambda k: pl.semaphore_signal(
        barrier, inc=1, device_id={"tensor": lax.rem(me + k, T)}, device_id_type=MESH))
    loop(1, R, lambda k: pl.semaphore_signal(
        barrier, inc=1, device_id={"rollout": lax.rem(ro + k, R)}, device_id_type=MESH))

    for j in range(8):
        pltpu.make_async_copy(
            wq.at[pl.ds(4 * j, 4)], WQ.at[pl.ds(4 * j, 4)], lsem.at[0]).start()
    pltpu.make_async_copy(wk_t, WKV.at[pl.ds(0, 64), :], lsem.at[16]).start()
    pltpu.make_async_copy(wv_t, WKV.at[pl.ds(64, 64), :], lsem.at[17]).start()
    for i in range(4):
        for g in range(KV_HEADS):
            pltpu.make_async_copy(
                kv.at[i, :, :, pl.ds(HEAD_DIM * g, HEAD_DIM)], KV.at[i, g], lsem.at[19]).start()

    def wo_columns(q, parity):
        return wo.at[:, pl.ds(pl.multiple_of((2 * q + parity) * CHUNK, CHUNK), CHUNK)]

    wo_rows = pl.ds(pl.multiple_of(core * CHUNK, CHUNK), CHUNK)
    loop(0, 8, lambda q: pltpu.make_async_copy(
        wo_columns(q, core), WO.at[q, wo_rows, :], lsem.at[18]).start())

    order_row = order[...]
    mine = jnp.sum(
        jnp.where(lanes((1, 128)) == ro * T + me, order_row, 0), axis=1, keepdims=True)
    is_up = jnp.broadcast_to((mine >> 5) & 1, (128, 128))
    row = lax.broadcasted_iota(jnp.int32, (128, 128), 0)
    up_row = 64 * ((row >> 2) & 1) + 4 * (row >> 3) + (row & 3)
    wanted = jnp.where(is_up == 1, up_row, row)
    pick = jnp.where(lanes((128, 128)) == wanted, 1.0, 0.0).astype(bf16)
    flat = piece[...].astype(f32)
    for r in range(128):
        PF[r:r + 1, :] = flat[:, 128 * r:128 * r + 128]
    CP[...] = mm(pick, PF[...].astype(bf16)).astype(bf16)
    A1R[ro] = CP[...]
    place = jnp.where(row == jnp.broadcast_to(order_row, (128, 128)), 1.0, 0.0).astype(bf16)

    pl.semaphore_wait(barrier, T - 1 + R - 1)

    def send_piece(peer, sem):
        pltpu.make_async_remote_copy(
            src_ref=CP, dst_ref=A1R.at[ro], send_sem=a1sem.at[0, sem],
            recv_sem=a1sem.at[1, sem], device_id={"rollout": peer}, device_id_type=MESH).start()

    loop(1, 4, lambda k: send_piece(lax.rem(ro + 2 * k, R), 0))
    other = ro + 1 - 2 * lax.rem(ro, 2)
    loop(0, 4, lambda k: send_piece(lax.rem(other + 2 * k, R), 1))
    loop(0, 8, lambda q: tensor_copy(
        wo_columns(q, 1 - core), WO.at[q, wo_rows, :], wosem.at[0], wosem.at[1], sib).start())

    def permute_hidden(j):
        for c in range(4):
            at = pl.multiple_of(CHUNK * j + 128 * c, 128)
            HF[c] = hid[:, pl.ds(at, 128)].astype(f32)
        for c in range(4):
            for i in range(4):
                ST[0, j, 16 * i:16 * i + 16, 128 * c:128 * c + 128] = (
                    HF[c, pl.ds(i, 16, stride=4), :].astype(bf16))
    loop(0, T, permute_hidden)

    Q32[320:512, :] = jnp.zeros((192, 128), f32)

    def square_sum(s, j, total):
        x = ST[s, j].astype(f32)
        x = x * x
        return total + (x[:, 0:128] + x[:, 128:256]) + (x[:, 256:384] + x[:, 384:512])

    def normalize(s, total):
        inv = lax.rsqrt(jnp.sum(total, axis=1, keepdims=True) * (1.0 / D) + norm_epsilon)
        def body(j):
            NB[j] = (ST[s, j].astype(f32) * inv * gain[j]).astype(bf16)
        loop(0, T, body)

    zero_total = jnp.zeros((64, 128), f32)
    zero_query = jnp.zeros((64, CHUNK), f32)
    normalize(0, lax.fori_loop(0, T, lambda j, t: square_sum(0, j, t), zero_total))

    def project_kv(j, new):
        columns = pl.ds(pl.multiple_of(CHUNK * j, CHUNK), CHUNK)
        return new + mm_t(NB[j], WKV[:, columns])

    for half in range(2):
        z = lax.rem(ro + half, 2)
        wait(A1R.at[pl.ds(0, 3 + half)], a1sem.at[1, half])
        for y in range(4):
            held = A1R[2 * y + z].astype(f32).reshape(T, 8, 128)
            OF[:, 8 * y:8 * y + 8, :] = held
        A2S[half] = OF[...].astype(bf16)
        loop(1, T, lambda k: tensor_copy(
            A2S.at[half, lax.rem(me + k, T)], A2R.at[z, me], a2sem.at[half, 0],
            a2sem.at[half, 1], lax.rem(me + k, T)).start())
        A2R[z, me] = A2S[half, me]

    wait(WKV.at[pl.ds(0, 64), :], lsem.at[16])
    wait(WKV.at[pl.ds(64, 64), :], lsem.at[17])
    new = lax.fori_loop(0, T, project_kv, zero_total)
    wait(WQ, lsem.at[0])
    for half in range(2):
        wait(A2R.at[0, pl.ds(0, T - 1)], a2sem.at[half, 1])

    for z in range(2):
        arrived = A2R[z].astype(f32).reshape(T, 4, 8, 128)
        for y in range(4):
            r = 2 * y + z
            XF[128 * r:128 * r + 128, :] = arrived[:, y].reshape(128, 128)
    FL = AOE
    for s in range(8):
        FL[pl.ds(s, 128, stride=8), :] = mm(place, XF[pl.ds(s, 128, stride=8), :].astype(bf16))
    spread_pairs(FL[0:256, :], AE)
    AQ[me] = (AE[0:256, :] + swap_halves(AE[256:512, :])).astype(bf16)
    loop(1, 8, lambda k: tensor_copy(
        AQ.at[me], AQ.at[me], a3dsem.at[0, k], a3dsem.at[1, k], lax.rem(me + 2 * k, T)).start())
    tensor_copy(AQ.at[me], AQ.at[me], a3fsem.at[0, 0], a3fsem.at[1, 0], sib).start()
    for c in range(4):
        up = (low_rank_scale * FL[pl.ds(256 + c, 64, stride=4), :]).astype(bf16)
        none = jnp.zeros_like(up)
        BQ[0, 0:64, 128 * c:128 * c + 128] = up
        BQ[0, 64:128, 128 * c:128 * c + 128] = none
        BQ[1, 0:64, 128 * c:128 * c + 128] = none
        BQ[1, 64:128, 128 * c:128 * c + 128] = up
        up = FL[pl.ds(768 + c, 64, stride=4), :].astype(bf16)
        BO[0:64, 128 * c:128 * c + 128] = up
        BO[64:128, 128 * c:128 * c + 128] = up
    AOS[...] = FL[512:768, :].astype(bf16).reshape(8, 32, 128)

    loop(1, T, lambda k: tensor_copy(
        AOS.at[lax.rem(me + k, T) // 2], AOR.at[me], aosem.at[0], aosem.at[1],
        lax.rem(me + k, T)).start())
    AOR[me] = AOS[chip]

    def merge(j):
        strip = pl.ds(pl.multiple_of(16 * j, 16), 16)
        for half in range(2):
            for m in range(4):
                change = mm(AQ[j, 64 * m:64 * m + 64, :], BQ[half]).reshape(4, 16, CHUNK)
                blocks = pl.ds(16 * half + 4 * m, 4)
                WQ[blocks, strip, :] = (WQ[blocks, strip, :].astype(f32) + change).astype(bf16)

    def merge_direct(k):
        j = lax.rem(me + T - 2 * k, T)

        @pl.when(k > 0)
        def _():
            wait(AQ.at[j], a3dsem.at[1, k])
            tensor_copy(AQ.at[j], AQ.at[j], a3fsem.at[0, k], a3fsem.at[1, k], sib).start()
        merge(j)

    def merge_passed(k):
        j = lax.rem(sib + T - 2 * k, T)
        wait(AQ.at[j], a3fsem.at[1, k])
        merge(j)

    def merge_both(k):
        merge_direct(k)
        merge_passed(k - 2)

    loop(0, 2, merge_direct)
    loop(2, 8, merge_both)
    loop(6, 8, merge_passed)

    low_half = lanes((8, 128)) < 64
    sub = lax.broadcasted_iota(jnp.int32, (8, 128), 0) & 3
    lengths = jnp.zeros((8, 128), jnp.int32)
    for i in range(4):
        lengths = jnp.where(sub == i, lens[i], lengths)
    wide = lanes((64, 2 * CAP))

    for s in range(STEPS):
        def project(j, q):
            return q + mm(NB[j], WQ[pl.ds(2 * j, 2)].reshape(CHUNK, CHUNK))

        if s == 0:
            q = lax.fori_loop(0, T, project, zero_query)
        for h in range(4):
            Q32[64 * h:64 * h + 64, :] = q[:, 128 * h:128 * h + 128]
        Q32[256:320, :] = new
        for t in range(T):
            QS[s, t] = Q32[pl.ds(t, 32, stride=16), :].astype(bf16)
        loop(1, T, lambda k: tensor_copy(
            QS.at[s, lax.rem(me + k, T)], QR.at[s, me], qsem.at[s, 0], qsem.at[s, 1],
            lax.rem(me + k, T)).start())
        QR[s, me] = QS[s, me]

        angles = (lengths + s).astype(f32) * freq[...]
        cosine = jnp.cos(angles)
        sine = jnp.where(low_half, -jnp.sin(angles), jnp.sin(angles))

        if s == 0:
            wait(AOR.at[pl.ds(0, T - 1)], aosem.at[1])
            blocks = AOR[...].astype(f32).reshape(T, 4, 8, 128)
            for b in range(4):
                XF[128 * b:128 * b + 128, :] = blocks[:, b].reshape(128, 128)
            spread_pairs(XF[0:512, :], AOE)
            AO[...] = AOE[...].astype(bf16)

        wait(QR.at[s, pl.ds(0, T - 1)], qsem.at[s, 1])
        got = QR[s].astype(f32)
        heads = got[:, 0:16].reshape(T, 2, 8, 128)
        heads = heads * cosine + swap_halves(heads) * sine
        QX[...] = heads.astype(bf16).astype(f32).reshape(256, 128)
        fresh = got[:, 16:24].reshape(8, 2, 8, 128)
        even, odd = fresh[:, 0], fresh[:, 1]
        low = lanes(even.shape) < 64
        key = jnp.where(low, even, swap_halves(odd))
        key = key * cosine + swap_halves(key) * sine
        KN[s] = key.astype(bf16).astype(f32).reshape(64, 128)
        VN[s] = jnp.where(low, swap_halves(even), odd).reshape(64, 128)

        if s == 0:
            wait(KV, lsem.at[19])

        def attend(i):
            queries = [QX[pl.ds(32 * g + i, 8, stride=4), :] for g in range(KV_HEADS)]
            scores = jnp.concatenate(
                [mm_t(queries[g].astype(bf16), KV[i, g].reshape(2 * CAP, HEAD_DIM))
                 for g in range(KV_HEADS)], axis=0) * score_scale
            seen = ((wide & 1) == 0) & (wide < 2 * lens[i])
            scores = jnp.where(seen, scores, -1e30)
            rows = jnp.concatenate(queries, axis=0)
            largest = jnp.max(scores, axis=1, keepdims=True)
            news, values = [], []
            for n in range(s + 1):
                k = KN[n, pl.ds(i, 8, stride=8), :]
                v = VN[n, pl.ds(i, 8, stride=8), :]
                k = jnp.broadcast_to(k[:, None, :], (8, 8, 128)).reshape(64, 128)
                values.append(jnp.broadcast_to(v[:, None, :], (8, 8, 128)).reshape(64, 128))
                news.append(jnp.sum(rows * k, axis=1, keepdims=True) * score_scale)
                largest = jnp.maximum(largest, news[-1])
            expo = jnp.exp(scores - largest)
            news = [jnp.exp(x - largest) for x in news]
            total = jnp.sum(expo, axis=1, keepdims=True)
            for x in news:
                total = total + x
            weights = pltpu.roll((expo / total).astype(bf16).astype(f32), 1, 1).astype(bf16)
            result = jnp.concatenate(
                [mm(weights[8 * g:8 * g + 8], KV[i, g].reshape(2 * CAP, HEAD_DIM))
                 for g in range(KV_HEADS)], axis=0)
            for x, v in zip(news, values):
                result = result + (x / total).astype(bf16).astype(f32) * v
            AF[pl.ds(i, 64, stride=4), :] = result

        for i in range(4):
            attend(i)
        AM[s] = AF[...].astype(bf16).reshape(8, 32, 128)
        loop(1, T, lambda k: tensor_copy(
            AM.at[s, lax.rem(me + k, T) // 2], AR.at[s, me], asem.at[s, 0], asem.at[s, 1],
            lax.rem(me + k, T)).start())
        AR[s, me] = AM[s, chip]
        wait(AR.at[s, pl.ds(0, T - 1)], asem.at[s, 1])
        XF[0:512, :] = AR[s].astype(f32).reshape(512, 128)
        for h in range(8):
            for i in range(4):
                AT[16 * i:16 * i + 16, 128 * h:128 * h + 128] = (
                    XF[pl.ds(4 * h + i, 16, stride=32), :].astype(bf16))

        attended = AT[...]
        t = mm(attended, AO[...])
        TOS[s] = pack_rank(t).astype(bf16)
        loop(1, 8, lambda k: tensor_copy(
            TOS.at[s], TOR.at[s, chip], tosem.at[s, 0], tosem.at[s, 1],
            lax.rem(me + 2 * k, T)).start())
        TOR[s, chip] = TOS[s]
        if s == 0:
            wait(WO.at[:, pl.ds(0, CHUNK), :], lsem.at[18])
            wait(WO.at[:, pl.ds(0, CHUNK), :], wosem.at[1])

        def part(k):
            q = lax.rem(chip + k, 8)
            RSS[s, q] = mm(AT[...], WO[q]).astype(bf16)
            tensor_copy(
                RSS.at[s, q], RB.at[s, chip], rssem.at[s, 0], rssem.at[s, 1],
                2 * q + core).start()
        loop(1, 8, part)
        RB[s, chip] = jnp.zeros((64, CHUNK), bf16)
        y = mm(attended, WO[chip])
        y = y + ST[s, me].astype(f32)
        wait(TOR.at[s, pl.ds(0, 7)], tosem.at[s, 1])
        rank = jnp.sum(TOR[s].astype(f32), axis=0)
        y = y + low_rank_scale * mm(unpack_split(rank), BO[...])
        wait(RB.at[s, pl.ds(0, 7)], rssem.at[s, 1])
        for q in range(8):
            y = y + RB[s, q].astype(f32)
        y = y.astype(bf16)

        if s + 1 < STEPS:
            ST[1, me] = y
            squares = y.astype(f32) * y.astype(f32)
            squares = (squares[:, 0:128] + squares[:, 128:256]) + (
                squares[:, 256:384] + squares[:, 384:512])
            SQS[...] = jnp.zeros_like(SQS)
            SQS[0:1, 0:64] = jnp.sum(squares.T, axis=0, keepdims=True)
            loop(1, T, lambda k: tensor_copy(
                SQS, SQR.at[me], sqsem.at[0], sqsem.at[1], lax.rem(me + k, T)).start())
            loop(1, 8, lambda k: tensor_copy(
                ST.at[1, me], ST.at[1, me], agdsem.at[0, k], agdsem.at[1, k],
                lax.rem(me + 2 * k, T)).start())
        yf = y.astype(f32)
        for c in range(4):
            for i in range(4):
                OUTF[c, pl.ds(i, 16, stride=4), :] = yf[16 * i:16 * i + 16, 128 * c:128 * c + 128]
        for c in range(4):
            out[s, :, 128 * c:128 * c + 128] = OUTF[c].astype(bf16)

        if s + 1 < STEPS:
            SQR[me] = SQS[...]
            wait(SQR.at[pl.ds(0, T - 1)], sqsem.at[1])
            total = jnp.sum(SQR[...], axis=0)[0:1]
            total = jnp.broadcast_to(total, (128, 128)).T[0:64, 0:1]
            inv = lax.rsqrt(total * (1.0 / D) + norm_epsilon)

            def take(j, carry):
                q, new = carry
                NB[j] = (ST[1, j].astype(f32) * inv * gain[j]).astype(bf16)
                return project(j, q), project_kv(j, new)

            def take_direct(k, carry):
                j = lax.rem(me + T - 2 * k, T)

                @pl.when(k > 0)
                def _():
                    wait(ST.at[1, j], agdsem.at[1, k])
                tensor_copy(
                    ST.at[1, j], ST.at[1, j], agfsem.at[0, k], agfsem.at[1, k], sib).start()
                return take(j, carry)

            def take_passed(k, carry):
                j = lax.rem(sib + T - 2 * k, T)
                wait(ST.at[1, j], agfsem.at[1, k])
                return take(j, carry)

            carry = lax.fori_loop(0, 2, take_direct, (zero_query, zero_total))
            carry = lax.fori_loop(
                2, 8, lambda k, c: take_passed(k - 2, take_direct(k, c)), carry)
            q, new = lax.fori_loop(6, 8, take_passed, carry)

    wait(A1R.at[pl.ds(0, 3)], a1sem.at[0, 0])
    wait(A1R.at[pl.ds(0, 4)], a1sem.at[0, 1])
    wait(WO.at[:, pl.ds(0, CHUNK), :], wosem.at[0])
    for half in range(2):
        wait(A2R.at[0, pl.ds(0, T - 1)], a2sem.at[half, 0])
    loop(1, 8, lambda k: wait(AQ.at[me], a3dsem.at[0, k]))
    loop(0, 8, lambda k: wait(AQ.at[me], a3fsem.at[0, k]))
    wait(AOR.at[pl.ds(0, T - 1)], aosem.at[0])
    for s in range(STEPS):
        wait(QR.at[s, pl.ds(0, T - 1)], qsem.at[s, 0])
        wait(AR.at[s, pl.ds(0, T - 1)], asem.at[s, 0])
        wait(TOR.at[s, pl.ds(0, 7)], tosem.at[s, 0])
        wait(RB.at[s, pl.ds(0, 7)], rssem.at[s, 0])
    loop(1, 8, lambda k: wait(ST.at[1, me], agdsem.at[0, k]))
    loop(0, 8, lambda k: wait(ST.at[1, me], agfsem.at[0, k]))
    wait(SQR.at[pl.ds(0, T - 1)], sqsem.at[0])


def body(
    hidden_in,
    norm_gain,
    query_weight_base,
    w_key,
    w_value,
    output_weight_base,
    kv_cache,
    cache_lengths,
    adapter_shards,
    shard_order,
):
    half_dim = HEAD_DIM // 2
    exponent = np.arange(half_dim, dtype=np.float32) * np.float32(2.0 / HEAD_DIM)
    frequency = np.float32(rope_theta) ** (-exponent)
    freq = jnp.asarray(np.concatenate([frequency, frequency]).reshape(1, HEAD_DIM))
    vmem = pl.BlockSpec(memory_space=pltpu.VMEM)
    smem = pl.BlockSpec(memory_space=pltpu.SMEM)
    hbm = pl.BlockSpec(memory_space=pl.ANY)
    V = pltpu.VMEM
    dma = pltpu.SemaphoreType.DMA
    return pl.pallas_call(
        kernel,
        out_shape=jax.ShapeDtypeStruct((STEPS, 64, CHUNK), bf16),
        in_specs=[vmem, vmem, hbm, hbm, hbm, hbm, hbm, smem, vmem, vmem, vmem],
        out_specs=vmem,
        scratch_shapes=[
            V((32, 256, CHUNK), bf16),
            V((128, D), bf16),
            V((8, 2 * CHUNK, CHUNK), bf16),
            V((4, KV_HEADS, CAP, 2, HEAD_DIM), bf16),
            V((4, 64, 128), f32),
            V((2, T, 64, CHUNK), bf16),
            V((T, 64, CHUNK), bf16),
            V((128, 128), f32),
            V((128, 128), bf16),
            V((R, 128, 128), bf16),
            V((2, T, 32, 128), bf16),
            V((2, T, 32, 128), bf16),
            V((1024, 128), f32),
            V((T, 32, 128), f32),
            V((512, 128), f32),
            V((T, 256, 128), bf16),
            V((2, 128, CHUNK), bf16),
            V((128, CHUNK), bf16),
            V((8, 32, 128), bf16),
            V((T, 32, 128), bf16),
            V((1024, 128), f32),
            V((1024, 128), bf16),
            V((512, 128), f32),
            V((STEPS, T, 32, 128), bf16),
            V((STEPS, T, 32, 128), bf16),
            V((256, 128), f32),
            V((STEPS, 64, 128), f32),
            V((STEPS, 64, 128), f32),
            V((256, 128), f32),
            V((STEPS, 8, 32, 128), bf16),
            V((STEPS, T, 32, 128), bf16),
            V((64, 2 * CHUNK), bf16),
            V((STEPS, 32, 128), bf16),
            V((STEPS, 8, 32, 128), bf16),
            V((STEPS, 8, 64, CHUNK), bf16),
            V((STEPS, 8, 64, CHUNK), bf16),
            V((4, 64, 128), f32),
            V((8, 128), f32),
            V((T, 8, 128), f32),
            dma((20,)),
            dma((2,)),
            dma((2, 2)),
            dma((2, 2)),
            dma((2, 8)),
            dma((2, 8)),
            dma((2,)),
            dma((STEPS, 2)),
            dma((STEPS, 2)),
            dma((STEPS, 2)),
            dma((STEPS, 2)),
            dma((2, 8)),
            dma((2, 8)),
            dma((2,)),
        ],
        compiler_params=pltpu.CompilerParams(
            collective_id=0, has_side_effects=True, vmem_limit_bytes=56 * 2**20
        ),
        cost_estimate=pl.CostEstimate(
            flops=5 * 10**9, bytes_accessed=25 * 2**20, transcendentals=10**6
        ),
    )(
        hidden_in,
        norm_gain.reshape(T, 1, CHUNK),
        query_weight_base.reshape(32, 256, CHUNK),
        w_key.T,
        w_value.T,
        output_weight_base,
        kv_cache,
        cache_lengths,
        freq,
        adapter_shards,
        shard_order.reshape(1, 128),
    )


def solution(mesh):
    return jax.shard_map(
        body,
        mesh=mesh,
        in_specs=(
            P("rollout", None),
            P(),
            P(None, "tensor"),
            P(None, "tensor"),
            P(None, "tensor"),
            P("tensor", None),
            P(("rollout", "tensor"), None, None, None),
            P(("rollout", "tensor")),
            P(("rollout", "tensor"), None),
            P(),
        ),
        out_specs=P(None, "rollout", "tensor"),
        check_vma=False,
    )
```

```python
import jax
import jax.numpy as jnp
import numpy as np
from jax import lax
from jax.experimental import pallas as pl
from jax.experimental.pallas import tpu as pltpu
from jax.sharding import PartitionSpec as P

D = 8192
HEADS = 64
KV_HEADS = 8
HEAD_DIM = 128
RANK = 64
STEPS = 2
CAP = 256
T = 16
R = 8
CHUNK = D // T

low_rank_scale = 2.0
norm_epsilon = 1e-05
rope_theta = 500000.0
score_scale = 1.0 / np.sqrt(np.float32(HEAD_DIM))

f32 = jnp.float32
bf16 = jnp.bfloat16
MESH = pl.DeviceIdType.MESH


def mm(a, b):
    return jnp.dot(a, b, preferred_element_type=f32)


def mm_t(a, b):
    return lax.dot_general(a, b, (((1,), (1,)), ((), ())), preferred_element_type=f32)


def lanes(shape):
    return lax.broadcasted_iota(jnp.int32, shape, len(shape) - 1)


def swap_halves(x):
    return pltpu.roll(x, 64, len(x.shape) - 1)


def spread_pairs(x, ref):
    low = lanes(x.shape) < 64
    rows = x.shape[0]
    ref[pl.ds(0, rows, stride=2), :] = jnp.where(low, x, 0.0)
    ref[pl.ds(1, rows, stride=2), :] = jnp.where(low, swap_halves(x), 0.0)


def pack_rank(t):
    return t[0:32] + swap_halves(t[32:64])


def unpack_split(total):
    high = total.astype(bf16).astype(f32)
    rest = total - high
    low = lanes(total.shape) < 64
    top = jnp.where(low, high, swap_halves(rest))
    bottom = jnp.where(low, swap_halves(high), rest)
    return jnp.concatenate([top, bottom], axis=0).astype(bf16)


def kernel(
    hid, gain, wq, wk_t, wv_t, wo, kv, lens, freq, piece, order,
    out,
    WQ, WKV, WO, KV, HF, ST, NB,
    PF, CP, A1R, A2S, A2R, XF, OF, AE, AQ, BQ, BO, AOS, AOR, AOE, AO,
    Q32, QS, QR, QX, KN, VN, AF, AM, AR, AT, TOS, TOR, RSS, RB, OUTF, SQS, SQR,
    lsem, wosem, a1sem, a2sem, a3dsem, a3fsem, aosem, qsem, asem, tosem, rssem, agdsem, agfsem, sqsem,
):
    me = lax.axis_index("tensor")
    ro = lax.axis_index("rollout")
    core = lax.rem(me, 2)
    chip = me // 2
    sib = me + 1 - 2 * core

    def wait(ref, sem):
        pltpu.make_async_copy(ref, ref, sem).wait()

    def tensor_copy(src, dst, send, recv, peer):
        return pltpu.make_async_remote_copy(
            src_ref=src, dst_ref=dst, send_sem=send, recv_sem=recv,
            device_id={"tensor": peer}, device_id_type=MESH,
        )

    def loop(lo, hi, body):
        def step(k, carry):
            body(k)
            return carry
        lax.fori_loop(lo, hi, step, 0)

    barrier = pltpu.get_barrier_semaphore()
    loop(1, T, lambda k: pl.semaphore_signal(
        barrier, inc=1, device_id={"tensor": lax.rem(me + k, T)}, device_id_type=MESH))
    loop(1, R, lambda k: pl.semaphore_signal(
        barrier, inc=1, device_id={"rollout": lax.rem(ro + k, R)}, device_id_type=MESH))

    for j in range(8):
        pltpu.make_async_copy(
            wq.at[pl.ds(4 * j, 4)], WQ.at[pl.ds(4 * j, 4)], lsem.at[0]).start()
    pltpu.make_async_copy(wk_t, WKV.at[pl.ds(0, 64), :], lsem.at[16]).start()
    pltpu.make_async_copy(wv_t, WKV.at[pl.ds(64, 64), :], lsem.at[17]).start()
    for i in range(4):
        for g in range(KV_HEADS):
            pltpu.make_async_copy(
                kv.at[i, :, :, pl.ds(HEAD_DIM * g, HEAD_DIM)], KV.at[i, g], lsem.at[19]).start()

    def wo_columns(q, parity):
        return wo.at[:, pl.ds(pl.multiple_of((2 * q + parity) * CHUNK, CHUNK), CHUNK)]

    wo_rows = pl.ds(pl.multiple_of(core * CHUNK, CHUNK), CHUNK)
    loop(0, 8, lambda q: pltpu.make_async_copy(
        wo_columns(q, core), WO.at[q, wo_rows, :], lsem.at[18]).start())

    order_row = order[...]
    mine = jnp.sum(
        jnp.where(lanes((1, 128)) == ro * T + me, order_row, 0), axis=1, keepdims=True)
    is_up = jnp.broadcast_to((mine >> 5) & 1, (128, 128))
    row = lax.broadcasted_iota(jnp.int32, (128, 128), 0)
    up_row = 64 * ((row >> 2) & 1) + 4 * (row >> 3) + (row & 3)
    wanted = jnp.where(is_up == 1, up_row, row)
    pick = jnp.where(lanes((128, 128)) == wanted, 1.0, 0.0).astype(bf16)
    flat = piece[...].astype(f32)
    for r in range(128):
        PF[r:r + 1, :] = flat[:, 128 * r:128 * r + 128]
    CP[...] = mm(pick, PF[...].astype(bf16)).astype(bf16)
    A1R[ro] = CP[...]
    place = jnp.where(row == jnp.broadcast_to(order_row, (128, 128)), 1.0, 0.0).astype(bf16)

    pl.semaphore_wait(barrier, T - 1 + R - 1)

    def send_piece(peer, sem):
        pltpu.make_async_remote_copy(
            src_ref=CP, dst_ref=A1R.at[ro], send_sem=a1sem.at[0, sem],
            recv_sem=a1sem.at[1, sem], device_id={"rollout": peer}, device_id_type=MESH).start()

    loop(1, 4, lambda k: send_piece(lax.rem(ro + 2 * k, R), 0))
    other = ro + 1 - 2 * lax.rem(ro, 2)
    loop(0, 4, lambda k: send_piece(lax.rem(other + 2 * k, R), 1))
    loop(0, 8, lambda q: tensor_copy(
        wo_columns(q, 1 - core), WO.at[q, wo_rows, :], wosem.at[0], wosem.at[1], sib).start())

    def permute_hidden(j):
        for c in range(4):
            at = pl.multiple_of(CHUNK * j + 128 * c, 128)
            HF[c] = hid[:, pl.ds(at, 128)].astype(f32)
        for c in range(4):
            for i in range(4):
                ST[0, j, 16 * i:16 * i + 16, 128 * c:128 * c + 128] = (
                    HF[c, pl.ds(i, 16, stride=4), :].astype(bf16))
    loop(0, T, permute_hidden)

    Q32[320:512, :] = jnp.zeros((192, 128), f32)

    def square_sum(s, j, total):
        x = ST[s, j].astype(f32)
        x = x * x
        return total + (x[:, 0:128] + x[:, 128:256]) + (x[:, 256:384] + x[:, 384:512])

    def normalize(s, total):
        inv = lax.rsqrt(jnp.sum(total, axis=1, keepdims=True) * (1.0 / D) + norm_epsilon)
        def body(j):
            NB[j] = (ST[s, j].astype(f32) * inv * gain[j]).astype(bf16)
        loop(0, T, body)

    zero_total = jnp.zeros((64, 128), f32)
    zero_query = jnp.zeros((64, CHUNK), f32)
    normalize(0, lax.fori_loop(0, T, lambda j, t: square_sum(0, j, t), zero_total))

    def project_kv(j, new):
        columns = pl.ds(pl.multiple_of(CHUNK * j, CHUNK), CHUNK)
        return new + mm_t(NB[j], WKV[:, columns])

    for half in range(2):
        z = lax.rem(ro + half, 2)
        wait(A1R.at[pl.ds(0, 3 + half)], a1sem.at[1, half])
        for y in range(4):
            held = A1R[2 * y + z].astype(f32).reshape(T, 8, 128)
            OF[:, 8 * y:8 * y + 8, :] = held
        A2S[half] = OF[...].astype(bf16)
        loop(1, T, lambda k: tensor_copy(
            A2S.at[half, lax.rem(me + k, T)], A2R.at[z, me], a2sem.at[half, 0],
            a2sem.at[half, 1], lax.rem(me + k, T)).start())
        A2R[z, me] = A2S[half, me]

    wait(WKV.at[pl.ds(0, 64), :], lsem.at[16])
    wait(WKV.at[pl.ds(64, 64), :], lsem.at[17])
    new = lax.fori_loop(0, T, project_kv, zero_total, unroll=4)
    wait(WQ, lsem.at[0])
    for half in range(2):
        wait(A2R.at[0, pl.ds(0, T - 1)], a2sem.at[half, 1])

    for z in range(2):
        arrived = A2R[z].astype(f32).reshape(T, 4, 8, 128)
        for y in range(4):
            r = 2 * y + z
            XF[128 * r:128 * r + 128, :] = arrived[:, y].reshape(128, 128)
    FL = AOE
    for s in range(8):
        FL[pl.ds(s, 128, stride=8), :] = mm(place, XF[pl.ds(s, 128, stride=8), :].astype(bf16))
    spread_pairs(FL[0:256, :], AE)
    AQ[me] = (AE[0:256, :] + swap_halves(AE[256:512, :])).astype(bf16)
    loop(1, 8, lambda k: tensor_copy(
        AQ.at[me], AQ.at[me], a3dsem.at[0, k], a3dsem.at[1, k], lax.rem(me + 2 * k, T)).start())
    tensor_copy(AQ.at[me], AQ.at[me], a3fsem.at[0, 0], a3fsem.at[1, 0], sib).start()
    for c in range(4):
        up = (low_rank_scale * FL[pl.ds(256 + c, 64, stride=4), :]).astype(bf16)
        none = jnp.zeros_like(up)
        BQ[0, 0:64, 128 * c:128 * c + 128] = up
        BQ[0, 64:128, 128 * c:128 * c + 128] = none
        BQ[1, 0:64, 128 * c:128 * c + 128] = none
        BQ[1, 64:128, 128 * c:128 * c + 128] = up
        up = FL[pl.ds(768 + c, 64, stride=4), :].astype(bf16)
        BO[0:64, 128 * c:128 * c + 128] = up
        BO[64:128, 128 * c:128 * c + 128] = up
    AOS[...] = FL[512:768, :].astype(bf16).reshape(8, 32, 128)

    def merge(j):
        strip = pl.ds(pl.multiple_of(16 * j, 16), 16)
        for half in range(2):
            for m in range(4):
                change = mm(AQ[j, 64 * m:64 * m + 64, :], BQ[half]).reshape(4, 16, CHUNK)
                blocks = pl.ds(16 * half + 4 * m, 4)
                WQ[blocks, strip, :] = (WQ[blocks, strip, :].astype(f32) + change).astype(bf16)

    def merge_direct(k):
        j = lax.rem(me + T - 2 * k, T)

        @pl.when(k > 0)
        def _():
            wait(AQ.at[j], a3dsem.at[1, k])
            tensor_copy(AQ.at[j], AQ.at[j], a3fsem.at[0, k], a3fsem.at[1, k], sib).start()
        merge(j)

    def merge_passed(k):
        j = lax.rem(sib + T - 2 * k, T)
        wait(AQ.at[j], a3fsem.at[1, k])
        merge(j)

    def merge_both(k):
        merge_direct(k)
        merge_passed(k - 2)

    loop(0, 2, merge_direct)
    loop(2, 8, merge_both)
    loop(6, 8, merge_passed)

    low_half = lanes((8, 128)) < 64
    sub = lax.broadcasted_iota(jnp.int32, (8, 128), 0) & 3
    lengths = jnp.zeros((8, 128), jnp.int32)
    for i in range(4):
        lengths = jnp.where(sub == i, lens[i], lengths)
    wide = lanes((64, 2 * CAP))

    for s in range(STEPS):
        def project(j, q):
            return q + mm(NB[j], WQ[pl.ds(2 * j, 2)].reshape(CHUNK, CHUNK))

        if s == 0:
            q = lax.fori_loop(0, T, project, zero_query, unroll=4)
        for h in range(4):
            Q32[64 * h:64 * h + 64, :] = q[:, 128 * h:128 * h + 128]
        Q32[256:320, :] = new
        for t in range(T):
            QS[s, t] = Q32[pl.ds(t, 32, stride=16), :].astype(bf16)
        loop(1, T, lambda k: tensor_copy(
            QS.at[s, lax.rem(me + k, T)], QR.at[s, me], qsem.at[s, 0], qsem.at[s, 1],
            lax.rem(me + k, T)).start())
        QR[s, me] = QS[s, me]
        if s == 0:
            loop(1, T, lambda k: tensor_copy(
                AOS.at[lax.rem(me + k, T) // 2], AOR.at[me], aosem.at[0], aosem.at[1],
                lax.rem(me + k, T)).start())
            AOR[me] = AOS[chip]

        angles = (lengths + s).astype(f32) * freq[...]
        cosine = jnp.cos(angles)
        sine = jnp.where(low_half, -jnp.sin(angles), jnp.sin(angles))

        wait(QR.at[s, pl.ds(0, T - 1)], qsem.at[s, 1])
        got = QR[s].astype(f32)
        heads = got[:, 0:16].reshape(T, 2, 8, 128)
        heads = heads * cosine + swap_halves(heads) * sine
        QX[...] = heads.astype(bf16).astype(f32).reshape(256, 128)
        fresh = got[:, 16:24].reshape(8, 2, 8, 128)
        even, odd = fresh[:, 0], fresh[:, 1]
        low = lanes(even.shape) < 64
        key = jnp.where(low, even, swap_halves(odd))
        key = key * cosine + swap_halves(key) * sine
        KN[s] = key.astype(bf16).astype(f32).reshape(64, 128)
        VN[s] = jnp.where(low, swap_halves(even), odd).reshape(64, 128)

        if s == 0:
            wait(KV, lsem.at[19])

        def attend(i):
            queries = [QX[pl.ds(32 * g + i, 8, stride=4), :] for g in range(KV_HEADS)]
            scores = jnp.concatenate(
                [mm_t(queries[g].astype(bf16), KV[i, g].reshape(2 * CAP, HEAD_DIM))
                 for g in range(KV_HEADS)], axis=0) * score_scale
            seen = ((wide & 1) == 0) & (wide < 2 * lens[i])
            scores = jnp.where(seen, scores, -1e30)
            rows = jnp.concatenate(queries, axis=0)
            largest = jnp.max(scores, axis=1, keepdims=True)
            news, values = [], []
            for n in range(s + 1):
                k = KN[n, pl.ds(i, 8, stride=8), :]
                v = VN[n, pl.ds(i, 8, stride=8), :]
                k = jnp.broadcast_to(k[:, None, :], (8, 8, 128)).reshape(64, 128)
                values.append(jnp.broadcast_to(v[:, None, :], (8, 8, 128)).reshape(64, 128))
                news.append(jnp.sum(rows * k, axis=1, keepdims=True) * score_scale)
                largest = jnp.maximum(largest, news[-1])
            expo = jnp.exp(scores - largest)
            news = [jnp.exp(x - largest) for x in news]
            total = jnp.sum(expo, axis=1, keepdims=True)
            for x in news:
                total = total + x
            share = 1.0 / total
            weights = pltpu.roll((expo * share).astype(bf16).astype(f32), 1, 1).astype(bf16)
            result = jnp.concatenate(
                [mm(weights[8 * g:8 * g + 8], KV[i, g].reshape(2 * CAP, HEAD_DIM))
                 for g in range(KV_HEADS)], axis=0)
            for x, v in zip(news, values):
                result = result + (x * share).astype(bf16).astype(f32) * v
            AF[pl.ds(i, 64, stride=4), :] = result

        for i in range(4):
            attend(i)
        AM[s] = AF[...].astype(bf16).reshape(8, 32, 128)
        loop(1, T, lambda k: tensor_copy(
            AM.at[s, lax.rem(me + k, T) // 2], AR.at[s, me], asem.at[s, 0], asem.at[s, 1],
            lax.rem(me + k, T)).start())
        AR[s, me] = AM[s, chip]
        if s == 0:
            wait(AOR.at[pl.ds(0, T - 1)], aosem.at[1])
            blocks = AOR[...].astype(f32).reshape(T, 4, 8, 128)
            for b in range(4):
                XF[128 * b:128 * b + 128, :] = blocks[:, b].reshape(128, 128)
            spread_pairs(XF[0:512, :], AOE)
            AO[...] = AOE[...].astype(bf16)
        wait(AR.at[s, pl.ds(0, T - 1)], asem.at[s, 1])
        XF[0:512, :] = AR[s].astype(f32).reshape(512, 128)
        for h in range(8):
            for i in range(4):
                AT[16 * i:16 * i + 16, 128 * h:128 * h + 128] = (
                    XF[pl.ds(4 * h + i, 16, stride=32), :].astype(bf16))

        attended = AT[...]
        if s == 0:
            wait(WO.at[:, pl.ds(0, CHUNK), :], lsem.at[18])
            wait(WO.at[:, pl.ds(0, CHUNK), :], wosem.at[1])

        def part(k):
            q = lax.rem(chip + k, 8)
            RSS[s, q] = mm(AT[...], WO[q]).astype(bf16)
            tensor_copy(
                RSS.at[s, q], RB.at[s, chip], rssem.at[s, 0], rssem.at[s, 1],
                2 * q + core).start()
        loop(1, 8, part)
        t = mm(attended, AO[...])
        TOS[s] = pack_rank(t).astype(bf16)
        loop(1, 8, lambda k: tensor_copy(
            TOS.at[s], TOR.at[s, chip], tosem.at[s, 0], tosem.at[s, 1],
            lax.rem(me + 2 * k, T)).start())
        TOR[s, chip] = TOS[s]
        RB[s, chip] = jnp.zeros((64, CHUNK), bf16)
        y = mm(attended, WO[chip])
        y = y + ST[s, me].astype(f32)
        wait(TOR.at[s, pl.ds(0, 7)], tosem.at[s, 1])
        rank = jnp.sum(TOR[s].astype(f32), axis=0)
        y = y + low_rank_scale * mm(unpack_split(rank), BO[...])
        wait(RB.at[s, pl.ds(0, 7)], rssem.at[s, 1])
        for q in range(8):
            y = y + RB[s, q].astype(f32)
        y = y.astype(bf16)

        if s + 1 < STEPS:
            ST[1, me] = y
            squares = y.astype(f32) * y.astype(f32)
            squares = (squares[:, 0:128] + squares[:, 128:256]) + (
                squares[:, 256:384] + squares[:, 384:512])
            SQS[...] = jnp.zeros_like(SQS)
            SQS[0:1, 0:64] = jnp.sum(squares.T, axis=0, keepdims=True)
            loop(1, T, lambda k: tensor_copy(
                SQS, SQR.at[me], sqsem.at[0], sqsem.at[1], lax.rem(me + k, T)).start())
            loop(1, 8, lambda k: tensor_copy(
                ST.at[1, me], ST.at[1, me], agdsem.at[0, k], agdsem.at[1, k],
                lax.rem(me + 2 * k, T)).start())
        yf = y.astype(f32)
        for c in range(4):
            for i in range(4):
                OUTF[c, pl.ds(i, 16, stride=4), :] = yf[16 * i:16 * i + 16, 128 * c:128 * c + 128]
        for c in range(4):
            out[s, :, 128 * c:128 * c + 128] = OUTF[c].astype(bf16)

        if s + 1 < STEPS:
            SQR[me] = SQS[...]
            wait(SQR.at[pl.ds(0, T - 1)], sqsem.at[1])
            total = jnp.sum(SQR[...], axis=0)[0:1]
            total = jnp.broadcast_to(total, (128, 128)).T[0:64, 0:1]
            inv = lax.rsqrt(total * (1.0 / D) + norm_epsilon)

            def take(j, carry):
                q, new = carry
                NB[j] = (ST[1, j].astype(f32) * inv * gain[j]).astype(bf16)
                return project(j, q), project_kv(j, new)

            def take_direct(k, carry):
                j = lax.rem(me + T - 2 * k, T)

                @pl.when(k > 0)
                def _():
                    wait(ST.at[1, j], agdsem.at[1, k])
                tensor_copy(
                    ST.at[1, j], ST.at[1, j], agfsem.at[0, k], agfsem.at[1, k], sib).start()
                return take(j, carry)

            def take_passed(k, carry):
                j = lax.rem(sib + T - 2 * k, T)
                wait(ST.at[1, j], agfsem.at[1, k])
                return take(j, carry)

            carry = lax.fori_loop(0, 2, take_direct, (zero_query, zero_total))
            carry = lax.fori_loop(
                2, 8, lambda k, c: take_passed(k - 2, take_direct(k, c)), carry)
            q, new = lax.fori_loop(6, 8, take_passed, carry)

    wait(A1R.at[pl.ds(0, 3)], a1sem.at[0, 0])
    wait(A1R.at[pl.ds(0, 4)], a1sem.at[0, 1])
    wait(WO.at[:, pl.ds(0, CHUNK), :], wosem.at[0])
    for half in range(2):
        wait(A2R.at[0, pl.ds(0, T - 1)], a2sem.at[half, 0])
    loop(1, 8, lambda k: wait(AQ.at[me], a3dsem.at[0, k]))
    loop(0, 8, lambda k: wait(AQ.at[me], a3fsem.at[0, k]))
    wait(AOR.at[pl.ds(0, T - 1)], aosem.at[0])
    for s in range(STEPS):
        wait(QR.at[s, pl.ds(0, T - 1)], qsem.at[s, 0])
        wait(AR.at[s, pl.ds(0, T - 1)], asem.at[s, 0])
        wait(TOR.at[s, pl.ds(0, 7)], tosem.at[s, 0])
        wait(RB.at[s, pl.ds(0, 7)], rssem.at[s, 0])
    loop(1, 8, lambda k: wait(ST.at[1, me], agdsem.at[0, k]))
    loop(0, 8, lambda k: wait(ST.at[1, me], agfsem.at[0, k]))
    wait(SQR.at[pl.ds(0, T - 1)], sqsem.at[0])


def body(
    hidden_in,
    norm_gain,
    query_weight_base,
    w_key,
    w_value,
    output_weight_base,
    kv_cache,
    cache_lengths,
    adapter_shards,
    shard_order,
):
    half_dim = HEAD_DIM // 2
    exponent = np.arange(half_dim, dtype=np.float32) * np.float32(2.0 / HEAD_DIM)
    frequency = np.float32(rope_theta) ** (-exponent)
    freq = jnp.asarray(np.concatenate([frequency, frequency]).reshape(1, HEAD_DIM))
    vmem = pl.BlockSpec(memory_space=pltpu.VMEM)
    smem = pl.BlockSpec(memory_space=pltpu.SMEM)
    hbm = pl.BlockSpec(memory_space=pl.ANY)
    V = pltpu.VMEM
    dma = pltpu.SemaphoreType.DMA
    return pl.pallas_call(
        kernel,
        out_shape=jax.ShapeDtypeStruct((STEPS, 64, CHUNK), bf16),
        in_specs=[vmem, vmem, hbm, hbm, hbm, hbm, hbm, smem, vmem, vmem, vmem],
        out_specs=vmem,
        scratch_shapes=[
            V((32, 256, CHUNK), bf16),
            V((128, D), bf16),
            V((8, 2 * CHUNK, CHUNK), bf16),
            V((4, KV_HEADS, CAP, 2, HEAD_DIM), bf16),
            V((4, 64, 128), f32),
            V((2, T, 64, CHUNK), bf16),
            V((T, 64, CHUNK), bf16),
            V((128, 128), f32),
            V((128, 128), bf16),
            V((R, 128, 128), bf16),
            V((2, T, 32, 128), bf16),
            V((2, T, 32, 128), bf16),
            V((1024, 128), f32),
            V((T, 32, 128), f32),
            V((512, 128), f32),
            V((T, 256, 128), bf16),
            V((2, 128, CHUNK), bf16),
            V((128, CHUNK), bf16),
            V((8, 32, 128), bf16),
            V((T, 32, 128), bf16),
            V((1024, 128), f32),
            V((1024, 128), bf16),
            V((512, 128), f32),
            V((STEPS, T, 32, 128), bf16),
            V((STEPS, T, 32, 128), bf16),
            V((256, 128), f32),
            V((STEPS, 64, 128), f32),
            V((STEPS, 64, 128), f32),
            V((256, 128), f32),
            V((STEPS, 8, 32, 128), bf16),
            V((STEPS, T, 32, 128), bf16),
            V((64, 2 * CHUNK), bf16),
            V((STEPS, 32, 128), bf16),
            V((STEPS, 8, 32, 128), bf16),
            V((STEPS, 8, 64, CHUNK), bf16),
            V((STEPS, 8, 64, CHUNK), bf16),
            V((4, 64, 128), f32),
            V((8, 128), f32),
            V((T, 8, 128), f32),
            dma((20,)),
            dma((2,)),
            dma((2, 2)),
            dma((2, 2)),
            dma((2, 8)),
            dma((2, 8)),
            dma((2,)),
            dma((STEPS, 2)),
            dma((STEPS, 2)),
            dma((STEPS, 2)),
            dma((STEPS, 2)),
            dma((2, 8)),
            dma((2, 8)),
            dma((2,)),
        ],
        compiler_params=pltpu.CompilerParams(
            collective_id=0, has_side_effects=True, vmem_limit_bytes=56 * 2**20
        ),
        cost_estimate=pl.CostEstimate(
            flops=5 * 10**9, bytes_accessed=25 * 2**20, transcendentals=10**6
        ),
    )(
        hidden_in,
        norm_gain.reshape(T, 1, CHUNK),
        query_weight_base.reshape(32, 256, CHUNK),
        w_key.T,
        w_value.T,
        output_weight_base,
        kv_cache,
        cache_lengths,
        freq,
        adapter_shards,
        shard_order.reshape(1, 128),
    )


def solution(mesh):
    return jax.shard_map(
        body,
        mesh=mesh,
        in_specs=(
            P("rollout", None),
            P(),
            P(None, "tensor"),
            P(None, "tensor"),
            P(None, "tensor"),
            P("tensor", None),
            P(("rollout", "tensor"), None, None, None),
            P(("rollout", "tensor")),
            P(("rollout", "tensor"), None),
            P(),
        ),
        out_specs=P(None, "rollout", "tensor"),
        check_vma=False,
    )
```

```python
import jax
import jax.numpy as jnp
import numpy as np
from jax import lax
from jax.experimental import pallas as pl
from jax.experimental.pallas import tpu as pltpu
from jax.sharding import PartitionSpec as P

D = 8192
HEADS = 64
KV_HEADS = 8
HEAD_DIM = 128
RANK = 64
STEPS = 2
CAP = 256
T = 16
R = 8
CHUNK = D // T

low_rank_scale = 2.0
norm_epsilon = 1e-05
rope_theta = 500000.0
score_scale = 1.0 / np.sqrt(np.float32(HEAD_DIM))

f32 = jnp.float32
bf16 = jnp.bfloat16
MESH = pl.DeviceIdType.MESH


def mm(a, b):
    return jnp.dot(a, b, preferred_element_type=f32)


def mm_t(a, b):
    return lax.dot_general(a, b, (((1,), (1,)), ((), ())), preferred_element_type=f32)


def lanes(shape):
    return lax.broadcasted_iota(jnp.int32, shape, len(shape) - 1)


def swap_halves(x):
    return pltpu.roll(x, 64, len(x.shape) - 1)


def spread_pairs(x, ref):
    low = lanes(x.shape) < 64
    rows = x.shape[0]
    ref[pl.ds(0, rows, stride=2), :] = jnp.where(low, x, 0.0)
    ref[pl.ds(1, rows, stride=2), :] = jnp.where(low, swap_halves(x), 0.0)


def pack_rank(t):
    return t[0:32] + swap_halves(t[32:64])


def unpack_split(total):
    high = total.astype(bf16).astype(f32)
    rest = total - high
    low = lanes(total.shape) < 64
    top = jnp.where(low, high, swap_halves(rest))
    bottom = jnp.where(low, swap_halves(high), rest)
    return jnp.concatenate([top, bottom], axis=0).astype(bf16)


def kernel(
    hid, gain, wq, wk_t, wv_t, wo, kv, lens, freq, piece, order,
    out,
    WQ, WKV, WO, KV, HF, ST, NB,
    PF, CP, A1R, A2S, A2R, XF, OF, AE, AQ, BQ, BO, AOS, AOR, AOE, AO,
    Q32, QS, QR, QX, KN, VN, AF, AM, AR, AT, TOS, TOR, RSS, RB, OUTF, SQS, SQR,
    lsem, wosem, a1sem, a2sem, a3dsem, a3fsem, aosem, qsem, asem, tosem, rssem, agdsem, agfsem, sqsem,
):
    me = lax.axis_index("tensor")
    ro = lax.axis_index("rollout")
    core = lax.rem(me, 2)
    chip = me // 2
    sib = me + 1 - 2 * core

    def wait(ref, sem):
        pltpu.make_async_copy(ref, ref, sem).wait()

    def tensor_copy(src, dst, send, recv, peer):
        return pltpu.make_async_remote_copy(
            src_ref=src, dst_ref=dst, send_sem=send, recv_sem=recv,
            device_id={"tensor": peer}, device_id_type=MESH,
        )

    def loop(lo, hi, body):
        def step(k, carry):
            body(k)
            return carry
        lax.fori_loop(lo, hi, step, 0)

    barrier = pltpu.get_barrier_semaphore()
    loop(1, T, lambda k: pl.semaphore_signal(
        barrier, inc=1, device_id={"tensor": lax.rem(me + k, T)}, device_id_type=MESH))
    loop(1, R, lambda k: pl.semaphore_signal(
        barrier, inc=1, device_id={"rollout": lax.rem(ro + k, R)}, device_id_type=MESH))

    for j in range(8):
        pltpu.make_async_copy(
            wq.at[pl.ds(4 * j, 4)], WQ.at[pl.ds(4 * j, 4)], lsem.at[0]).start()
    pltpu.make_async_copy(wk_t, WKV.at[pl.ds(0, 64), :], lsem.at[16]).start()
    pltpu.make_async_copy(wv_t, WKV.at[pl.ds(64, 64), :], lsem.at[17]).start()
    for i in range(4):
        for g in range(KV_HEADS):
            pltpu.make_async_copy(
                kv.at[i, :, :, pl.ds(HEAD_DIM * g, HEAD_DIM)], KV.at[i, g], lsem.at[19]).start()

    def wo_columns(q, parity):
        return wo.at[:, pl.ds(pl.multiple_of((2 * q + parity) * CHUNK, CHUNK), CHUNK)]

    wo_rows = pl.ds(pl.multiple_of(core * CHUNK, CHUNK), CHUNK)
    loop(0, 8, lambda q: pltpu.make_async_copy(
        wo_columns(q, core), WO.at[q, wo_rows, :], lsem.at[18]).start())

    order_row = order[...]
    mine = jnp.sum(
        jnp.where(lanes((1, 128)) == ro * T + me, order_row, 0), axis=1, keepdims=True)
    is_up = jnp.broadcast_to((mine >> 5) & 1, (128, 128))
    row = lax.broadcasted_iota(jnp.int32, (128, 128), 0)
    up_row = 64 * ((row >> 2) & 1) + 4 * (row >> 3) + (row & 3)
    wanted = jnp.where(is_up == 1, up_row, row)
    pick = jnp.where(lanes((128, 128)) == wanted, 1.0, 0.0).astype(bf16)
    flat = piece[...].astype(f32)
    for r in range(128):
        PF[r:r + 1, :] = flat[:, 128 * r:128 * r + 128]
    CP[...] = mm(pick, PF[...].astype(bf16)).astype(bf16)
    A1R[ro] = CP[...]
    place = jnp.where(row == jnp.broadcast_to(order_row, (128, 128)), 1.0, 0.0).astype(bf16)

    pl.semaphore_wait(barrier, T - 1 + R - 1)

    def send_piece(peer, sem):
        pltpu.make_async_remote_copy(
            src_ref=CP, dst_ref=A1R.at[ro], send_sem=a1sem.at[0, sem],
            recv_sem=a1sem.at[1, sem], device_id={"rollout": peer}, device_id_type=MESH).start()

    loop(1, 4, lambda k: send_piece(lax.rem(ro + 2 * k, R), 0))
    other = ro + 1 - 2 * lax.rem(ro, 2)
    loop(0, 4, lambda k: send_piece(lax.rem(other + 2 * k, R), 1))
    loop(0, 8, lambda q: tensor_copy(
        wo_columns(q, 1 - core), WO.at[q, wo_rows, :], wosem.at[0], wosem.at[1], sib).start())

    def permute_hidden(j):
        for c in range(4):
            at = pl.multiple_of(CHUNK * j + 128 * c, 128)
            HF[c] = hid[:, pl.ds(at, 128)].astype(f32)
        for c in range(4):
            for i in range(4):
                ST[0, j, 16 * i:16 * i + 16, 128 * c:128 * c + 128] = (
                    HF[c, pl.ds(i, 16, stride=4), :].astype(bf16))
    loop(0, T, permute_hidden)

    Q32[320:512, :] = jnp.zeros((192, 128), f32)

    def square_sum(s, j, total):
        x = ST[s, j].astype(f32)
        x = x * x
        return total + (x[:, 0:128] + x[:, 128:256]) + (x[:, 256:384] + x[:, 384:512])

    def normalize(s, total):
        inv = lax.rsqrt(jnp.sum(total, axis=1, keepdims=True) * (1.0 / D) + norm_epsilon)
        def body(j):
            NB[j] = (ST[s, j].astype(f32) * inv * gain[j]).astype(bf16)
        loop(0, T, body)

    zero_total = jnp.zeros((64, 128), f32)
    zero_query = jnp.zeros((64, CHUNK), f32)
    normalize(0, lax.fori_loop(0, T, lambda j, t: square_sum(0, j, t), zero_total))

    def project_kv(j, new):
        columns = pl.ds(pl.multiple_of(CHUNK * j, CHUNK), CHUNK)
        return new + mm_t(NB[j], WKV[:, columns])

    for half in range(2):
        z = lax.rem(ro + half, 2)
        wait(A1R.at[pl.ds(0, 3 + half)], a1sem.at[1, half])
        for y in range(4):
            held = A1R[2 * y + z].astype(f32).reshape(T, 8, 128)
            OF[:, 8 * y:8 * y + 8, :] = held
        A2S[half] = OF[...].astype(bf16)
        loop(1, T, lambda k: tensor_copy(
            A2S.at[half, lax.rem(me + k, T)], A2R.at[z, me], a2sem.at[half, 0],
            a2sem.at[half, 1], lax.rem(me + k, T)).start())
        A2R[z, me] = A2S[half, me]

    wait(WKV.at[pl.ds(0, 64), :], lsem.at[16])
    wait(WKV.at[pl.ds(64, 64), :], lsem.at[17])
    new = lax.fori_loop(0, T, project_kv, zero_total, unroll=4)
    wait(WQ, lsem.at[0])
    for half in range(2):
        wait(A2R.at[0, pl.ds(0, T - 1)], a2sem.at[half, 1])

    for z in range(2):
        arrived = A2R[z].astype(f32).reshape(T, 4, 8, 128)
        for y in range(4):
            r = 2 * y + z
            XF[128 * r:128 * r + 128, :] = arrived[:, y].reshape(128, 128)
    FL = AOE
    for s in range(8):
        FL[pl.ds(s, 128, stride=8), :] = mm(place, XF[pl.ds(s, 128, stride=8), :].astype(bf16))
    spread_pairs(FL[0:256, :], AE)
    AQ[me] = (AE[0:256, :] + swap_halves(AE[256:512, :])).astype(bf16)
    loop(1, 8, lambda k: tensor_copy(
        AQ.at[me], AQ.at[me], a3dsem.at[0, k], a3dsem.at[1, k], lax.rem(me + 2 * k, T)).start())
    tensor_copy(AQ.at[me], AQ.at[me], a3fsem.at[0, 0], a3fsem.at[1, 0], sib).start()
    for c in range(4):
        up = (low_rank_scale * FL[pl.ds(256 + c, 64, stride=4), :]).astype(bf16)
        none = jnp.zeros_like(up)
        BQ[0, 0:64, 128 * c:128 * c + 128] = up
        BQ[0, 64:128, 128 * c:128 * c + 128] = none
        BQ[1, 0:64, 128 * c:128 * c + 128] = none
        BQ[1, 64:128, 128 * c:128 * c + 128] = up
        up = FL[pl.ds(768 + c, 64, stride=4), :].astype(bf16)
        BO[0:64, 128 * c:128 * c + 128] = up
        BO[64:128, 128 * c:128 * c + 128] = up
    AOS[...] = FL[512:768, :].astype(bf16).reshape(8, 32, 128)

    def merge(j):
        strip = pl.ds(pl.multiple_of(16 * j, 16), 16)
        for half in range(2):
            blocks = pl.ds(16 * half, 16)
            for n in range(2):
                columns = slice(256 * n, 256 * n + 256)
                change = mm(AQ[j], BQ[half, :, columns]).reshape(16, 16, 256)
                WQ[blocks, strip, columns] = (
                    WQ[blocks, strip, columns].astype(f32) + change).astype(bf16)

    def own_side(k):
        return lax.rem(me + T - 2 * k, T)

    def other_side(k):
        return lax.rem(sib + T - 2 * k, T)

    def pass_on_strips(k):
        j = own_side(k)
        wait(AQ.at[j], a3dsem.at[1, k])
        tensor_copy(AQ.at[j], AQ.at[j], a3fsem.at[0, k], a3fsem.at[1, k], sib).start()

    merge(me)
    loop(1, 8, pass_on_strips)
    loop(1, 8, lambda k: merge(own_side(k)))
    loop(0, 8, lambda k: wait(AQ.at[other_side(k)], a3fsem.at[1, k]))
    loop(0, 8, lambda k: merge(other_side(k)))

    low_half = lanes((8, 128)) < 64
    sub = lax.broadcasted_iota(jnp.int32, (8, 128), 0) & 3
    lengths = jnp.zeros((8, 128), jnp.int32)
    for i in range(4):
        lengths = jnp.where(sub == i, lens[i], lengths)
    wide = lanes((64, 2 * CAP))

    for s in range(STEPS):
        def project(j, q):
            return q + mm(NB[j], WQ[pl.ds(2 * j, 2)].reshape(CHUNK, CHUNK))

        if s == 0:
            q = lax.fori_loop(0, T, project, zero_query, unroll=4)
        for h in range(4):
            Q32[64 * h:64 * h + 64, :] = q[:, 128 * h:128 * h + 128]
        Q32[256:320, :] = new
        for t in range(T):
            QS[s, t] = Q32[pl.ds(t, 32, stride=16), :].astype(bf16)
        loop(1, T, lambda k: tensor_copy(
            QS.at[s, lax.rem(me + k, T)], QR.at[s, me], qsem.at[s, 0], qsem.at[s, 1],
            lax.rem(me + k, T)).start())
        QR[s, me] = QS[s, me]
        if s == 0:
            loop(1, T, lambda k: tensor_copy(
                AOS.at[lax.rem(me + k, T) // 2], AOR.at[me], aosem.at[0], aosem.at[1],
                lax.rem(me + k, T)).start())
            AOR[me] = AOS[chip]

        angles = (lengths + s).astype(f32) * freq[...]
        cosine = jnp.cos(angles)
        sine = jnp.where(low_half, -jnp.sin(angles), jnp.sin(angles))

        wait(QR.at[s, pl.ds(0, T - 1)], qsem.at[s, 1])
        got = QR[s].astype(f32)
        heads = got[:, 0:16].reshape(T, 2, 8, 128)
        heads = heads * cosine + swap_halves(heads) * sine
        QX[...] = heads.astype(bf16).astype(f32).reshape(256, 128)
        fresh = got[:, 16:24].reshape(8, 2, 8, 128)
        even, odd = fresh[:, 0], fresh[:, 1]
        low = lanes(even.shape) < 64
        key = jnp.where(low, even, swap_halves(odd))
        key = key * cosine + swap_halves(key) * sine
        KN[s] = key.astype(bf16).astype(f32).reshape(64, 128)
        VN[s] = jnp.where(low, swap_halves(even), odd).reshape(64, 128)

        if s == 0:
            wait(KV, lsem.at[19])

        def attend(i):
            queries = [QX[pl.ds(32 * g + i, 8, stride=4), :] for g in range(KV_HEADS)]
            scores = jnp.concatenate(
                [mm_t(queries[g].astype(bf16), KV[i, g].reshape(2 * CAP, HEAD_DIM))
                 for g in range(KV_HEADS)], axis=0) * score_scale
            seen = ((wide & 1) == 0) & (wide < 2 * lens[i])
            scores = jnp.where(seen, scores, -1e30)
            rows = jnp.concatenate(queries, axis=0)
            largest = jnp.max(scores, axis=1, keepdims=True)
            news, values = [], []
            for n in range(s + 1):
                k = KN[n, pl.ds(i, 8, stride=8), :]
                v = VN[n, pl.ds(i, 8, stride=8), :]
                k = jnp.broadcast_to(k[:, None, :], (8, 8, 128)).reshape(64, 128)
                values.append(jnp.broadcast_to(v[:, None, :], (8, 8, 128)).reshape(64, 128))
                news.append(jnp.sum(rows * k, axis=1, keepdims=True) * score_scale)
                largest = jnp.maximum(largest, news[-1])
            expo = jnp.exp(scores - largest)
            news = [jnp.exp(x - largest) for x in news]
            total = jnp.sum(expo, axis=1, keepdims=True)
            for x in news:
                total = total + x
            share = 1.0 / total
            weights = pltpu.roll((expo * share).astype(bf16).astype(f32), 1, 1).astype(bf16)
            result = jnp.concatenate(
                [mm(weights[8 * g:8 * g + 8], KV[i, g].reshape(2 * CAP, HEAD_DIM))
                 for g in range(KV_HEADS)], axis=0)
            for x, v in zip(news, values):
                result = result + (x * share).astype(bf16).astype(f32) * v
            AF[pl.ds(i, 64, stride=4), :] = result

        for i in range(4):
            attend(i)
        AM[s] = AF[...].astype(bf16).reshape(8, 32, 128)
        loop(1, T, lambda k: tensor_copy(
            AM.at[s, lax.rem(me + k, T) // 2], AR.at[s, me], asem.at[s, 0], asem.at[s, 1],
            lax.rem(me + k, T)).start())
        AR[s, me] = AM[s, chip]
        if s == 0:
            wait(AOR.at[pl.ds(0, T - 1)], aosem.at[1])
            blocks = AOR[...].astype(f32).reshape(T, 4, 8, 128)
            for b in range(4):
                XF[128 * b:128 * b + 128, :] = blocks[:, b].reshape(128, 128)
            spread_pairs(XF[0:512, :], AOE)
            AO[...] = AOE[...].astype(bf16)
        wait(AR.at[s, pl.ds(0, T - 1)], asem.at[s, 1])
        XF[0:512, :] = AR[s].astype(f32).reshape(512, 128)
        for h in range(8):
            for i in range(4):
                AT[16 * i:16 * i + 16, 128 * h:128 * h + 128] = (
                    XF[pl.ds(4 * h + i, 16, stride=32), :].astype(bf16))

        attended = AT[...]
        if s == 0:
            wait(WO.at[:, pl.ds(0, CHUNK), :], lsem.at[18])
            wait(WO.at[:, pl.ds(0, CHUNK), :], wosem.at[1])

        def part(k):
            q = lax.rem(chip + k, 8)
            RSS[s, q] = mm(AT[...], WO[q]).astype(bf16)
            tensor_copy(
                RSS.at[s, q], RB.at[s, chip], rssem.at[s, 0], rssem.at[s, 1],
                2 * q + core).start()
        loop(1, 8, part)
        t = mm(attended, AO[...])
        TOS[s] = pack_rank(t).astype(bf16)
        loop(1, 8, lambda k: tensor_copy(
            TOS.at[s], TOR.at[s, chip], tosem.at[s, 0], tosem.at[s, 1],
            lax.rem(me + 2 * k, T)).start())
        TOR[s, chip] = TOS[s]
        RB[s, chip] = jnp.zeros((64, CHUNK), bf16)
        y = mm(attended, WO[chip])
        y = y + ST[s, me].astype(f32)
        wait(TOR.at[s, pl.ds(0, 7)], tosem.at[s, 1])
        rank = jnp.sum(TOR[s].astype(f32), axis=0)
        y = y + low_rank_scale * mm(unpack_split(rank), BO[...])
        wait(RB.at[s, pl.ds(0, 7)], rssem.at[s, 1])
        for q in range(8):
            y = y + RB[s, q].astype(f32)
        y = y.astype(bf16)

        if s + 1 < STEPS:
            ST[1, me] = y
            squares = y.astype(f32) * y.astype(f32)
            squares = (squares[:, 0:128] + squares[:, 128:256]) + (
                squares[:, 256:384] + squares[:, 384:512])
            SQS[...] = jnp.zeros_like(SQS)
            SQS[0:1, 0:64] = jnp.sum(squares.T, axis=0, keepdims=True)
            loop(1, T, lambda k: tensor_copy(
                SQS, SQR.at[me], sqsem.at[0], sqsem.at[1], lax.rem(me + k, T)).start())
            loop(1, 8, lambda k: tensor_copy(
                ST.at[1, me], ST.at[1, me], agdsem.at[0, k], agdsem.at[1, k],
                lax.rem(me + 2 * k, T)).start())
            tensor_copy(
                ST.at[1, me], ST.at[1, me], agfsem.at[0, 0], agfsem.at[1, 0], sib).start()
        yf = y.astype(f32)
        for c in range(4):
            for i in range(4):
                OUTF[c, pl.ds(i, 16, stride=4), :] = yf[16 * i:16 * i + 16, 128 * c:128 * c + 128]
        for c in range(4):
            out[s, :, 128 * c:128 * c + 128] = OUTF[c].astype(bf16)

        if s + 1 < STEPS:
            SQR[me] = SQS[...]
            wait(SQR.at[pl.ds(0, T - 1)], sqsem.at[1])
            total = jnp.sum(SQR[...], axis=0)[0:1]
            total = jnp.broadcast_to(total, (128, 128)).T[0:64, 0:1]
            inv = lax.rsqrt(total * (1.0 / D) + norm_epsilon)

            def take(j, carry):
                q, new = carry
                NB[j] = (ST[1, j].astype(f32) * inv * gain[j]).astype(bf16)
                return project(j, q), project_kv(j, new)

            def pass_on_stream(k):
                j = own_side(k)
                wait(ST.at[1, j], agdsem.at[1, k])
                tensor_copy(
                    ST.at[1, j], ST.at[1, j], agfsem.at[0, k], agfsem.at[1, k], sib).start()

            loop(1, 8, pass_on_stream)
            carry = lax.fori_loop(
                0, 8, lambda k, c: take(own_side(k), c), (zero_query, zero_total), unroll=4)
            loop(0, 8, lambda k: wait(ST.at[1, other_side(k)], agfsem.at[1, k]))
            q, new = lax.fori_loop(
                0, 8, lambda k, c: take(other_side(k), c), carry, unroll=4)

    wait(A1R.at[pl.ds(0, 3)], a1sem.at[0, 0])
    wait(A1R.at[pl.ds(0, 4)], a1sem.at[0, 1])
    wait(WO.at[:, pl.ds(0, CHUNK), :], wosem.at[0])
    for half in range(2):
        wait(A2R.at[0, pl.ds(0, T - 1)], a2sem.at[half, 0])
    loop(1, 8, lambda k: wait(AQ.at[me], a3dsem.at[0, k]))
    loop(0, 8, lambda k: wait(AQ.at[me], a3fsem.at[0, k]))
    wait(AOR.at[pl.ds(0, T - 1)], aosem.at[0])
    for s in range(STEPS):
        wait(QR.at[s, pl.ds(0, T - 1)], qsem.at[s, 0])
        wait(AR.at[s, pl.ds(0, T - 1)], asem.at[s, 0])
        wait(TOR.at[s, pl.ds(0, 7)], tosem.at[s, 0])
        wait(RB.at[s, pl.ds(0, 7)], rssem.at[s, 0])
    loop(1, 8, lambda k: wait(ST.at[1, me], agdsem.at[0, k]))
    loop(0, 8, lambda k: wait(ST.at[1, me], agfsem.at[0, k]))
    wait(SQR.at[pl.ds(0, T - 1)], sqsem.at[0])


def body(
    hidden_in,
    norm_gain,
    query_weight_base,
    w_key,
    w_value,
    output_weight_base,
    kv_cache,
    cache_lengths,
    adapter_shards,
    shard_order,
):
    half_dim = HEAD_DIM // 2
    exponent = np.arange(half_dim, dtype=np.float32) * np.float32(2.0 / HEAD_DIM)
    frequency = np.float32(rope_theta) ** (-exponent)
    freq = jnp.asarray(np.concatenate([frequency, frequency]).reshape(1, HEAD_DIM))
    vmem = pl.BlockSpec(memory_space=pltpu.VMEM)
    smem = pl.BlockSpec(memory_space=pltpu.SMEM)
    hbm = pl.BlockSpec(memory_space=pl.ANY)
    V = pltpu.VMEM
    dma = pltpu.SemaphoreType.DMA
    return pl.pallas_call(
        kernel,
        out_shape=jax.ShapeDtypeStruct((STEPS, 64, CHUNK), bf16),
        in_specs=[vmem, vmem, hbm, hbm, hbm, hbm, hbm, smem, vmem, vmem, vmem],
        out_specs=vmem,
        scratch_shapes=[
            V((32, 256, CHUNK), bf16),
            V((128, D), bf16),
            V((8, 2 * CHUNK, CHUNK), bf16),
            V((4, KV_HEADS, CAP, 2, HEAD_DIM), bf16),
            V((4, 64, 128), f32),
            V((2, T, 64, CHUNK), bf16),
            V((T, 64, CHUNK), bf16),
            V((128, 128), f32),
            V((128, 128), bf16),
            V((R, 128, 128), bf16),
            V((2, T, 32, 128), bf16),
            V((2, T, 32, 128), bf16),
            V((1024, 128), f32),
            V((T, 32, 128), f32),
            V((512, 128), f32),
            V((T, 256, 128), bf16),
            V((2, 128, CHUNK), bf16),
            V((128, CHUNK), bf16),
            V((8, 32, 128), bf16),
            V((T, 32, 128), bf16),
            V((1024, 128), f32),
            V((1024, 128), bf16),
            V((512, 128), f32),
            V((STEPS, T, 32, 128), bf16),
            V((STEPS, T, 32, 128), bf16),
            V((256, 128), f32),
            V((STEPS, 64, 128), f32),
            V((STEPS, 64, 128), f32),
            V((256, 128), f32),
            V((STEPS, 8, 32, 128), bf16),
            V((STEPS, T, 32, 128), bf16),
            V((64, 2 * CHUNK), bf16),
            V((STEPS, 32, 128), bf16),
            V((STEPS, 8, 32, 128), bf16),
            V((STEPS, 8, 64, CHUNK), bf16),
            V((STEPS, 8, 64, CHUNK), bf16),
            V((4, 64, 128), f32),
            V((8, 128), f32),
            V((T, 8, 128), f32),
            dma((20,)),
            dma((2,)),
            dma((2, 2)),
            dma((2, 2)),
            dma((2, 8)),
            dma((2, 8)),
            dma((2,)),
            dma((STEPS, 2)),
            dma((STEPS, 2)),
            dma((STEPS, 2)),
            dma((STEPS, 2)),
            dma((2, 8)),
            dma((2, 8)),
            dma((2,)),
        ],
        compiler_params=pltpu.CompilerParams(
            collective_id=0, has_side_effects=True, vmem_limit_bytes=56 * 2**20
        ),
        cost_estimate=pl.CostEstimate(
            flops=5 * 10**9, bytes_accessed=25 * 2**20, transcendentals=10**6
        ),
    )(
        hidden_in,
        norm_gain.reshape(T, 1, CHUNK),
        query_weight_base.reshape(32, 256, CHUNK),
        w_key.T,
        w_value.T,
        output_weight_base,
        kv_cache,
        cache_lengths,
        freq,
        adapter_shards,
        shard_order.reshape(1, 128),
    )


def solution(mesh):
    return jax.shard_map(
        body,
        mesh=mesh,
        in_specs=(
            P("rollout", None),
            P(),
            P(None, "tensor"),
            P(None, "tensor"),
            P(None, "tensor"),
            P("tensor", None),
            P(("rollout", "tensor"), None, None, None),
            P(("rollout", "tensor")),
            P(("rollout", "tensor"), None),
            P(),
        ),
        out_specs=P(None, "rollout", "tensor"),
        check_vma=False,
    )
```

```python
import jax
import jax.numpy as jnp
import numpy as np
from jax import lax
from jax.experimental import pallas as pl
from jax.experimental.pallas import tpu as pltpu
from jax.sharding import PartitionSpec as P

D = 8192
HEADS = 64
KV_HEADS = 8
HEAD_DIM = 128
RANK = 64
STEPS = 2
CAP = 256
T = 16
R = 8
CHUNK = D // T

low_rank_scale = 2.0
norm_epsilon = 1e-05
rope_theta = 500000.0
score_scale = 1.0 / np.sqrt(np.float32(HEAD_DIM))

f32 = jnp.float32
bf16 = jnp.bfloat16
MESH = pl.DeviceIdType.MESH


def mm(a, b):
    return jnp.dot(a, b, preferred_element_type=f32)


def mm_t(a, b):
    return lax.dot_general(a, b, (((1,), (1,)), ((), ())), preferred_element_type=f32)


def lanes(shape):
    return lax.broadcasted_iota(jnp.int32, shape, len(shape) - 1)


def swap_halves(x):
    return pltpu.roll(x, 64, len(x.shape) - 1)


def spread_pairs(x, ref):
    low = lanes(x.shape) < 64
    rows = x.shape[0]
    ref[pl.ds(0, rows, stride=2), :] = jnp.where(low, x, 0.0)
    ref[pl.ds(1, rows, stride=2), :] = jnp.where(low, swap_halves(x), 0.0)


def pack_rank(t):
    return t[0:32] + swap_halves(t[32:64])


def unpack_split(total):
    high = total.astype(bf16).astype(f32)
    rest = total - high
    low = lanes(total.shape) < 64
    top = jnp.where(low, high, swap_halves(rest))
    bottom = jnp.where(low, swap_halves(high), rest)
    return jnp.concatenate([top, bottom], axis=0).astype(bf16)


def kernel(
    hid, gain, wq, wk_t, wv_t, wo, kv, lens, freq, piece, order,
    out,
    WQ, WKV, WO, KV, HF, ST, NB,
    PF, CP, A1R, A2S, A2R, XF, OF, AE, AQ, BQ, BO, AOS, AOR, AOE, AO,
    Q32, QS, QR, QX, KN, VN, AF, AM, AR, AT, TOS, TOR, RSS, RB, OUTF, SQS, SQR, DI, KEYS, VALS,
    lsem, wosem, a1sem, a2sem, a3dsem, a3fsem, aosem, qsem, asem, tosem, rssem, agdsem, agfsem, sqsem,
):
    me = lax.axis_index("tensor")
    ro = lax.axis_index("rollout")
    core = lax.rem(me, 2)
    chip = me // 2
    sib = me + 1 - 2 * core

    def wait(ref, sem):
        pltpu.make_async_copy(ref, ref, sem).wait()

    def tensor_copy(src, dst, send, recv, peer):
        return pltpu.make_async_remote_copy(
            src_ref=src, dst_ref=dst, send_sem=send, recv_sem=recv,
            device_id={"tensor": peer}, device_id_type=MESH,
        )

    def loop(lo, hi, body):
        def step(k, carry):
            body(k)
            return carry
        lax.fori_loop(lo, hi, step, 0)

    barrier = pltpu.get_barrier_semaphore()
    loop(1, T, lambda k: pl.semaphore_signal(
        barrier, inc=1, device_id={"tensor": lax.rem(me + k, T)}, device_id_type=MESH))
    loop(1, R, lambda k: pl.semaphore_signal(
        barrier, inc=1, device_id={"rollout": lax.rem(ro + k, R)}, device_id_type=MESH))

    for j in range(8):
        pltpu.make_async_copy(
            wq.at[pl.ds(4 * j, 4)], WQ.at[pl.ds(4 * j, 4)], lsem.at[0]).start()
    pltpu.make_async_copy(wk_t, WKV.at[pl.ds(0, 64), :], lsem.at[16]).start()
    pltpu.make_async_copy(wv_t, WKV.at[pl.ds(64, 64), :], lsem.at[17]).start()
    for i in range(4):
        for g in range(KV_HEADS):
            pltpu.make_async_copy(
                kv.at[i, :, :, pl.ds(HEAD_DIM * g, HEAD_DIM)], KV.at[i, g], lsem.at[19]).start()

    def wo_columns(q, parity):
        return wo.at[:, pl.ds(pl.multiple_of((2 * q + parity) * CHUNK, CHUNK), CHUNK)]

    wo_rows = pl.ds(pl.multiple_of(core * CHUNK, CHUNK), CHUNK)
    loop(0, 8, lambda q: pltpu.make_async_copy(
        wo_columns(q, core), WO.at[q, wo_rows, :], lsem.at[18]).start())

    order_row = order[...]
    mine = jnp.sum(
        jnp.where(lanes((1, 128)) == ro * T + me, order_row, 0), axis=1, keepdims=True)
    is_up = jnp.broadcast_to((mine >> 5) & 1, (128, 128))
    row = lax.broadcasted_iota(jnp.int32, (128, 128), 0)
    up_row = 64 * ((row >> 2) & 1) + 4 * (row >> 3) + (row & 3)
    wanted = jnp.where(is_up == 1, up_row, row)
    pick = jnp.where(lanes((128, 128)) == wanted, 1.0, 0.0).astype(bf16)
    flat = piece[...].astype(f32)
    for r in range(128):
        PF[r:r + 1, :] = flat[:, 128 * r:128 * r + 128]
    CP[...] = mm(pick, PF[...].astype(bf16)).astype(bf16)
    A1R[ro] = CP[...]
    place = jnp.where(row == jnp.broadcast_to(order_row, (128, 128)), 1.0, 0.0).astype(bf16)

    pl.semaphore_wait(barrier, T - 1 + R - 1)

    def send_piece(peer, sem):
        pltpu.make_async_remote_copy(
            src_ref=CP, dst_ref=A1R.at[ro], send_sem=a1sem.at[0, sem],
            recv_sem=a1sem.at[1, sem], device_id={"rollout": peer}, device_id_type=MESH).start()

    loop(1, 4, lambda k: send_piece(lax.rem(ro + 2 * k, R), 0))
    other = ro + 1 - 2 * lax.rem(ro, 2)
    loop(0, 4, lambda k: send_piece(lax.rem(other + 2 * k, R), 1))
    loop(0, 8, lambda q: tensor_copy(
        wo_columns(q, 1 - core), WO.at[q, wo_rows, :], wosem.at[0], wosem.at[1], sib).start())

    def permute_hidden(j):
        for c in range(4):
            at = pl.multiple_of(CHUNK * j + 128 * c, 128)
            HF[c] = hid[:, pl.ds(at, 128)].astype(f32)
        for c in range(4):
            for i in range(4):
                ST[0, j, 16 * i:16 * i + 16, 128 * c:128 * c + 128] = (
                    HF[c, pl.ds(i, 16, stride=4), :].astype(bf16))
    loop(0, T, permute_hidden)

    Q32[320:512, :] = jnp.zeros((192, 128), f32)

    def square_sum(s, j, total):
        x = ST[s, j].astype(f32)
        x = x * x
        return total + (x[:, 0:128] + x[:, 128:256]) + (x[:, 256:384] + x[:, 384:512])

    def normalize(s, total):
        inv = lax.rsqrt(jnp.sum(total, axis=1, keepdims=True) * (1.0 / D) + norm_epsilon)
        def body(j):
            NB[j] = (ST[s, j].astype(f32) * inv * gain[j]).astype(bf16)
        loop(0, T, body)

    zero_total = jnp.zeros((64, 128), f32)
    zero_query = jnp.zeros((64, CHUNK), f32)
    normalize(0, lax.fori_loop(0, T, lambda j, t: square_sum(0, j, t), zero_total))

    def project_kv(j, new):
        columns = pl.ds(pl.multiple_of(CHUNK * j, CHUNK), CHUNK)
        return new + mm_t(NB[j], WKV[:, columns])

    for half in range(2):
        z = lax.rem(ro + half, 2)
        wait(A1R.at[pl.ds(0, 3 + half)], a1sem.at[1, half])
        for y in range(4):
            held = A1R[2 * y + z].astype(f32).reshape(T, 8, 128)
            OF[:, 8 * y:8 * y + 8, :] = held
        A2S[half] = OF[...].astype(bf16)
        loop(1, T, lambda k: tensor_copy(
            A2S.at[half, lax.rem(me + k, T)], A2R.at[z, me], a2sem.at[half, 0],
            a2sem.at[half, 1], lax.rem(me + k, T)).start())
        A2R[z, me] = A2S[half, me]

    wait(WKV.at[pl.ds(0, 64), :], lsem.at[16])
    wait(WKV.at[pl.ds(64, 64), :], lsem.at[17])
    new = lax.fori_loop(0, T, project_kv, zero_total, unroll=4)
    wait(WQ, lsem.at[0])
    for half in range(2):
        wait(A2R.at[0, pl.ds(0, T - 1)], a2sem.at[half, 1])

    for z in range(2):
        arrived = A2R[z].astype(f32).reshape(T, 4, 8, 128)
        for y in range(4):
            r = 2 * y + z
            XF[128 * r:128 * r + 128, :] = arrived[:, y].reshape(128, 128)
    FL = AOE
    for s in range(8):
        FL[pl.ds(s, 128, stride=8), :] = mm(place, XF[pl.ds(s, 128, stride=8), :].astype(bf16))
    spread_pairs(FL[0:256, :], AE)
    AQ[me] = (AE[0:256, :] + swap_halves(AE[256:512, :])).astype(bf16)
    loop(1, 8, lambda k: tensor_copy(
        AQ.at[me], AQ.at[me], a3dsem.at[0, k], a3dsem.at[1, k], lax.rem(me + 2 * k, T)).start())
    tensor_copy(AQ.at[me], AQ.at[me], a3fsem.at[0, 0], a3fsem.at[1, 0], sib).start()
    for c in range(4):
        up = (low_rank_scale * FL[pl.ds(256 + c, 64, stride=4), :]).astype(bf16)
        none = jnp.zeros_like(up)
        BQ[0, 0:64, 128 * c:128 * c + 128] = up
        BQ[0, 64:128, 128 * c:128 * c + 128] = none
        BQ[1, 0:64, 128 * c:128 * c + 128] = none
        BQ[1, 64:128, 128 * c:128 * c + 128] = up
        up = FL[pl.ds(768 + c, 64, stride=4), :].astype(bf16)
        BO[0:64, 128 * c:128 * c + 128] = up
        BO[64:128, 128 * c:128 * c + 128] = up
    AOS[...] = FL[512:768, :].astype(bf16).reshape(8, 32, 128)

    def merge(j):
        strip = pl.ds(pl.multiple_of(16 * j, 16), 16)
        for half in range(2):
            blocks = pl.ds(16 * half, 16)
            for n in range(2):
                columns = slice(256 * n, 256 * n + 256)
                change = mm(AQ[j], BQ[half, :, columns]).reshape(16, 16, 256)
                WQ[blocks, strip, columns] = (
                    WQ[blocks, strip, columns].astype(f32) + change).astype(bf16)

    def own_side(k):
        return lax.rem(me + T - 2 * k, T)

    def other_side(k):
        return lax.rem(sib + T - 2 * k, T)

    def pass_on_strips(k):
        j = own_side(k)
        wait(AQ.at[j], a3dsem.at[1, k])
        tensor_copy(AQ.at[j], AQ.at[j], a3fsem.at[0, k], a3fsem.at[1, k], sib).start()

    wait(KV, lsem.at[19])

    def part_cache(n):
        i, g = n // KV_HEADS, lax.rem(n, KV_HEADS)
        DI[...] = KV[i, g].reshape(2 * CAP, HEAD_DIM).astype(f32)
        KEYS[i, g] = DI[pl.ds(0, CAP, stride=2), :].astype(bf16)
        VALS[i, g] = DI[pl.ds(1, CAP, stride=2), :].astype(bf16)

    merge(me)
    loop(0, 4 * KV_HEADS, part_cache)
    loop(1, 8, pass_on_strips)
    loop(1, 8, lambda k: merge(own_side(k)))
    loop(0, 8, lambda k: wait(AQ.at[other_side(k)], a3fsem.at[1, k]))
    loop(0, 8, lambda k: merge(other_side(k)))

    low_half = lanes((8, 128)) < 64
    sub = lax.broadcasted_iota(jnp.int32, (8, 128), 0) & 3
    lengths = jnp.zeros((8, 128), jnp.int32)
    for i in range(4):
        lengths = jnp.where(sub == i, lens[i], lengths)
    wide = lanes((64, CAP))

    for s in range(STEPS):
        def project(j, q):
            return q + mm(NB[j], WQ[pl.ds(2 * j, 2)].reshape(CHUNK, CHUNK))

        if s == 0:
            q = lax.fori_loop(0, T, project, zero_query, unroll=4)
        for h in range(4):
            Q32[64 * h:64 * h + 64, :] = q[:, 128 * h:128 * h + 128]
        Q32[256:320, :] = new
        for t in range(T):
            QS[s, t] = Q32[pl.ds(t, 32, stride=16), :].astype(bf16)
        loop(1, T, lambda k: tensor_copy(
            QS.at[s, lax.rem(me + k, T)], QR.at[s, me], qsem.at[s, 0], qsem.at[s, 1],
            lax.rem(me + k, T)).start())
        QR[s, me] = QS[s, me]
        if s == 0:
            loop(1, T, lambda k: tensor_copy(
                AOS.at[lax.rem(me + k, T) // 2], AOR.at[me], aosem.at[0], aosem.at[1],
                lax.rem(me + k, T)).start())
            AOR[me] = AOS[chip]

        angles = (lengths + s).astype(f32) * freq[...]
        cosine = jnp.cos(angles)
        sine = jnp.where(low_half, -jnp.sin(angles), jnp.sin(angles))

        wait(QR.at[s, pl.ds(0, T - 1)], qsem.at[s, 1])
        got = QR[s].astype(f32)
        heads = got[:, 0:16].reshape(T, 2, 8, 128)
        heads = heads * cosine + swap_halves(heads) * sine
        QX[...] = heads.astype(bf16).astype(f32).reshape(256, 128)
        fresh = got[:, 16:24].reshape(8, 2, 8, 128)
        even, odd = fresh[:, 0], fresh[:, 1]
        low = lanes(even.shape) < 64
        key = jnp.where(low, even, swap_halves(odd))
        key = key * cosine + swap_halves(key) * sine
        KN[s] = key.astype(bf16).astype(f32).reshape(64, 128)
        VN[s] = jnp.where(low, swap_halves(even), odd).reshape(64, 128)


        def attend(i):
            queries = [QX[pl.ds(32 * g + i, 8, stride=4), :] for g in range(KV_HEADS)]
            scores = jnp.concatenate(
                [mm_t(queries[g].astype(bf16), KEYS[i, g])
                 for g in range(KV_HEADS)], axis=0) * score_scale
            scores = jnp.where(wide < lens[i], scores, -1e30)
            rows = jnp.concatenate(queries, axis=0)
            largest = jnp.max(scores, axis=1, keepdims=True)
            news, values = [], []
            for n in range(s + 1):
                k = KN[n, pl.ds(i, 8, stride=8), :]
                v = VN[n, pl.ds(i, 8, stride=8), :]
                k = jnp.broadcast_to(k[:, None, :], (8, 8, 128)).reshape(64, 128)
                values.append(jnp.broadcast_to(v[:, None, :], (8, 8, 128)).reshape(64, 128))
                news.append(jnp.sum(rows * k, axis=1, keepdims=True) * score_scale)
                largest = jnp.maximum(largest, news[-1])
            expo = jnp.exp(scores - largest)
            news = [jnp.exp(x - largest) for x in news]
            total = jnp.sum(expo, axis=1, keepdims=True)
            for x in news:
                total = total + x
            share = 1.0 / total
            weights = (expo * share).astype(bf16)
            result = jnp.concatenate(
                [mm(weights[8 * g:8 * g + 8], VALS[i, g])
                 for g in range(KV_HEADS)], axis=0)
            for x, v in zip(news, values):
                result = result + (x * share).astype(bf16).astype(f32) * v
            AF[pl.ds(i, 64, stride=4), :] = result

        for i in range(4):
            attend(i)
        AM[s] = AF[...].astype(bf16).reshape(8, 32, 128)
        loop(1, T, lambda k: tensor_copy(
            AM.at[s, lax.rem(me + k, T) // 2], AR.at[s, me], asem.at[s, 0], asem.at[s, 1],
            lax.rem(me + k, T)).start())
        AR[s, me] = AM[s, chip]
        if s == 0:
            wait(AOR.at[pl.ds(0, T - 1)], aosem.at[1])
            blocks = AOR[...].astype(f32).reshape(T, 4, 8, 128)
            for b in range(4):
                XF[128 * b:128 * b + 128, :] = blocks[:, b].reshape(128, 128)
            spread_pairs(XF[0:512, :], AOE)
            AO[...] = AOE[...].astype(bf16)
        wait(AR.at[s, pl.ds(0, T - 1)], asem.at[s, 1])
        XF[0:512, :] = AR[s].astype(f32).reshape(512, 128)
        for h in range(8):
            for i in range(4):
                AT[16 * i:16 * i + 16, 128 * h:128 * h + 128] = (
                    XF[pl.ds(4 * h + i, 16, stride=32), :].astype(bf16))

        attended = AT[...]
        if s == 0:
            wait(WO.at[:, pl.ds(0, CHUNK), :], lsem.at[18])
            wait(WO.at[:, pl.ds(0, CHUNK), :], wosem.at[1])

        def part(k):
            q = lax.rem(chip + k, 8)
            RSS[s, q] = mm(AT[...], WO[q]).astype(bf16)
            tensor_copy(
                RSS.at[s, q], RB.at[s, chip], rssem.at[s, 0], rssem.at[s, 1],
                2 * q + core).start()
        loop(1, 8, part)
        t = mm(attended, AO[...])
        TOS[s] = pack_rank(t).astype(bf16)
        loop(1, 8, lambda k: tensor_copy(
            TOS.at[s], TOR.at[s, chip], tosem.at[s, 0], tosem.at[s, 1],
            lax.rem(me + 2 * k, T)).start())
        TOR[s, chip] = TOS[s]
        RB[s, chip] = jnp.zeros((64, CHUNK), bf16)
        y = mm(attended, WO[chip])
        y = y + ST[s, me].astype(f32)
        wait(TOR.at[s, pl.ds(0, 7)], tosem.at[s, 1])
        rank = jnp.sum(TOR[s].astype(f32), axis=0)
        y = y + low_rank_scale * mm(unpack_split(rank), BO[...])
        wait(RB.at[s, pl.ds(0, 7)], rssem.at[s, 1])
        for q in range(8):
            y = y + RB[s, q].astype(f32)
        y = y.astype(bf16)

        if s + 1 < STEPS:
            ST[1, me] = y
            squares = y.astype(f32) * y.astype(f32)
            squares = (squares[:, 0:128] + squares[:, 128:256]) + (
                squares[:, 256:384] + squares[:, 384:512])
            SQS[...] = jnp.zeros_like(SQS)
            SQS[0:1, 0:64] = jnp.sum(squares.T, axis=0, keepdims=True)
            loop(1, T, lambda k: tensor_copy(
                SQS, SQR.at[me], sqsem.at[0], sqsem.at[1], lax.rem(me + k, T)).start())
            loop(1, 8, lambda k: tensor_copy(
                ST.at[1, me], ST.at[1, me], agdsem.at[0, k], agdsem.at[1, k],
                lax.rem(me + 2 * k, T)).start())
            tensor_copy(
                ST.at[1, me], ST.at[1, me], agfsem.at[0, 0], agfsem.at[1, 0], sib).start()
        yf = y.astype(f32)
        for c in range(4):
            for i in range(4):
                OUTF[c, pl.ds(i, 16, stride=4), :] = yf[16 * i:16 * i + 16, 128 * c:128 * c + 128]
        for c in range(4):
            out[s, :, 128 * c:128 * c + 128] = OUTF[c].astype(bf16)

        if s + 1 < STEPS:
            SQR[me] = SQS[...]
            wait(SQR.at[pl.ds(0, T - 1)], sqsem.at[1])
            total = jnp.sum(SQR[...], axis=0)[0:1]
            total = jnp.broadcast_to(total, (128, 128)).T[0:64, 0:1]
            inv = lax.rsqrt(total * (1.0 / D) + norm_epsilon)

            def take(j, carry):
                q, new = carry
                NB[j] = (ST[1, j].astype(f32) * inv * gain[j]).astype(bf16)
                return project(j, q), project_kv(j, new)

            def pass_on_stream(k):
                j = own_side(k)
                wait(ST.at[1, j], agdsem.at[1, k])
                tensor_copy(
                    ST.at[1, j], ST.at[1, j], agfsem.at[0, k], agfsem.at[1, k], sib).start()

            loop(1, 8, pass_on_stream)
            carry = lax.fori_loop(
                0, 8, lambda k, c: take(own_side(k), c), (zero_query, zero_total), unroll=4)
            loop(0, 8, lambda k: wait(ST.at[1, other_side(k)], agfsem.at[1, k]))
            q, new = lax.fori_loop(
                0, 8, lambda k, c: take(other_side(k), c), carry, unroll=4)

    wait(A1R.at[pl.ds(0, 3)], a1sem.at[0, 0])
    wait(A1R.at[pl.ds(0, 4)], a1sem.at[0, 1])
    wait(WO.at[:, pl.ds(0, CHUNK), :], wosem.at[0])
    for half in range(2):
        wait(A2R.at[0, pl.ds(0, T - 1)], a2sem.at[half, 0])
    loop(1, 8, lambda k: wait(AQ.at[me], a3dsem.at[0, k]))
    loop(0, 8, lambda k: wait(AQ.at[me], a3fsem.at[0, k]))
    wait(AOR.at[pl.ds(0, T - 1)], aosem.at[0])
    for s in range(STEPS):
        wait(QR.at[s, pl.ds(0, T - 1)], qsem.at[s, 0])
        wait(AR.at[s, pl.ds(0, T - 1)], asem.at[s, 0])
        wait(TOR.at[s, pl.ds(0, 7)], tosem.at[s, 0])
        wait(RB.at[s, pl.ds(0, 7)], rssem.at[s, 0])
    loop(1, 8, lambda k: wait(ST.at[1, me], agdsem.at[0, k]))
    loop(0, 8, lambda k: wait(ST.at[1, me], agfsem.at[0, k]))
    wait(SQR.at[pl.ds(0, T - 1)], sqsem.at[0])


def body(
    hidden_in,
    norm_gain,
    query_weight_base,
    w_key,
    w_value,
    output_weight_base,
    kv_cache,
    cache_lengths,
    adapter_shards,
    shard_order,
):
    half_dim = HEAD_DIM // 2
    exponent = np.arange(half_dim, dtype=np.float32) * np.float32(2.0 / HEAD_DIM)
    frequency = np.float32(rope_theta) ** (-exponent)
    freq = jnp.asarray(np.concatenate([frequency, frequency]).reshape(1, HEAD_DIM))
    vmem = pl.BlockSpec(memory_space=pltpu.VMEM)
    smem = pl.BlockSpec(memory_space=pltpu.SMEM)
    hbm = pl.BlockSpec(memory_space=pl.ANY)
    V = pltpu.VMEM
    dma = pltpu.SemaphoreType.DMA
    return pl.pallas_call(
        kernel,
        out_shape=jax.ShapeDtypeStruct((STEPS, 64, CHUNK), bf16),
        in_specs=[vmem, vmem, hbm, hbm, hbm, hbm, hbm, smem, vmem, vmem, vmem],
        out_specs=vmem,
        scratch_shapes=[
            V((32, 256, CHUNK), bf16),
            V((128, D), bf16),
            V((8, 2 * CHUNK, CHUNK), bf16),
            V((4, KV_HEADS, CAP, 2, HEAD_DIM), bf16),
            V((4, 64, 128), f32),
            V((2, T, 64, CHUNK), bf16),
            V((T, 64, CHUNK), bf16),
            V((128, 128), f32),
            V((128, 128), bf16),
            V((R, 128, 128), bf16),
            V((2, T, 32, 128), bf16),
            V((2, T, 32, 128), bf16),
            V((1024, 128), f32),
            V((T, 32, 128), f32),
            V((512, 128), f32),
            V((T, 256, 128), bf16),
            V((2, 128, CHUNK), bf16),
            V((128, CHUNK), bf16),
            V((8, 32, 128), bf16),
            V((T, 32, 128), bf16),
            V((1024, 128), f32),
            V((1024, 128), bf16),
            V((512, 128), f32),
            V((STEPS, T, 32, 128), bf16),
            V((STEPS, T, 32, 128), bf16),
            V((256, 128), f32),
            V((STEPS, 64, 128), f32),
            V((STEPS, 64, 128), f32),
            V((256, 128), f32),
            V((STEPS, 8, 32, 128), bf16),
            V((STEPS, T, 32, 128), bf16),
            V((64, 2 * CHUNK), bf16),
            V((STEPS, 32, 128), bf16),
            V((STEPS, 8, 32, 128), bf16),
            V((STEPS, 8, 64, CHUNK), bf16),
            V((STEPS, 8, 64, CHUNK), bf16),
            V((4, 64, 128), f32),
            V((8, 128), f32),
            V((T, 8, 128), f32),
            V((2 * CAP, HEAD_DIM), f32),
            V((4, KV_HEADS, CAP, HEAD_DIM), bf16),
            V((4, KV_HEADS, CAP, HEAD_DIM), bf16),
            dma((20,)),
            dma((2,)),
            dma((2, 2)),
            dma((2, 2)),
            dma((2, 8)),
            dma((2, 8)),
            dma((2,)),
            dma((STEPS, 2)),
            dma((STEPS, 2)),
            dma((STEPS, 2)),
            dma((STEPS, 2)),
            dma((2, 8)),
            dma((2, 8)),
            dma((2,)),
        ],
        compiler_params=pltpu.CompilerParams(
            collective_id=0, has_side_effects=True, vmem_limit_bytes=56 * 2**20
        ),
        cost_estimate=pl.CostEstimate(
            flops=5 * 10**9, bytes_accessed=25 * 2**20, transcendentals=10**6
        ),
    )(
        hidden_in,
        norm_gain.reshape(T, 1, CHUNK),
        query_weight_base.reshape(32, 256, CHUNK),
        w_key.T,
        w_value.T,
        output_weight_base,
        kv_cache,
        cache_lengths,
        freq,
        adapter_shards,
        shard_order.reshape(1, 128),
    )


def solution(mesh):
    return jax.shard_map(
        body,
        mesh=mesh,
        in_specs=(
            P("rollout", None),
            P(),
            P(None, "tensor"),
            P(None, "tensor"),
            P(None, "tensor"),
            P("tensor", None),
            P(("rollout", "tensor"), None, None, None),
            P(("rollout", "tensor")),
            P(("rollout", "tensor"), None),
            P(),
        ),
        out_specs=P(None, "rollout", "tensor"),
        check_vma=False,
    )
```

```python
import jax
import jax.numpy as jnp
import numpy as np
from jax import lax
from jax.experimental import pallas as pl
from jax.experimental.pallas import tpu as pltpu
from jax.sharding import PartitionSpec as P

D = 8192
HEADS = 64
KV_HEADS = 8
HEAD_DIM = 128
RANK = 64
STEPS = 2
CAP = 256
T = 16
R = 8
CHUNK = D // T

low_rank_scale = 2.0
norm_epsilon = 1e-05
rope_theta = 500000.0
score_scale = 1.0 / np.sqrt(np.float32(HEAD_DIM))

f32 = jnp.float32
bf16 = jnp.bfloat16
MESH = pl.DeviceIdType.MESH


def mm(a, b):
    return jnp.dot(a, b, preferred_element_type=f32)


def mm_t(a, b):
    return lax.dot_general(a, b, (((1,), (1,)), ((), ())), preferred_element_type=f32)


def lanes(shape):
    return lax.broadcasted_iota(jnp.int32, shape, len(shape) - 1)


def swap_halves(x):
    return pltpu.roll(x, 64, len(x.shape) - 1)


def spread_pairs(x, ref):
    low = lanes(x.shape) < 64
    rows = x.shape[0]
    ref[pl.ds(0, rows, stride=2), :] = jnp.where(low, x, 0.0)
    ref[pl.ds(1, rows, stride=2), :] = jnp.where(low, swap_halves(x), 0.0)


def pack_rank(t):
    return t[0:32] + swap_halves(t[32:64])


def unpack_split(total):
    high = total.astype(bf16).astype(f32)
    rest = total - high
    low = lanes(total.shape) < 64
    top = jnp.where(low, high, swap_halves(rest))
    bottom = jnp.where(low, swap_halves(high), rest)
    return jnp.concatenate([top, bottom], axis=0).astype(bf16)


def kernel(
    hid, gain, wq, wk_t, wv_t, wo, kv, lens, freq, piece, order,
    out,
    WQ, WKV, WO, KV, HF, ST, SG, NB,
    PF, CP, A1R, A2S, A2R, XF, OF, AE, AQ, BQ, BO, AOS, AOR, AOE, AO,
    Q32, QS, QR, QX, KN, VN, AF, AM, AR, AT, TOS, TOR, RSS, RB, OUTF, SQS, SQR, DI, KEYS, VALS,
    lsem, wosem, a1sem, a2sem, a3dsem, a3fsem, aosem, qsem, asem, tosem, rssem, agdsem, agfsem, sqsem,
):
    me = lax.axis_index("tensor")
    ro = lax.axis_index("rollout")
    core = lax.rem(me, 2)
    chip = me // 2
    sib = me + 1 - 2 * core

    def wait(ref, sem):
        pltpu.make_async_copy(ref, ref, sem).wait()

    def tensor_copy(src, dst, send, recv, peer):
        return pltpu.make_async_remote_copy(
            src_ref=src, dst_ref=dst, send_sem=send, recv_sem=recv,
            device_id={"tensor": peer}, device_id_type=MESH,
        )

    def loop(lo, hi, body):
        def step(k, carry):
            body(k)
            return carry
        lax.fori_loop(lo, hi, step, 0)

    barrier = pltpu.get_barrier_semaphore()
    loop(1, T, lambda k: pl.semaphore_signal(
        barrier, inc=1, device_id={"tensor": lax.rem(me + k, T)}, device_id_type=MESH))
    loop(1, R, lambda k: pl.semaphore_signal(
        barrier, inc=1, device_id={"rollout": lax.rem(ro + k, R)}, device_id_type=MESH))

    for j in range(8):
        pltpu.make_async_copy(
            wq.at[pl.ds(4 * j, 4)], WQ.at[pl.ds(4 * j, 4)], lsem.at[0]).start()
    pltpu.make_async_copy(wk_t, WKV.at[pl.ds(0, 64), :], lsem.at[16]).start()
    pltpu.make_async_copy(wv_t, WKV.at[pl.ds(64, 64), :], lsem.at[17]).start()
    for i in range(4):
        for g in range(KV_HEADS):
            pltpu.make_async_copy(
                kv.at[i, :, :, pl.ds(HEAD_DIM * g, HEAD_DIM)], KV.at[i, g], lsem.at[19]).start()

    def wo_columns(q, parity):
        return wo.at[:, pl.ds(pl.multiple_of((2 * q + parity) * CHUNK, CHUNK), CHUNK)]

    wo_rows = pl.ds(pl.multiple_of(core * CHUNK, CHUNK), CHUNK)
    loop(0, 8, lambda q: pltpu.make_async_copy(
        wo_columns(q, core), WO.at[q, wo_rows, :], lsem.at[18]).start())

    order_row = order[...]
    mine = jnp.sum(
        jnp.where(lanes((1, 128)) == ro * T + me, order_row, 0), axis=1, keepdims=True)
    is_up = jnp.broadcast_to((mine >> 5) & 1, (128, 128))
    row = lax.broadcasted_iota(jnp.int32, (128, 128), 0)
    up_row = 64 * ((row >> 2) & 1) + 4 * (row >> 3) + (row & 3)
    wanted = jnp.where(is_up == 1, up_row, row)
    pick = jnp.where(lanes((128, 128)) == wanted, 1.0, 0.0).astype(bf16)
    flat = piece[...].astype(f32)
    for r in range(128):
        PF[r:r + 1, :] = flat[:, 128 * r:128 * r + 128]
    CP[...] = mm(pick, PF[...].astype(bf16)).astype(bf16)
    A1R[ro] = CP[...]
    place = jnp.where(row == jnp.broadcast_to(order_row, (128, 128)), 1.0, 0.0).astype(bf16)

    pl.semaphore_wait(barrier, T - 1 + R - 1)

    def send_piece(peer, sem):
        pltpu.make_async_remote_copy(
            src_ref=CP, dst_ref=A1R.at[ro], send_sem=a1sem.at[0, sem],
            recv_sem=a1sem.at[1, sem], device_id={"rollout": peer}, device_id_type=MESH).start()

    loop(1, 4, lambda k: send_piece(lax.rem(ro + 2 * k, R), 0))
    other = ro + 1 - 2 * lax.rem(ro, 2)
    loop(0, 4, lambda k: send_piece(lax.rem(other + 2 * k, R), 1))
    loop(0, 8, lambda q: tensor_copy(
        wo_columns(q, 1 - core), WO.at[q, wo_rows, :], wosem.at[0], wosem.at[1], sib).start())

    def permute_hidden(j):
        for c in range(4):
            at = pl.multiple_of(CHUNK * j + 128 * c, 128)
            HF[c] = hid[:, pl.ds(at, 128)].astype(f32)
        for c in range(4):
            for i in range(4):
                ST[j, 16 * i:16 * i + 16, 128 * c:128 * c + 128] = (
                    HF[c, pl.ds(i, 16, stride=4), :].astype(bf16))
    loop(0, T, permute_hidden)

    Q32[320:512, :] = jnp.zeros((192, 128), f32)

    def square_sum(j, total):
        x = ST[j].astype(f32)
        x = x * x
        return total + (x[:, 0:128] + x[:, 128:256]) + (x[:, 256:384] + x[:, 384:512])

    def normalize(total):
        inv = lax.rsqrt(jnp.sum(total, axis=1, keepdims=True) * (1.0 / D) + norm_epsilon)
        def body(j):
            NB[j] = (ST[j].astype(f32) * inv * gain[j]).astype(bf16)
        loop(0, T, body)

    zero_total = jnp.zeros((64, 128), f32)
    zero_query = jnp.zeros((64, CHUNK), f32)
    normalize(lax.fori_loop(0, T, square_sum, zero_total))

    def project_kv(j, new):
        columns = pl.ds(pl.multiple_of(CHUNK * j, CHUNK), CHUNK)
        return new + mm_t(NB[j], WKV[:, columns])

    for half in range(2):
        z = lax.rem(ro + half, 2)
        wait(A1R.at[pl.ds(0, 3 + half)], a1sem.at[1, half])
        for y in range(4):
            held = A1R[2 * y + z].astype(f32).reshape(T, 8, 128)
            OF[:, 8 * y:8 * y + 8, :] = held
        A2S[half] = OF[...].astype(bf16)
        loop(1, T, lambda k: tensor_copy(
            A2S.at[half, lax.rem(me + k, T)], A2R.at[z, me], a2sem.at[half, 0],
            a2sem.at[half, 1], lax.rem(me + k, T)).start())
        A2R[z, me] = A2S[half, me]

    wait(WKV.at[pl.ds(0, 64), :], lsem.at[16])
    wait(WKV.at[pl.ds(64, 64), :], lsem.at[17])
    new = lax.fori_loop(0, T, project_kv, zero_total, unroll=4)
    wait(WQ, lsem.at[0])
    for half in range(2):
        wait(A2R.at[0, pl.ds(0, T - 1)], a2sem.at[half, 1])

    for z in range(2):
        arrived = A2R[z].astype(f32).reshape(T, 4, 8, 128)
        for y in range(4):
            r = 2 * y + z
            XF[128 * r:128 * r + 128, :] = arrived[:, y].reshape(128, 128)
    FL = AOE
    for s in range(8):
        FL[pl.ds(s, 128, stride=8), :] = mm(place, XF[pl.ds(s, 128, stride=8), :].astype(bf16))
    spread_pairs(FL[0:256, :], AE)
    AQ[me] = (AE[0:256, :] + swap_halves(AE[256:512, :])).astype(bf16)
    loop(1, 8, lambda k: tensor_copy(
        AQ.at[me], AQ.at[me], a3dsem.at[0, k], a3dsem.at[1, k], lax.rem(me + 2 * k, T)).start())
    tensor_copy(AQ.at[me], AQ.at[me], a3fsem.at[0, 0], a3fsem.at[1, 0], sib).start()
    for c in range(4):
        up = (low_rank_scale * FL[pl.ds(256 + c, 64, stride=4), :]).astype(bf16)
        none = jnp.zeros_like(up)
        BQ[0, 0:64, 128 * c:128 * c + 128] = up
        BQ[0, 64:128, 128 * c:128 * c + 128] = none
        BQ[1, 0:64, 128 * c:128 * c + 128] = none
        BQ[1, 64:128, 128 * c:128 * c + 128] = up
        up = FL[pl.ds(768 + c, 64, stride=4), :].astype(bf16)
        BO[0:64, 128 * c:128 * c + 128] = up
        BO[64:128, 128 * c:128 * c + 128] = up
    AOS[...] = FL[512:768, :].astype(bf16).reshape(8, 32, 128)

    def merge(j):
        strip = pl.ds(pl.multiple_of(16 * j, 16), 16)
        for half in range(2):
            blocks = pl.ds(16 * half, 16)
            for n in range(2):
                columns = slice(256 * n, 256 * n + 256)
                change = mm(AQ[j], BQ[half, :, columns]).reshape(16, 16, 256)
                WQ[blocks, strip, columns] = (
                    WQ[blocks, strip, columns].astype(f32) + change).astype(bf16)

    def own_side(k):
        return lax.rem(me + T - 2 * k, T)

    def other_side(k):
        return lax.rem(sib + T - 2 * k, T)

    def pass_on_strips(k):
        j = own_side(k)
        wait(AQ.at[j], a3dsem.at[1, k])
        tensor_copy(AQ.at[j], AQ.at[j], a3fsem.at[0, k], a3fsem.at[1, k], sib).start()

    wait(KV, lsem.at[19])

    def part_cache(n):
        i, g = n // KV_HEADS, lax.rem(n, KV_HEADS)
        DI[...] = KV[i, g].reshape(2 * CAP, HEAD_DIM).astype(f32)
        KEYS[i, g] = DI[pl.ds(0, CAP, stride=2), :].astype(bf16)
        VALS[i, g] = DI[pl.ds(1, CAP, stride=2), :].astype(bf16)

    merge(me)
    loop(0, 4 * KV_HEADS, part_cache)
    loop(1, 8, pass_on_strips)
    loop(1, 8, lambda k: merge(own_side(k)))
    loop(0, 8, lambda k: wait(AQ.at[other_side(k)], a3fsem.at[1, k]))
    loop(0, 8, lambda k: merge(other_side(k)))

    low_half = lanes((8, 128)) < 64
    sub = lax.broadcasted_iota(jnp.int32, (8, 128), 0) & 3
    lengths = jnp.zeros((8, 128), jnp.int32)
    for i in range(4):
        lengths = jnp.where(sub == i, lens[i], lengths)
    wide = lanes((64, CAP))

    for s in range(STEPS):
        def project(j, q):
            return q + mm(NB[j], WQ[pl.ds(2 * j, 2)].reshape(CHUNK, CHUNK))

        if s == 0:
            q = lax.fori_loop(0, T, project, zero_query, unroll=4)
        for h in range(4):
            Q32[64 * h:64 * h + 64, :] = q[:, 128 * h:128 * h + 128]
        Q32[256:320, :] = new
        for t in range(T):
            QS[s, t] = Q32[pl.ds(t, 32, stride=16), :].astype(bf16)
        loop(1, T, lambda k: tensor_copy(
            QS.at[s, lax.rem(me + k, T)], QR.at[s, me], qsem.at[s, 0], qsem.at[s, 1],
            lax.rem(me + k, T)).start())
        QR[s, me] = QS[s, me]
        if s == 0:
            loop(1, T, lambda k: tensor_copy(
                AOS.at[lax.rem(me + k, T) // 2], AOR.at[me], aosem.at[0], aosem.at[1],
                lax.rem(me + k, T)).start())
            AOR[me] = AOS[chip]

        angles = (lengths + s).astype(f32) * freq[...]
        cosine = jnp.cos(angles)
        sine = jnp.where(low_half, -jnp.sin(angles), jnp.sin(angles))

        wait(QR.at[s, pl.ds(0, T - 1)], qsem.at[s, 1])
        got = QR[s].astype(f32)
        heads = got[:, 0:16].reshape(T, 2, 8, 128)
        heads = heads * cosine + swap_halves(heads) * sine
        QX[...] = heads.astype(bf16).astype(f32).reshape(256, 128)
        fresh = got[:, 16:24].reshape(8, 2, 8, 128)
        even, odd = fresh[:, 0], fresh[:, 1]
        low = lanes(even.shape) < 64
        key = jnp.where(low, even, swap_halves(odd))
        key = key * cosine + swap_halves(key) * sine
        KN[s] = key.astype(bf16).astype(f32).reshape(64, 128)
        VN[s] = jnp.where(low, swap_halves(even), odd).reshape(64, 128)


        def attend(i):
            queries = [QX[pl.ds(32 * g + i, 8, stride=4), :] for g in range(KV_HEADS)]
            scores = jnp.concatenate(
                [mm_t(queries[g].astype(bf16), KEYS[i, g])
                 for g in range(KV_HEADS)], axis=0) * score_scale
            scores = jnp.where(wide < lens[i], scores, -1e30)
            rows = jnp.concatenate(queries, axis=0)
            largest = jnp.max(scores, axis=1, keepdims=True)
            news, values = [], []
            for n in range(s + 1):
                k = KN[n, pl.ds(i, 8, stride=8), :]
                v = VN[n, pl.ds(i, 8, stride=8), :]
                k = jnp.broadcast_to(k[:, None, :], (8, 8, 128)).reshape(64, 128)
                values.append(jnp.broadcast_to(v[:, None, :], (8, 8, 128)).reshape(64, 128))
                news.append(jnp.sum(rows * k, axis=1, keepdims=True) * score_scale)
                largest = jnp.maximum(largest, news[-1])
            expo = jnp.exp(scores - largest)
            news = [jnp.exp(x - largest) for x in news]
            total = jnp.sum(expo, axis=1, keepdims=True)
            for x in news:
                total = total + x
            share = 1.0 / total
            weights = (expo * share).astype(bf16)
            result = jnp.concatenate(
                [mm(weights[8 * g:8 * g + 8], VALS[i, g])
                 for g in range(KV_HEADS)], axis=0)
            for x, v in zip(news, values):
                result = result + (x * share).astype(bf16).astype(f32) * v
            AF[pl.ds(i, 64, stride=4), :] = result

        for i in range(4):
            attend(i)
        AM[s] = AF[...].astype(bf16).reshape(8, 32, 128)
        loop(1, T, lambda k: tensor_copy(
            AM.at[s, lax.rem(me + k, T) // 2], AR.at[s, me], asem.at[s, 0], asem.at[s, 1],
            lax.rem(me + k, T)).start())
        AR[s, me] = AM[s, chip]
        if s == 0:
            wait(AOR.at[pl.ds(0, T - 1)], aosem.at[1])
            blocks = AOR[...].astype(f32).reshape(T, 4, 8, 128)
            for b in range(4):
                XF[128 * b:128 * b + 128, :] = blocks[:, b].reshape(128, 128)
            spread_pairs(XF[0:512, :], AOE)
            AO[...] = AOE[...].astype(bf16)
        wait(AR.at[s, pl.ds(0, T - 1)], asem.at[s, 1])
        XF[0:512, :] = AR[s].astype(f32).reshape(512, 128)
        for h in range(8):
            for i in range(4):
                AT[16 * i:16 * i + 16, 128 * h:128 * h + 128] = (
                    XF[pl.ds(4 * h + i, 16, stride=32), :].astype(bf16))

        attended = AT[...]
        if s == 0:
            wait(WO.at[:, pl.ds(0, CHUNK), :], lsem.at[18])
            wait(WO.at[:, pl.ds(0, CHUNK), :], wosem.at[1])

        halves = [slice(256 * half, 256 * half + 256) for half in range(2)]

        def send_parts(half):
            def part(k):
                q = lax.rem(chip + k, 8)
                RSS[s, half, q] = mm(AT[...], WO[q, :, halves[half]]).astype(bf16)
                tensor_copy(
                    RSS.at[s, half, q], RB.at[s, half, chip], rssem.at[s, half, 0],
                    rssem.at[s, half, 1], 2 * q + core).start()
            loop(1, 8, part)

        send_parts(0)
        t = mm(attended, AO[...])
        TOS[s] = pack_rank(t).astype(bf16)
        loop(1, 8, lambda k: tensor_copy(
            TOS.at[s], TOR.at[s, chip], tosem.at[s, 0], tosem.at[s, 1],
            lax.rem(me + 2 * k, T)).start())
        TOR[s, chip] = TOS[s]
        send_parts(1)
        bases = []
        for half in range(2):
            own = ST[me, :, halves[half]] if s == 0 else SG[me, half]
            bases.append(mm(attended, WO[chip, :, halves[half]]) + own.astype(f32))
        wait(TOR.at[s, pl.ds(0, 7)], tosem.at[s, 1])
        rank = unpack_split(jnp.sum(TOR[s].astype(f32), axis=0))
        parts = []
        for half in range(2):
            y = bases[half] + low_rank_scale * mm(rank, BO[:, halves[half]])
            RB[s, half, chip] = jnp.zeros((64, CHUNK // 2), bf16)
            wait(RB.at[s, half, pl.ds(0, 7)], rssem.at[s, half, 1])
            for q in range(8):
                y = y + RB[s, half, q].astype(f32)
            y = y.astype(bf16)
            parts.append(y)
            if s + 1 < STEPS:
                SG[me, half] = y
                if half == 1:
                    squares = [x.astype(f32) * x.astype(f32) for x in parts]
                    squares = (squares[0][:, 0:128] + squares[0][:, 128:256]) + (
                        squares[1][:, 0:128] + squares[1][:, 128:256])
                    SQS[...] = jnp.zeros_like(SQS)
                    SQS[0:1, 0:64] = jnp.sum(squares.T, axis=0, keepdims=True)
                    loop(1, T, lambda k: tensor_copy(
                        SQS, SQR.at[me], sqsem.at[0], sqsem.at[1], lax.rem(me + k, T)).start())
                loop(1, 8, lambda k: tensor_copy(
                    SG.at[me, half], SG.at[me, half], agdsem.at[0, half, k],
                    agdsem.at[1, half, k], lax.rem(me + 2 * k, T)).start())
        if s + 1 < STEPS:
            tensor_copy(SG.at[me], SG.at[me], agfsem.at[0, 0], agfsem.at[1, 0], sib).start()
        y = jnp.concatenate(parts, axis=1)
        yf = y.astype(f32)
        for c in range(4):
            for i in range(4):
                OUTF[c, pl.ds(i, 16, stride=4), :] = yf[16 * i:16 * i + 16, 128 * c:128 * c + 128]
        for c in range(4):
            out[s, :, 128 * c:128 * c + 128] = OUTF[c].astype(bf16)

        if s + 1 < STEPS:
            SQR[me] = SQS[...]
            wait(SQR.at[pl.ds(0, T - 1)], sqsem.at[1])
            total = jnp.sum(SQR[...], axis=0)[0:1]
            total = jnp.broadcast_to(total, (128, 128)).T[0:64, 0:1]
            inv = lax.rsqrt(total * (1.0 / D) + norm_epsilon)

            def take(j, carry):
                q, new = carry
                x = jnp.concatenate([SG[j, 0], SG[j, 1]], axis=1).astype(f32)
                NB[j] = (x * inv * gain[j]).astype(bf16)
                return project(j, q), project_kv(j, new)

            def pass_on_stream(k):
                j = own_side(k)
                for half in range(2):
                    wait(SG.at[j, half], agdsem.at[1, half, k])
                tensor_copy(
                    SG.at[j], SG.at[j], agfsem.at[0, k], agfsem.at[1, k], sib).start()

            loop(1, 8, pass_on_stream)
            carry = lax.fori_loop(
                0, 8, lambda k, c: take(own_side(k), c), (zero_query, zero_total), unroll=4)
            loop(0, 8, lambda k: wait(SG.at[other_side(k)], agfsem.at[1, k]))
            q, new = lax.fori_loop(
                0, 8, lambda k, c: take(other_side(k), c), carry, unroll=4)

    wait(A1R.at[pl.ds(0, 3)], a1sem.at[0, 0])
    wait(A1R.at[pl.ds(0, 4)], a1sem.at[0, 1])
    wait(WO.at[:, pl.ds(0, CHUNK), :], wosem.at[0])
    for half in range(2):
        wait(A2R.at[0, pl.ds(0, T - 1)], a2sem.at[half, 0])
    loop(1, 8, lambda k: wait(AQ.at[me], a3dsem.at[0, k]))
    loop(0, 8, lambda k: wait(AQ.at[me], a3fsem.at[0, k]))
    wait(AOR.at[pl.ds(0, T - 1)], aosem.at[0])
    for s in range(STEPS):
        wait(QR.at[s, pl.ds(0, T - 1)], qsem.at[s, 0])
        wait(AR.at[s, pl.ds(0, T - 1)], asem.at[s, 0])
        wait(TOR.at[s, pl.ds(0, 7)], tosem.at[s, 0])
        for half in range(2):
            wait(RB.at[s, half, pl.ds(0, 7)], rssem.at[s, half, 0])
    for half in range(2):
        loop(1, 8, lambda k: wait(SG.at[me, half], agdsem.at[0, half, k]))
    loop(0, 8, lambda k: wait(SG.at[me], agfsem.at[0, k]))
    wait(SQR.at[pl.ds(0, T - 1)], sqsem.at[0])


def body(
    hidden_in,
    norm_gain,
    query_weight_base,
    w_key,
    w_value,
    output_weight_base,
    kv_cache,
    cache_lengths,
    adapter_shards,
    shard_order,
):
    half_dim = HEAD_DIM // 2
    exponent = np.arange(half_dim, dtype=np.float32) * np.float32(2.0 / HEAD_DIM)
    frequency = np.float32(rope_theta) ** (-exponent)
    freq = jnp.asarray(np.concatenate([frequency, frequency]).reshape(1, HEAD_DIM))
    vmem = pl.BlockSpec(memory_space=pltpu.VMEM)
    smem = pl.BlockSpec(memory_space=pltpu.SMEM)
    hbm = pl.BlockSpec(memory_space=pl.ANY)
    V = pltpu.VMEM
    dma = pltpu.SemaphoreType.DMA
    return pl.pallas_call(
        kernel,
        out_shape=jax.ShapeDtypeStruct((STEPS, 64, CHUNK), bf16),
        in_specs=[vmem, vmem, hbm, hbm, hbm, hbm, hbm, smem, vmem, vmem, vmem],
        out_specs=vmem,
        scratch_shapes=[
            V((32, 256, CHUNK), bf16),
            V((128, D), bf16),
            V((8, 2 * CHUNK, CHUNK), bf16),
            V((4, KV_HEADS, CAP, 2, HEAD_DIM), bf16),
            V((4, 64, 128), f32),
            V((T, 64, CHUNK), bf16),
            V((T, 2, 64, CHUNK // 2), bf16),
            V((T, 64, CHUNK), bf16),
            V((128, 128), f32),
            V((128, 128), bf16),
            V((R, 128, 128), bf16),
            V((2, T, 32, 128), bf16),
            V((2, T, 32, 128), bf16),
            V((1024, 128), f32),
            V((T, 32, 128), f32),
            V((512, 128), f32),
            V((T, 256, 128), bf16),
            V((2, 128, CHUNK), bf16),
            V((128, CHUNK), bf16),
            V((8, 32, 128), bf16),
            V((T, 32, 128), bf16),
            V((1024, 128), f32),
            V((1024, 128), bf16),
            V((512, 128), f32),
            V((STEPS, T, 32, 128), bf16),
            V((STEPS, T, 32, 128), bf16),
            V((256, 128), f32),
            V((STEPS, 64, 128), f32),
            V((STEPS, 64, 128), f32),
            V((256, 128), f32),
            V((STEPS, 8, 32, 128), bf16),
            V((STEPS, T, 32, 128), bf16),
            V((64, 2 * CHUNK), bf16),
            V((STEPS, 32, 128), bf16),
            V((STEPS, 8, 32, 128), bf16),
            V((STEPS, 2, 8, 64, CHUNK // 2), bf16),
            V((STEPS, 2, 8, 64, CHUNK // 2), bf16),
            V((4, 64, 128), f32),
            V((8, 128), f32),
            V((T, 8, 128), f32),
            V((2 * CAP, HEAD_DIM), f32),
            V((4, KV_HEADS, CAP, HEAD_DIM), bf16),
            V((4, KV_HEADS, CAP, HEAD_DIM), bf16),
            dma((20,)),
            dma((2,)),
            dma((2, 2)),
            dma((2, 2)),
            dma((2, 8)),
            dma((2, 8)),
            dma((2,)),
            dma((STEPS, 2)),
            dma((STEPS, 2)),
            dma((STEPS, 2)),
            dma((STEPS, 2, 2)),
            dma((2, 2, 8)),
            dma((2, 8)),
            dma((2,)),
        ],
        compiler_params=pltpu.CompilerParams(
            collective_id=0, has_side_effects=True, vmem_limit_bytes=56 * 2**20
        ),
        cost_estimate=pl.CostEstimate(
            flops=5 * 10**9, bytes_accessed=25 * 2**20, transcendentals=10**6
        ),
    )(
        hidden_in,
        norm_gain.reshape(T, 1, CHUNK),
        query_weight_base.reshape(32, 256, CHUNK),
        w_key.T,
        w_value.T,
        output_weight_base,
        kv_cache,
        cache_lengths,
        freq,
        adapter_shards,
        shard_order.reshape(1, 128),
    )


def solution(mesh):
    return jax.shard_map(
        body,
        mesh=mesh,
        in_specs=(
            P("rollout", None),
            P(),
            P(None, "tensor"),
            P(None, "tensor"),
            P(None, "tensor"),
            P("tensor", None),
            P(("rollout", "tensor"), None, None, None),
            P(("rollout", "tensor")),
            P(("rollout", "tensor"), None),
            P(),
        ),
        out_specs=P(None, "rollout", "tensor"),
        check_vma=False,
    )
```

```python
import jax
import jax.numpy as jnp
import numpy as np
from jax import lax
from jax.experimental import pallas as pl
from jax.experimental.pallas import tpu as pltpu
from jax.sharding import PartitionSpec as P

D = 8192
HEADS = 64
KV_HEADS = 8
HEAD_DIM = 128
RANK = 64
STEPS = 2
CAP = 256
T = 16
R = 8
CHUNK = D // T

low_rank_scale = 2.0
norm_epsilon = 1e-05
rope_theta = 500000.0
score_scale = 1.0 / np.sqrt(np.float32(HEAD_DIM))

f32 = jnp.float32
bf16 = jnp.bfloat16
MESH = pl.DeviceIdType.MESH


def mm(a, b):
    return jnp.dot(a, b, preferred_element_type=f32)


def mm_t(a, b):
    return lax.dot_general(a, b, (((1,), (1,)), ((), ())), preferred_element_type=f32)


def lanes(shape):
    return lax.broadcasted_iota(jnp.int32, shape, len(shape) - 1)


def swap_halves(x):
    return pltpu.roll(x, 64, len(x.shape) - 1)


def spread_pairs(x, ref):
    low = lanes(x.shape) < 64
    rows = x.shape[0]
    ref[pl.ds(0, rows, stride=2), :] = jnp.where(low, x, 0.0)
    ref[pl.ds(1, rows, stride=2), :] = jnp.where(low, swap_halves(x), 0.0)


def pack_rank(t):
    return t[0:32] + swap_halves(t[32:64])


def unpack_split(total):
    high = total.astype(bf16).astype(f32)
    rest = total - high
    low = lanes(total.shape) < 64
    top = jnp.where(low, high, swap_halves(rest))
    bottom = jnp.where(low, swap_halves(high), rest)
    return jnp.concatenate([top, bottom], axis=0).astype(bf16)


def kernel(
    hid, gain, wq, wk_t, wv_t, wo, kv, lens, freq, piece, order,
    out,
    WQ, WKV, WO, KV, HF, ST, SG, NB,
    PF, CP, A1R, A2S, A2R, XF, OF, AE, AQ, BQ, BO, AOS, AOR, AOE, AO,
    Q32, QS, QR, QX, KN, VN, AF, AM, AR, AT, TOS, TOR, RSS, RB, OUTF, SQS, SQR, DI, KEYS, VALS,
    lsem, wosem, a1sem, a2sem, a3dsem, a3fsem, aosem, qsem, asem, tosem, rssem, agdsem, agfsem, sqsem,
):
    me = lax.axis_index("tensor")
    ro = lax.axis_index("rollout")
    core = lax.rem(me, 2)
    chip = me // 2
    sib = me + 1 - 2 * core

    def wait(ref, sem):
        pltpu.make_async_copy(ref, ref, sem).wait()

    def tensor_copy(src, dst, send, recv, peer):
        return pltpu.make_async_remote_copy(
            src_ref=src, dst_ref=dst, send_sem=send, recv_sem=recv,
            device_id={"tensor": peer}, device_id_type=MESH,
        )

    def loop(lo, hi, body):
        def step(k, carry):
            body(k)
            return carry
        lax.fori_loop(lo, hi, step, 0)

    barrier = pltpu.get_barrier_semaphore()
    loop(1, T, lambda k: pl.semaphore_signal(
        barrier, inc=1, device_id={"tensor": lax.rem(me + k, T)}, device_id_type=MESH))
    loop(1, R, lambda k: pl.semaphore_signal(
        barrier, inc=1, device_id={"rollout": lax.rem(ro + k, R)}, device_id_type=MESH))

    for j in range(8):
        pltpu.make_async_copy(
            wq.at[pl.ds(4 * j, 4)], WQ.at[pl.ds(4 * j, 4)], lsem.at[0]).start()
    pltpu.make_async_copy(wk_t, WKV.at[pl.ds(0, 64), :], lsem.at[16]).start()
    pltpu.make_async_copy(wv_t, WKV.at[pl.ds(64, 64), :], lsem.at[17]).start()
    for i in range(4):
        for g in range(KV_HEADS):
            pltpu.make_async_copy(
                kv.at[i, :, :, pl.ds(HEAD_DIM * g, HEAD_DIM)], KV.at[i, g], lsem.at[19]).start()

    def wo_columns(q, parity):
        return wo.at[:, pl.ds(pl.multiple_of((2 * q + parity) * CHUNK, CHUNK), CHUNK)]

    wo_rows = pl.ds(pl.multiple_of(core * CHUNK, CHUNK), CHUNK)
    loop(0, 8, lambda q: pltpu.make_async_copy(
        wo_columns(q, core), WO.at[q, wo_rows, :], lsem.at[18]).start())

    order_row = order[...]
    mine = jnp.sum(
        jnp.where(lanes((1, 128)) == ro * T + me, order_row, 0), axis=1, keepdims=True)
    is_up = jnp.broadcast_to((mine >> 5) & 1, (128, 128))
    row = lax.broadcasted_iota(jnp.int32, (128, 128), 0)
    up_row = 64 * ((row >> 2) & 1) + 4 * (row >> 3) + (row & 3)
    wanted = jnp.where(is_up == 1, up_row, row)
    pick = jnp.where(lanes((128, 128)) == wanted, 1.0, 0.0).astype(bf16)
    flat = piece[...].astype(f32)
    for r in range(128):
        PF[r:r + 1, :] = flat[:, 128 * r:128 * r + 128]
    CP[...] = mm(pick, PF[...].astype(bf16)).astype(bf16)
    A1R[ro] = CP[...]
    place = jnp.where(row == jnp.broadcast_to(order_row, (128, 128)), 1.0, 0.0).astype(bf16)

    pl.semaphore_wait(barrier, T - 1 + R - 1)

    def send_piece(peer, sem):
        pltpu.make_async_remote_copy(
            src_ref=CP, dst_ref=A1R.at[ro], send_sem=a1sem.at[0, sem],
            recv_sem=a1sem.at[1, sem], device_id={"rollout": peer}, device_id_type=MESH).start()

    loop(1, 4, lambda k: send_piece(lax.rem(ro + 2 * k, R), 0))
    other = ro + 1 - 2 * lax.rem(ro, 2)
    loop(0, 4, lambda k: send_piece(lax.rem(other + 2 * k, R), 1))
    loop(0, 8, lambda q: tensor_copy(
        wo_columns(q, 1 - core), WO.at[q, wo_rows, :], wosem.at[0], wosem.at[1], sib).start())

    def permute_hidden(j):
        for c in range(4):
            at = pl.multiple_of(CHUNK * j + 128 * c, 128)
            HF[c] = hid[:, pl.ds(at, 128)].astype(f32)
        for c in range(4):
            for i in range(4):
                ST[j, 16 * i:16 * i + 16, 128 * c:128 * c + 128] = (
                    HF[c, pl.ds(i, 16, stride=4), :].astype(bf16))
    loop(0, T, permute_hidden)

    Q32[320:512, :] = jnp.zeros((192, 128), f32)

    def square_sum(j, total):
        x = ST[j].astype(f32)
        x = x * x
        return total + (x[:, 0:128] + x[:, 128:256]) + (x[:, 256:384] + x[:, 384:512])

    def normalize(total):
        inv = lax.rsqrt(jnp.sum(total, axis=1, keepdims=True) * (1.0 / D) + norm_epsilon)
        def body(j):
            NB[j] = (ST[j].astype(f32) * inv * gain[j]).astype(bf16)
        loop(0, T, body)

    zero_total = jnp.zeros((64, 128), f32)
    zero_query = jnp.zeros((64, CHUNK), f32)
    normalize(lax.fori_loop(0, T, square_sum, zero_total))

    def project_kv(j, new):
        columns = pl.ds(pl.multiple_of(CHUNK * j, CHUNK), CHUNK)
        return new + mm_t(NB[j], WKV[:, columns])

    for half in range(2):
        z = lax.rem(ro + half, 2)
        wait(A1R.at[pl.ds(0, 3 + half)], a1sem.at[1, half])
        for y in range(4):
            held = A1R[2 * y + z].astype(f32).reshape(T, 8, 128)
            OF[:, 8 * y:8 * y + 8, :] = held
        A2S[half] = OF[...].astype(bf16)
        loop(1, T, lambda k: tensor_copy(
            A2S.at[half, lax.rem(me + k, T)], A2R.at[z, me], a2sem.at[half, 0],
            a2sem.at[half, 1], lax.rem(me + k, T)).start())
        A2R[z, me] = A2S[half, me]

    wait(WKV.at[pl.ds(0, 64), :], lsem.at[16])
    wait(WKV.at[pl.ds(64, 64), :], lsem.at[17])
    new = lax.fori_loop(0, T, project_kv, zero_total, unroll=4)
    wait(WQ, lsem.at[0])
    for half in range(2):
        wait(A2R.at[0, pl.ds(0, T - 1)], a2sem.at[half, 1])

    for z in range(2):
        arrived = A2R[z].astype(f32).reshape(T, 4, 8, 128)
        for y in range(4):
            r = 2 * y + z
            XF[128 * r:128 * r + 128, :] = arrived[:, y].reshape(128, 128)
    FL = AOE
    for s in range(8):
        FL[pl.ds(s, 128, stride=8), :] = mm(place, XF[pl.ds(s, 128, stride=8), :].astype(bf16))
    spread_pairs(FL[0:256, :], AE)
    AQ[me] = (AE[0:256, :] + swap_halves(AE[256:512, :])).astype(bf16)
    loop(1, 8, lambda k: tensor_copy(
        AQ.at[me], AQ.at[me], a3dsem.at[0, k], a3dsem.at[1, k], lax.rem(me + 2 * k, T)).start())
    tensor_copy(AQ.at[me], AQ.at[me], a3fsem.at[0, 0], a3fsem.at[1, 0], sib).start()
    for c in range(4):
        up = (low_rank_scale * FL[pl.ds(256 + c, 64, stride=4), :]).astype(bf16)
        none = jnp.zeros_like(up)
        BQ[0, 0:64, 128 * c:128 * c + 128] = up
        BQ[0, 64:128, 128 * c:128 * c + 128] = none
        BQ[1, 0:64, 128 * c:128 * c + 128] = none
        BQ[1, 64:128, 128 * c:128 * c + 128] = up
        up = FL[pl.ds(768 + c, 64, stride=4), :].astype(bf16)
        BO[0:64, 128 * c:128 * c + 128] = up
        BO[64:128, 128 * c:128 * c + 128] = up
    AOS[...] = FL[512:768, :].astype(bf16).reshape(8, 32, 128)

    def merge(j):
        strip = pl.ds(pl.multiple_of(16 * j, 16), 16)
        for half in range(2):
            blocks = pl.ds(16 * half, 16)
            for n in range(2):
                columns = slice(256 * n, 256 * n + 256)
                change = mm(AQ[j], BQ[half, :, columns]).reshape(16, 16, 256)
                WQ[blocks, strip, columns] = (
                    WQ[blocks, strip, columns].astype(f32) + change).astype(bf16)

    def own_side(k):
        return lax.rem(me + T - 2 * k, T)

    def other_side(k):
        return lax.rem(sib + T - 2 * k, T)

    def pass_on_strips(k):
        j = own_side(k)
        wait(AQ.at[j], a3dsem.at[1, k])
        tensor_copy(AQ.at[j], AQ.at[j], a3fsem.at[0, k], a3fsem.at[1, k], sib).start()

    wait(KV, lsem.at[19])

    def part_cache(n):
        i, g = n // KV_HEADS, lax.rem(n, KV_HEADS)
        DI[...] = KV[i, g].reshape(2 * CAP, HEAD_DIM).astype(f32)
        KEYS[i, g] = DI[pl.ds(0, CAP, stride=2), :].astype(bf16)
        VALS[i, g] = DI[pl.ds(1, CAP, stride=2), :].astype(bf16)

    merge(me)
    loop(0, 4 * KV_HEADS, part_cache)
    loop(1, 8, pass_on_strips)
    loop(1, 8, lambda k: merge(own_side(k)))
    loop(0, 8, lambda k: wait(AQ.at[other_side(k)], a3fsem.at[1, k]))
    loop(0, 8, lambda k: merge(other_side(k)))

    low_half = lanes((8, 128)) < 64
    sub = lax.broadcasted_iota(jnp.int32, (8, 128), 0) & 3
    lengths = jnp.zeros((8, 128), jnp.int32)
    for i in range(4):
        lengths = jnp.where(sub == i, lens[i], lengths)
    wide = lanes((64, CAP))

    for s in range(STEPS):
        def project(j, q):
            return q + mm(NB[j], WQ[pl.ds(2 * j, 2)].reshape(CHUNK, CHUNK))

        if s == 0:
            q = lax.fori_loop(0, T, project, zero_query, unroll=4)
        for h in range(4):
            Q32[64 * h:64 * h + 64, :] = q[:, 128 * h:128 * h + 128]
        Q32[256:320, :] = new
        for t in range(T):
            QS[s, t] = Q32[pl.ds(t, 32, stride=16), :].astype(bf16)
        loop(1, T, lambda k: tensor_copy(
            QS.at[s, lax.rem(me + k, T)], QR.at[s, me], qsem.at[s, 0], qsem.at[s, 1],
            lax.rem(me + k, T)).start())
        QR[s, me] = QS[s, me]
        if s == 0:
            loop(1, T, lambda k: tensor_copy(
                AOS.at[lax.rem(me + k, T) // 2], AOR.at[me], aosem.at[0], aosem.at[1],
                lax.rem(me + k, T)).start())
            AOR[me] = AOS[chip]

        angles = (lengths + s).astype(f32) * freq[...]
        cosine = jnp.cos(angles)
        sine = jnp.where(low_half, -jnp.sin(angles), jnp.sin(angles))

        wait(QR.at[s, pl.ds(0, T - 1)], qsem.at[s, 1])
        got = QR[s].astype(f32)
        heads = got[:, 0:16].reshape(T, 2, 8, 128)
        heads = heads * cosine + swap_halves(heads) * sine
        QX[...] = heads.astype(bf16).astype(f32).reshape(256, 128)
        fresh = got[:, 16:24].reshape(8, 2, 8, 128)
        even, odd = fresh[:, 0], fresh[:, 1]
        low = lanes(even.shape) < 64
        key = jnp.where(low, even, swap_halves(odd))
        key = key * cosine + swap_halves(key) * sine
        KN[s] = key.astype(bf16).astype(f32).reshape(64, 128)
        VN[s] = jnp.where(low, swap_halves(even), odd).reshape(64, 128)


        def attend(i):
            queries = [QX[pl.ds(32 * g + i, 8, stride=4), :] for g in range(KV_HEADS)]
            scores = jnp.concatenate(
                [mm_t(queries[g].astype(bf16), KEYS[i, g])
                 for g in range(KV_HEADS)], axis=0) * score_scale
            scores = jnp.where(wide < lens[i], scores, -1e30)
            rows = jnp.concatenate(queries, axis=0)
            largest = jnp.max(scores, axis=1, keepdims=True)
            news, values = [], []
            for n in range(s + 1):
                k = KN[n, pl.ds(i, 8, stride=8), :]
                v = VN[n, pl.ds(i, 8, stride=8), :]
                k = jnp.broadcast_to(k[:, None, :], (8, 8, 128)).reshape(64, 128)
                values.append(jnp.broadcast_to(v[:, None, :], (8, 8, 128)).reshape(64, 128))
                news.append(jnp.sum(rows * k, axis=1, keepdims=True) * score_scale)
                largest = jnp.maximum(largest, news[-1])
            expo = jnp.exp(scores - largest)
            news = [jnp.exp(x - largest) for x in news]
            total = jnp.sum(expo, axis=1, keepdims=True)
            for x in news:
                total = total + x
            share = 1.0 / total
            weights = (expo * share).astype(bf16)
            result = jnp.concatenate(
                [mm(weights[8 * g:8 * g + 8], VALS[i, g])
                 for g in range(KV_HEADS)], axis=0)
            for x, v in zip(news, values):
                result = result + (x * share).astype(bf16).astype(f32) * v
            AF[pl.ds(i, 64, stride=4), :] = result

        for i in range(4):
            attend(i)
        AM[s] = AF[...].astype(bf16).reshape(8, 32, 128)
        loop(1, T, lambda k: tensor_copy(
            AM.at[s, lax.rem(me + k, T) // 2], AR.at[s, me], asem.at[s, 0], asem.at[s, 1],
            lax.rem(me + k, T)).start())
        AR[s, me] = AM[s, chip]
        if s == 0:
            wait(AOR.at[pl.ds(0, T - 1)], aosem.at[1])
            blocks = AOR[...].astype(f32).reshape(T, 4, 8, 128)
            for b in range(4):
                XF[128 * b:128 * b + 128, :] = blocks[:, b].reshape(128, 128)
            spread_pairs(XF[0:512, :], AOE)
            AO[...] = AOE[...].astype(bf16)
        wait(AR.at[s, pl.ds(0, T - 1)], asem.at[s, 1])
        XF[0:512, :] = AR[s].astype(f32).reshape(512, 128)
        for h in range(8):
            for i in range(4):
                AT[16 * i:16 * i + 16, 128 * h:128 * h + 128] = (
                    XF[pl.ds(4 * h + i, 16, stride=32), :].astype(bf16))

        attended = AT[...]
        if s == 0:
            wait(WO.at[:, pl.ds(0, CHUNK), :], lsem.at[18])
            wait(WO.at[:, pl.ds(0, CHUNK), :], wosem.at[1])

        halves = [slice(256 * half, 256 * half + 256) for half in range(2)]

        def send_parts(half):
            def part(k):
                q = lax.rem(chip + k, 8)
                RSS[s, half, q] = mm(AT[...], WO[q, :, halves[half]]).astype(bf16)
                tensor_copy(
                    RSS.at[s, half, q], RB.at[s, half, chip], rssem.at[s, half, 0],
                    rssem.at[s, half, 1], 2 * q + core).start()
            loop(1, 8, part)

        send_parts(0)
        t = mm(attended, AO[...])
        TOS[s] = pack_rank(t).astype(bf16)
        loop(1, 8, lambda k: tensor_copy(
            TOS.at[s], TOR.at[s, chip], tosem.at[s, 0], tosem.at[s, 1],
            lax.rem(me + 2 * k, T)).start())
        TOR[s, chip] = TOS[s]
        send_parts(1)
        bases = []
        for half in range(2):
            own = ST[me, :, halves[half]] if s == 0 else SG[me, half]
            bases.append(mm(attended, WO[chip, :, halves[half]]) + own.astype(f32))
        wait(TOR.at[s, pl.ds(0, 7)], tosem.at[s, 1])
        rank = unpack_split(jnp.sum(TOR[s].astype(f32), axis=0))
        parts = []
        for half in range(2):
            y = bases[half] + low_rank_scale * mm(rank, BO[:, halves[half]])
            RB[s, half, chip] = jnp.zeros((64, CHUNK // 2), bf16)
            wait(RB.at[s, half, pl.ds(0, 7)], rssem.at[s, half, 1])
            for q in range(8):
                y = y + RB[s, half, q].astype(f32)
            y = y.astype(bf16)
            parts.append(y)
            if s + 1 < STEPS:
                SG[me, half] = y
                if half == 1:
                    squares = [x.astype(f32) * x.astype(f32) for x in parts]
                    squares = (squares[0][:, 0:128] + squares[0][:, 128:256]) + (
                        squares[1][:, 0:128] + squares[1][:, 128:256])
                    SQS[...] = jnp.zeros_like(SQS)
                    SQS[0:1, 0:64] = jnp.sum(squares.T, axis=0, keepdims=True)
                    loop(1, T, lambda k: tensor_copy(
                        SQS, SQR.at[me], sqsem.at[0], sqsem.at[1], lax.rem(me + k, T)).start())
                loop(1, 8, lambda k: tensor_copy(
                    SG.at[me, half], SG.at[me, half], agdsem.at[0, half, k],
                    agdsem.at[1, half, k], lax.rem(me + 2 * k, T)).start())
                tensor_copy(
                    SG.at[me, half], SG.at[me, half], agfsem.at[0, half, 0],
                    agfsem.at[1, half, 0], sib).start()
        y = jnp.concatenate(parts, axis=1)
        yf = y.astype(f32)
        for c in range(4):
            for i in range(4):
                OUTF[c, pl.ds(i, 16, stride=4), :] = yf[16 * i:16 * i + 16, 128 * c:128 * c + 128]
        for c in range(4):
            out[s, :, 128 * c:128 * c + 128] = OUTF[c].astype(bf16)

        if s + 1 < STEPS:
            def pass_on_stream(half):
                def pass_on(k):
                    j = own_side(k)
                    wait(SG.at[j, half], agdsem.at[1, half, k])
                    tensor_copy(
                        SG.at[j, half], SG.at[j, half], agfsem.at[0, half, k],
                        agfsem.at[1, half, k], sib).start()
                loop(1, 8, pass_on)

            pass_on_stream(0)
            SQR[me] = SQS[...]
            wait(SQR.at[pl.ds(0, T - 1)], sqsem.at[1])
            total = jnp.sum(SQR[...], axis=0)[0:1]
            total = jnp.broadcast_to(total, (128, 128)).T[0:64, 0:1]
            inv = lax.rsqrt(total * (1.0 / D) + norm_epsilon)

            def take(j, half, carry):
                q, new = carry
                x = (SG[j, half].astype(f32) * inv * gain[j, :, halves[half]]).astype(bf16)
                columns = pl.ds(pl.multiple_of(CHUNK * j + 256 * half, 256), 256)
                return q + mm(x, WQ[2 * j + half]), new + mm_t(x, WKV[:, columns])

            carry = (zero_query, zero_total)
            for half in range(2):
                if half == 1:
                    pass_on_stream(1)
                carry = lax.fori_loop(
                    0, 8, lambda k, c: take(own_side(k), half, c), carry, unroll=4)
                loop(0, 8, lambda k: wait(SG.at[other_side(k), half], agfsem.at[1, half, k]))
                carry = lax.fori_loop(
                    0, 8, lambda k, c: take(other_side(k), half, c), carry, unroll=4)
            q, new = carry

    wait(A1R.at[pl.ds(0, 3)], a1sem.at[0, 0])
    wait(A1R.at[pl.ds(0, 4)], a1sem.at[0, 1])
    wait(WO.at[:, pl.ds(0, CHUNK), :], wosem.at[0])
    for half in range(2):
        wait(A2R.at[0, pl.ds(0, T - 1)], a2sem.at[half, 0])
    loop(1, 8, lambda k: wait(AQ.at[me], a3dsem.at[0, k]))
    loop(0, 8, lambda k: wait(AQ.at[me], a3fsem.at[0, k]))
    wait(AOR.at[pl.ds(0, T - 1)], aosem.at[0])
    for s in range(STEPS):
        wait(QR.at[s, pl.ds(0, T - 1)], qsem.at[s, 0])
        wait(AR.at[s, pl.ds(0, T - 1)], asem.at[s, 0])
        wait(TOR.at[s, pl.ds(0, 7)], tosem.at[s, 0])
        for half in range(2):
            wait(RB.at[s, half, pl.ds(0, 7)], rssem.at[s, half, 0])
    for half in range(2):
        loop(1, 8, lambda k: wait(SG.at[me, half], agdsem.at[0, half, k]))
        loop(0, 8, lambda k: wait(SG.at[me, half], agfsem.at[0, half, k]))
    wait(SQR.at[pl.ds(0, T - 1)], sqsem.at[0])


def body(
    hidden_in,
    norm_gain,
    query_weight_base,
    w_key,
    w_value,
    output_weight_base,
    kv_cache,
    cache_lengths,
    adapter_shards,
    shard_order,
):
    half_dim = HEAD_DIM // 2
    exponent = np.arange(half_dim, dtype=np.float32) * np.float32(2.0 / HEAD_DIM)
    frequency = np.float32(rope_theta) ** (-exponent)
    freq = jnp.asarray(np.concatenate([frequency, frequency]).reshape(1, HEAD_DIM))
    vmem = pl.BlockSpec(memory_space=pltpu.VMEM)
    smem = pl.BlockSpec(memory_space=pltpu.SMEM)
    hbm = pl.BlockSpec(memory_space=pl.ANY)
    V = pltpu.VMEM
    dma = pltpu.SemaphoreType.DMA
    return pl.pallas_call(
        kernel,
        out_shape=jax.ShapeDtypeStruct((STEPS, 64, CHUNK), bf16),
        in_specs=[vmem, vmem, hbm, hbm, hbm, hbm, hbm, smem, vmem, vmem, vmem],
        out_specs=vmem,
        scratch_shapes=[
            V((32, 256, CHUNK), bf16),
            V((128, D), bf16),
            V((8, 2 * CHUNK, CHUNK), bf16),
            V((4, KV_HEADS, CAP, 2, HEAD_DIM), bf16),
            V((4, 64, 128), f32),
            V((T, 64, CHUNK), bf16),
            V((T, 2, 64, CHUNK // 2), bf16),
            V((T, 64, CHUNK), bf16),
            V((128, 128), f32),
            V((128, 128), bf16),
            V((R, 128, 128), bf16),
            V((2, T, 32, 128), bf16),
            V((2, T, 32, 128), bf16),
            V((1024, 128), f32),
            V((T, 32, 128), f32),
            V((512, 128), f32),
            V((T, 256, 128), bf16),
            V((2, 128, CHUNK), bf16),
            V((128, CHUNK), bf16),
            V((8, 32, 128), bf16),
            V((T, 32, 128), bf16),
            V((1024, 128), f32),
            V((1024, 128), bf16),
            V((512, 128), f32),
            V((STEPS, T, 32, 128), bf16),
            V((STEPS, T, 32, 128), bf16),
            V((256, 128), f32),
            V((STEPS, 64, 128), f32),
            V((STEPS, 64, 128), f32),
            V((256, 128), f32),
            V((STEPS, 8, 32, 128), bf16),
            V((STEPS, T, 32, 128), bf16),
            V((64, 2 * CHUNK), bf16),
            V((STEPS, 32, 128), bf16),
            V((STEPS, 8, 32, 128), bf16),
            V((STEPS, 2, 8, 64, CHUNK // 2), bf16),
            V((STEPS, 2, 8, 64, CHUNK // 2), bf16),
            V((4, 64, 128), f32),
            V((8, 128), f32),
            V((T, 8, 128), f32),
            V((2 * CAP, HEAD_DIM), f32),
            V((4, KV_HEADS, CAP, HEAD_DIM), bf16),
            V((4, KV_HEADS, CAP, HEAD_DIM), bf16),
            dma((20,)),
            dma((2,)),
            dma((2, 2)),
            dma((2, 2)),
            dma((2, 8)),
            dma((2, 8)),
            dma((2,)),
            dma((STEPS, 2)),
            dma((STEPS, 2)),
            dma((STEPS, 2)),
            dma((STEPS, 2, 2)),
            dma((2, 2, 8)),
            dma((2, 2, 8)),
            dma((2,)),
        ],
        compiler_params=pltpu.CompilerParams(
            collective_id=0, has_side_effects=True, vmem_limit_bytes=56 * 2**20
        ),
        cost_estimate=pl.CostEstimate(
            flops=5 * 10**9, bytes_accessed=25 * 2**20, transcendentals=10**6
        ),
    )(
        hidden_in,
        norm_gain.reshape(T, 1, CHUNK),
        query_weight_base.reshape(32, 256, CHUNK),
        w_key.T,
        w_value.T,
        output_weight_base,
        kv_cache,
        cache_lengths,
        freq,
        adapter_shards,
        shard_order.reshape(1, 128),
    )


def solution(mesh):
    return jax.shard_map(
        body,
        mesh=mesh,
        in_specs=(
            P("rollout", None),
            P(),
            P(None, "tensor"),
            P(None, "tensor"),
            P(None, "tensor"),
            P("tensor", None),
            P(("rollout", "tensor"), None, None, None),
            P(("rollout", "tensor")),
            P(("rollout", "tensor"), None),
            P(),
        ),
        out_specs=P(None, "rollout", "tensor"),
        check_vma=False,
    )
```

```python
import jax
import jax.numpy as jnp
import numpy as np
from jax import lax
from jax.experimental import pallas as pl
from jax.experimental.pallas import tpu as pltpu
from jax.sharding import PartitionSpec as P

D = 8192
HEADS = 64
KV_HEADS = 8
HEAD_DIM = 128
RANK = 64
STEPS = 2
CAP = 256
T = 16
R = 8
CHUNK = D // T

low_rank_scale = 2.0
norm_epsilon = 1e-05
rope_theta = 500000.0
score_scale = 1.0 / np.sqrt(np.float32(HEAD_DIM))

f32 = jnp.float32
bf16 = jnp.bfloat16
MESH = pl.DeviceIdType.MESH


def mm(a, b):
    return jnp.dot(a, b, preferred_element_type=f32)


def mm_t(a, b):
    return lax.dot_general(a, b, (((1,), (1,)), ((), ())), preferred_element_type=f32)


def lanes(shape):
    return lax.broadcasted_iota(jnp.int32, shape, len(shape) - 1)


def swap_halves(x):
    return pltpu.roll(x, 64, len(x.shape) - 1)


def spread_pairs(x, ref):
    low = lanes(x.shape) < 64
    rows = x.shape[0]
    ref[pl.ds(0, rows, stride=2), :] = jnp.where(low, x, 0.0)
    ref[pl.ds(1, rows, stride=2), :] = jnp.where(low, swap_halves(x), 0.0)


def pack_rank(t):
    return t[0:32] + swap_halves(t[32:64])


def unpack_split(total):
    high = total.astype(bf16).astype(f32)
    rest = total - high
    low = lanes(total.shape) < 64
    top = jnp.where(low, high, swap_halves(rest))
    bottom = jnp.where(low, swap_halves(high), rest)
    return jnp.concatenate([top, bottom], axis=0).astype(bf16)


def kernel(
    hid, gain, wq, wk_t, wv_t, wo, kv, lens, freq, piece, order,
    out,
    WQ, WKV, WO, KV, HF, ST, SG, NB,
    PF, CP, A1R, A2S, A2R, XF, OF, AE, AQ, BQ, BO, AOS, AOR, AOE, AO,
    Q32, QS, QR, QX, KN, VN, AF, AM, AR, AT, TOS, TOR, RSS, RB, OUTF, SQS, SQR, DI, KEYS, VALS,
    lsem, wosem, a1sem, a2sem, a3dsem, a3fsem, aosem, qsem, asem, tosem, rssem, agdsem, agfsem, sqsem,
):
    me = lax.axis_index("tensor")
    ro = lax.axis_index("rollout")
    core = lax.rem(me, 2)
    chip = me // 2
    sib = me + 1 - 2 * core

    def wait(ref, sem):
        pltpu.make_async_copy(ref, ref, sem).wait()

    def tensor_copy(src, dst, send, recv, peer):
        return pltpu.make_async_remote_copy(
            src_ref=src, dst_ref=dst, send_sem=send, recv_sem=recv,
            device_id={"tensor": peer}, device_id_type=MESH,
        )

    def loop(lo, hi, body):
        def step(k, carry):
            body(k)
            return carry
        lax.fori_loop(lo, hi, step, 0)

    barrier = pltpu.get_barrier_semaphore()
    loop(1, T, lambda k: pl.semaphore_signal(
        barrier, inc=1, device_id={"tensor": lax.rem(me + k, T)}, device_id_type=MESH))
    loop(1, R, lambda k: pl.semaphore_signal(
        barrier, inc=1, device_id={"rollout": lax.rem(ro + k, R)}, device_id_type=MESH))

    for j in range(8):
        pltpu.make_async_copy(
            wq.at[pl.ds(4 * j, 4)], WQ.at[pl.ds(4 * j, 4)], lsem.at[0]).start()
    pltpu.make_async_copy(wk_t, WKV.at[pl.ds(0, 64), :], lsem.at[16]).start()
    pltpu.make_async_copy(wv_t, WKV.at[pl.ds(64, 64), :], lsem.at[17]).start()
    for i in range(4):
        for g in range(KV_HEADS):
            pltpu.make_async_copy(
                kv.at[i, :, :, pl.ds(HEAD_DIM * g, HEAD_DIM)], KV.at[i, g], lsem.at[19]).start()

    def wo_columns(q, parity):
        return wo.at[:, pl.ds(pl.multiple_of((2 * q + parity) * CHUNK, CHUNK), CHUNK)]

    wo_rows = pl.ds(pl.multiple_of(core * CHUNK, CHUNK), CHUNK)
    loop(0, 8, lambda q: pltpu.make_async_copy(
        wo_columns(q, core), WO.at[q, wo_rows, :], lsem.at[18]).start())

    order_row = order[...]
    mine = jnp.sum(
        jnp.where(lanes((1, 128)) == ro * T + me, order_row, 0), axis=1, keepdims=True)
    is_up = jnp.broadcast_to((mine >> 5) & 1, (128, 128))
    row = lax.broadcasted_iota(jnp.int32, (128, 128), 0)
    up_row = 64 * ((row >> 2) & 1) + 4 * (row >> 3) + (row & 3)
    wanted = jnp.where(is_up == 1, up_row, row)
    pick = jnp.where(lanes((128, 128)) == wanted, 1.0, 0.0).astype(bf16)
    flat = piece[...].astype(f32)
    for r in range(128):
        PF[r:r + 1, :] = flat[:, 128 * r:128 * r + 128]
    CP[...] = mm(pick, PF[...].astype(bf16)).astype(bf16)
    A1R[ro] = CP[...]
    place = jnp.where(row == jnp.broadcast_to(order_row, (128, 128)), 1.0, 0.0).astype(bf16)

    pl.semaphore_wait(barrier, T - 1 + R - 1)

    def send_piece(peer, sem):
        pltpu.make_async_remote_copy(
            src_ref=CP, dst_ref=A1R.at[ro], send_sem=a1sem.at[0, sem],
            recv_sem=a1sem.at[1, sem], device_id={"rollout": peer}, device_id_type=MESH).start()

    loop(1, 4, lambda k: send_piece(lax.rem(ro + 2 * k, R), 0))
    other = ro + 1 - 2 * lax.rem(ro, 2)
    loop(0, 4, lambda k: send_piece(lax.rem(other + 2 * k, R), 1))
    loop(0, 8, lambda q: tensor_copy(
        wo_columns(q, 1 - core), WO.at[q, wo_rows, :], wosem.at[0], wosem.at[1], sib).start())

    def permute_hidden(j):
        for c in range(4):
            at = pl.multiple_of(CHUNK * j + 128 * c, 128)
            HF[c] = hid[:, pl.ds(at, 128)].astype(f32)
        for c in range(4):
            for i in range(4):
                ST[j, 16 * i:16 * i + 16, 128 * c:128 * c + 128] = (
                    HF[c, pl.ds(i, 16, stride=4), :].astype(bf16))
    loop(0, T, permute_hidden)

    Q32[320:512, :] = jnp.zeros((192, 128), f32)

    def square_sum(j, total):
        x = ST[j].astype(f32)
        x = x * x
        return total + (x[:, 0:128] + x[:, 128:256]) + (x[:, 256:384] + x[:, 384:512])

    def normalize(total):
        inv = lax.rsqrt(jnp.sum(total, axis=1, keepdims=True) * (1.0 / D) + norm_epsilon)
        def body(j):
            NB[j] = (ST[j].astype(f32) * inv * gain[j]).astype(bf16)
        loop(0, T, body)

    zero_total = jnp.zeros((64, 128), f32)
    zero_query = jnp.zeros((64, CHUNK), f32)
    normalize(lax.fori_loop(0, T, square_sum, zero_total))

    def project_kv(j, new):
        columns = pl.ds(pl.multiple_of(CHUNK * j, CHUNK), CHUNK)
        return new + mm_t(NB[j], WKV[:, columns])

    for half in range(2):
        z = lax.rem(ro + half, 2)
        wait(A1R.at[pl.ds(0, 3 + half)], a1sem.at[1, half])
        for y in range(4):
            held = A1R[2 * y + z].astype(f32).reshape(T, 8, 128)
            OF[:, 8 * y:8 * y + 8, :] = held
        A2S[half] = OF[...].astype(bf16)
        loop(1, T, lambda k: tensor_copy(
            A2S.at[half, lax.rem(me + k, T)], A2R.at[z, me], a2sem.at[half, 0],
            a2sem.at[half, 1], lax.rem(me + k, T)).start())
        A2R[z, me] = A2S[half, me]

    wait(WKV.at[pl.ds(0, 64), :], lsem.at[16])
    wait(WKV.at[pl.ds(64, 64), :], lsem.at[17])
    new = lax.fori_loop(0, T, project_kv, zero_total, unroll=4)
    wait(WQ, lsem.at[0])
    for half in range(2):
        wait(A2R.at[0, pl.ds(0, T - 1)], a2sem.at[half, 1])

    for z in range(2):
        arrived = A2R[z].astype(f32).reshape(T, 4, 8, 128)
        for y in range(4):
            r = 2 * y + z
            XF[128 * r:128 * r + 128, :] = arrived[:, y].reshape(128, 128)
    FL = AOE
    for s in range(8):
        FL[pl.ds(s, 128, stride=8), :] = mm(place, XF[pl.ds(s, 128, stride=8), :].astype(bf16))
    spread_pairs(FL[0:256, :], AE)
    for r in range(2):
        AQ[me, r] = (AE[128 * r:128 * r + 128, :] + swap_halves(
            AE[256 + 128 * r:384 + 128 * r, :])).astype(bf16)
        loop(1, 8, lambda k: tensor_copy(
            AQ.at[me, r], AQ.at[me, r], a3dsem.at[0, r, k], a3dsem.at[1, r, k],
            lax.rem(me + 2 * k, T)).start())
        tensor_copy(
            AQ.at[me, r], AQ.at[me, r], a3fsem.at[0, r, 0], a3fsem.at[1, r, 0], sib).start()
    for c in range(4):
        up = (low_rank_scale * FL[pl.ds(256 + c, 64, stride=4), :]).astype(bf16)
        none = jnp.zeros_like(up)
        BQ[0, 0:64, 128 * c:128 * c + 128] = up
        BQ[0, 64:128, 128 * c:128 * c + 128] = none
        BQ[1, 0:64, 128 * c:128 * c + 128] = none
        BQ[1, 64:128, 128 * c:128 * c + 128] = up
        up = FL[pl.ds(768 + c, 64, stride=4), :].astype(bf16)
        BO[0:64, 128 * c:128 * c + 128] = up
        BO[64:128, 128 * c:128 * c + 128] = up
    AOS[...] = FL[512:768, :].astype(bf16).reshape(8, 32, 128)

    def merge(j, r):
        strip = pl.ds(pl.multiple_of(16 * j, 16), 16)
        for half in range(2):
            blocks = pl.ds(16 * half + 8 * r, 8)
            for n in range(2):
                columns = slice(256 * n, 256 * n + 256)
                change = mm(AQ[j, r], BQ[half, :, columns]).reshape(8, 16, 256)
                WQ[blocks, strip, columns] = (
                    WQ[blocks, strip, columns].astype(f32) + change).astype(bf16)

    def own_side(k):
        return lax.rem(me + T - 2 * k, T)

    def other_side(k):
        return lax.rem(sib + T - 2 * k, T)

    def pass_on_strips(r):
        def pass_on(k):
            j = own_side(k)
            wait(AQ.at[j, r], a3dsem.at[1, r, k])
            tensor_copy(
                AQ.at[j, r], AQ.at[j, r], a3fsem.at[0, r, k], a3fsem.at[1, r, k], sib).start()
        loop(1, 8, pass_on)

    wait(KV, lsem.at[19])

    def part_cache(n):
        i, g = n // KV_HEADS, lax.rem(n, KV_HEADS)
        DI[...] = KV[i, g].reshape(2 * CAP, HEAD_DIM).astype(f32)
        KEYS[i, g] = DI[pl.ds(0, CAP, stride=2), :].astype(bf16)
        VALS[i, g] = DI[pl.ds(1, CAP, stride=2), :].astype(bf16)

    merge(me, 0)
    merge(me, 1)
    loop(0, 4 * KV_HEADS, part_cache)
    for r in range(2):
        pass_on_strips(r)
        loop(1, 8, lambda k: merge(own_side(k), r))
        loop(0, 8, lambda k: wait(AQ.at[other_side(k), r], a3fsem.at[1, r, k]))
        loop(0, 8, lambda k: merge(other_side(k), r))

    low_half = lanes((8, 128)) < 64
    sub = lax.broadcasted_iota(jnp.int32, (8, 128), 0) & 3
    lengths = jnp.zeros((8, 128), jnp.int32)
    for i in range(4):
        lengths = jnp.where(sub == i, lens[i], lengths)
    wide = lanes((64, CAP))

    for s in range(STEPS):
        def project(j, q):
            return q + mm(NB[j], WQ[pl.ds(2 * j, 2)].reshape(CHUNK, CHUNK))

        if s == 0:
            q = lax.fori_loop(0, T, project, zero_query, unroll=4)
        for h in range(4):
            Q32[64 * h:64 * h + 64, :] = q[:, 128 * h:128 * h + 128]
        Q32[256:320, :] = new
        for t in range(T):
            QS[s, t] = Q32[pl.ds(t, 32, stride=16), :].astype(bf16)
        loop(1, T, lambda k: tensor_copy(
            QS.at[s, lax.rem(me + k, T)], QR.at[s, me], qsem.at[s, 0], qsem.at[s, 1],
            lax.rem(me + k, T)).start())
        QR[s, me] = QS[s, me]
        if s == 0:
            loop(1, T, lambda k: tensor_copy(
                AOS.at[lax.rem(me + k, T) // 2], AOR.at[me], aosem.at[0], aosem.at[1],
                lax.rem(me + k, T)).start())
            AOR[me] = AOS[chip]

        angles = (lengths + s).astype(f32) * freq[...]
        cosine = jnp.cos(angles)
        sine = jnp.where(low_half, -jnp.sin(angles), jnp.sin(angles))

        wait(QR.at[s, pl.ds(0, T - 1)], qsem.at[s, 1])
        got = QR[s].astype(f32)
        heads = got[:, 0:16].reshape(T, 2, 8, 128)
        heads = heads * cosine + swap_halves(heads) * sine
        QX[...] = heads.astype(bf16).astype(f32).reshape(256, 128)
        fresh = got[:, 16:24].reshape(8, 2, 8, 128)
        even, odd = fresh[:, 0], fresh[:, 1]
        low = lanes(even.shape) < 64
        key = jnp.where(low, even, swap_halves(odd))
        key = key * cosine + swap_halves(key) * sine
        KN[s] = key.astype(bf16).astype(f32).reshape(64, 128)
        VN[s] = jnp.where(low, swap_halves(even), odd).reshape(64, 128)


        def attend(i):
            queries = [QX[pl.ds(32 * g + i, 8, stride=4), :] for g in range(KV_HEADS)]
            scores = jnp.concatenate(
                [mm_t(queries[g].astype(bf16), KEYS[i, g])
                 for g in range(KV_HEADS)], axis=0) * score_scale
            scores = jnp.where(wide < lens[i], scores, -1e30)
            rows = jnp.concatenate(queries, axis=0)
            largest = jnp.max(scores, axis=1, keepdims=True)
            news, values = [], []
            for n in range(s + 1):
                k = KN[n, pl.ds(i, 8, stride=8), :]
                v = VN[n, pl.ds(i, 8, stride=8), :]
                k = jnp.broadcast_to(k[:, None, :], (8, 8, 128)).reshape(64, 128)
                values.append(jnp.broadcast_to(v[:, None, :], (8, 8, 128)).reshape(64, 128))
                news.append(jnp.sum(rows * k, axis=1, keepdims=True) * score_scale)
                largest = jnp.maximum(largest, news[-1])
            expo = jnp.exp(scores - largest)
            news = [jnp.exp(x - largest) for x in news]
            total = jnp.sum(expo, axis=1, keepdims=True)
            for x in news:
                total = total + x
            share = 1.0 / total
            weights = (expo * share).astype(bf16)
            result = jnp.concatenate(
                [mm(weights[8 * g:8 * g + 8], VALS[i, g])
                 for g in range(KV_HEADS)], axis=0)
            for x, v in zip(news, values):
                result = result + (x * share).astype(bf16).astype(f32) * v
            AF[pl.ds(i, 64, stride=4), :] = result

        for i in range(4):
            attend(i)
        AM[s] = AF[...].astype(bf16).reshape(8, 32, 128)
        loop(1, T, lambda k: tensor_copy(
            AM.at[s, lax.rem(me + k, T) // 2], AR.at[s, me], asem.at[s, 0], asem.at[s, 1],
            lax.rem(me + k, T)).start())
        AR[s, me] = AM[s, chip]
        if s == 0:
            wait(AOR.at[pl.ds(0, T - 1)], aosem.at[1])
            blocks = AOR[...].astype(f32).reshape(T, 4, 8, 128)
            for b in range(4):
                XF[128 * b:128 * b + 128, :] = blocks[:, b].reshape(128, 128)
            spread_pairs(XF[0:512, :], AOE)
            AO[...] = AOE[...].astype(bf16)
        wait(AR.at[s, pl.ds(0, T - 1)], asem.at[s, 1])
        XF[0:512, :] = AR[s].astype(f32).reshape(512, 128)
        for h in range(8):
            for i in range(4):
                AT[16 * i:16 * i + 16, 128 * h:128 * h + 128] = (
                    XF[pl.ds(4 * h + i, 16, stride=32), :].astype(bf16))

        attended = AT[...]
        if s == 0:
            wait(WO.at[:, pl.ds(0, CHUNK), :], lsem.at[18])
            wait(WO.at[:, pl.ds(0, CHUNK), :], wosem.at[1])

        halves = [slice(256 * half, 256 * half + 256) for half in range(2)]

        def send_parts(half):
            def part(k):
                q = lax.rem(chip + k, 8)
                RSS[s, half, q] = mm(AT[...], WO[q, :, halves[half]]).astype(bf16)
                tensor_copy(
                    RSS.at[s, half, q], RB.at[s, half, chip], rssem.at[s, half, 0],
                    rssem.at[s, half, 1], 2 * q + core).start()
            loop(1, 8, part)

        send_parts(0)
        t = mm(attended, AO[...])
        TOS[s] = pack_rank(t).astype(bf16)
        loop(1, 8, lambda k: tensor_copy(
            TOS.at[s], TOR.at[s, chip], tosem.at[s, 0], tosem.at[s, 1],
            lax.rem(me + 2 * k, T)).start())
        TOR[s, chip] = TOS[s]
        send_parts(1)
        bases = []
        for half in range(2):
            own = ST[me, :, halves[half]] if s == 0 else SG[me, half]
            bases.append(mm(attended, WO[chip, :, halves[half]]) + own.astype(f32))
        wait(TOR.at[s, pl.ds(0, 7)], tosem.at[s, 1])
        rank = unpack_split(jnp.sum(TOR[s].astype(f32), axis=0))
        parts = []
        for half in range(2):
            y = bases[half] + low_rank_scale * mm(rank, BO[:, halves[half]])
            RB[s, half, chip] = jnp.zeros((64, CHUNK // 2), bf16)
            wait(RB.at[s, half, pl.ds(0, 7)], rssem.at[s, half, 1])
            for q in range(8):
                y = y + RB[s, half, q].astype(f32)
            y = y.astype(bf16)
            parts.append(y)
            if s + 1 < STEPS:
                SG[me, half] = y
                if half == 1:
                    squares = [x.astype(f32) * x.astype(f32) for x in parts]
                    squares = (squares[0][:, 0:128] + squares[0][:, 128:256]) + (
                        squares[1][:, 0:128] + squares[1][:, 128:256])
                    SQS[...] = jnp.zeros_like(SQS)
                    SQS[0:1, 0:64] = jnp.sum(squares.T, axis=0, keepdims=True)
                    loop(1, T, lambda k: tensor_copy(
                        SQS, SQR.at[me], sqsem.at[0], sqsem.at[1], lax.rem(me + k, T)).start())
                loop(1, 8, lambda k: tensor_copy(
                    SG.at[me, half], SG.at[me, half], agdsem.at[0, half, k],
                    agdsem.at[1, half, k], lax.rem(me + 2 * k, T)).start())
                tensor_copy(
                    SG.at[me, half], SG.at[me, half], agfsem.at[0, half, 0],
                    agfsem.at[1, half, 0], sib).start()
        y = jnp.concatenate(parts, axis=1)
        yf = y.astype(f32)
        for c in range(4):
            for i in range(4):
                OUTF[c, pl.ds(i, 16, stride=4), :] = yf[16 * i:16 * i + 16, 128 * c:128 * c + 128]
        for c in range(4):
            out[s, :, 128 * c:128 * c + 128] = OUTF[c].astype(bf16)

        if s + 1 < STEPS:
            def pass_on_stream(half):
                def pass_on(k):
                    j = own_side(k)
                    wait(SG.at[j, half], agdsem.at[1, half, k])
                    tensor_copy(
                        SG.at[j, half], SG.at[j, half], agfsem.at[0, half, k],
                        agfsem.at[1, half, k], sib).start()
                loop(1, 8, pass_on)

            pass_on_stream(0)
            SQR[me] = SQS[...]
            wait(SQR.at[pl.ds(0, T - 1)], sqsem.at[1])
            total = jnp.sum(SQR[...], axis=0)[0:1]
            total = jnp.broadcast_to(total, (128, 128)).T[0:64, 0:1]
            inv = lax.rsqrt(total * (1.0 / D) + norm_epsilon)

            def take(j, half, carry):
                q, new = carry
                x = (SG[j, half].astype(f32) * inv * gain[j, :, halves[half]]).astype(bf16)
                columns = pl.ds(pl.multiple_of(CHUNK * j + 256 * half, 256), 256)
                return q + mm(x, WQ[2 * j + half]), new + mm_t(x, WKV[:, columns])

            carry = (zero_query, zero_total)
            for half in range(2):
                if half == 1:
                    pass_on_stream(1)
                carry = lax.fori_loop(
                    0, 8, lambda k, c: take(own_side(k), half, c), carry, unroll=4)
                loop(0, 8, lambda k: wait(SG.at[other_side(k), half], agfsem.at[1, half, k]))
                carry = lax.fori_loop(
                    0, 8, lambda k, c: take(other_side(k), half, c), carry, unroll=4)
            q, new = carry

    wait(A1R.at[pl.ds(0, 3)], a1sem.at[0, 0])
    wait(A1R.at[pl.ds(0, 4)], a1sem.at[0, 1])
    wait(WO.at[:, pl.ds(0, CHUNK), :], wosem.at[0])
    for half in range(2):
        wait(A2R.at[0, pl.ds(0, T - 1)], a2sem.at[half, 0])
    for r in range(2):
        loop(1, 8, lambda k: wait(AQ.at[me, r], a3dsem.at[0, r, k]))
        loop(0, 8, lambda k: wait(AQ.at[me, r], a3fsem.at[0, r, k]))
    wait(AOR.at[pl.ds(0, T - 1)], aosem.at[0])
    for s in range(STEPS):
        wait(QR.at[s, pl.ds(0, T - 1)], qsem.at[s, 0])
        wait(AR.at[s, pl.ds(0, T - 1)], asem.at[s, 0])
        wait(TOR.at[s, pl.ds(0, 7)], tosem.at[s, 0])
        for half in range(2):
            wait(RB.at[s, half, pl.ds(0, 7)], rssem.at[s, half, 0])
    for half in range(2):
        loop(1, 8, lambda k: wait(SG.at[me, half], agdsem.at[0, half, k]))
        loop(0, 8, lambda k: wait(SG.at[me, half], agfsem.at[0, half, k]))
    wait(SQR.at[pl.ds(0, T - 1)], sqsem.at[0])


def body(
    hidden_in,
    norm_gain,
    query_weight_base,
    w_key,
    w_value,
    output_weight_base,
    kv_cache,
    cache_lengths,
    adapter_shards,
    shard_order,
):
    half_dim = HEAD_DIM // 2
    exponent = np.arange(half_dim, dtype=np.float32) * np.float32(2.0 / HEAD_DIM)
    frequency = np.float32(rope_theta) ** (-exponent)
    freq = jnp.asarray(np.concatenate([frequency, frequency]).reshape(1, HEAD_DIM))
    vmem = pl.BlockSpec(memory_space=pltpu.VMEM)
    smem = pl.BlockSpec(memory_space=pltpu.SMEM)
    hbm = pl.BlockSpec(memory_space=pl.ANY)
    V = pltpu.VMEM
    dma = pltpu.SemaphoreType.DMA
    return pl.pallas_call(
        kernel,
        out_shape=jax.ShapeDtypeStruct((STEPS, 64, CHUNK), bf16),
        in_specs=[vmem, vmem, hbm, hbm, hbm, hbm, hbm, smem, vmem, vmem, vmem],
        out_specs=vmem,
        scratch_shapes=[
            V((32, 256, CHUNK), bf16),
            V((128, D), bf16),
            V((8, 2 * CHUNK, CHUNK), bf16),
            V((4, KV_HEADS, CAP, 2, HEAD_DIM), bf16),
            V((4, 64, 128), f32),
            V((T, 64, CHUNK), bf16),
            V((T, 2, 64, CHUNK // 2), bf16),
            V((T, 64, CHUNK), bf16),
            V((128, 128), f32),
            V((128, 128), bf16),
            V((R, 128, 128), bf16),
            V((2, T, 32, 128), bf16),
            V((2, T, 32, 128), bf16),
            V((1024, 128), f32),
            V((T, 32, 128), f32),
            V((512, 128), f32),
            V((T, 2, 128, 128), bf16),
            V((2, 128, CHUNK), bf16),
            V((128, CHUNK), bf16),
            V((8, 32, 128), bf16),
            V((T, 32, 128), bf16),
            V((1024, 128), f32),
            V((1024, 128), bf16),
            V((512, 128), f32),
            V((STEPS, T, 32, 128), bf16),
            V((STEPS, T, 32, 128), bf16),
            V((256, 128), f32),
            V((STEPS, 64, 128), f32),
            V((STEPS, 64, 128), f32),
            V((256, 128), f32),
            V((STEPS, 8, 32, 128), bf16),
            V((STEPS, T, 32, 128), bf16),
            V((64, 2 * CHUNK), bf16),
            V((STEPS, 32, 128), bf16),
            V((STEPS, 8, 32, 128), bf16),
            V((STEPS, 2, 8, 64, CHUNK // 2), bf16),
            V((STEPS, 2, 8, 64, CHUNK // 2), bf16),
            V((4, 64, 128), f32),
            V((8, 128), f32),
            V((T, 8, 128), f32),
            V((2 * CAP, HEAD_DIM), f32),
            V((4, KV_HEADS, CAP, HEAD_DIM), bf16),
            V((4, KV_HEADS, CAP, HEAD_DIM), bf16),
            dma((20,)),
            dma((2,)),
            dma((2, 2)),
            dma((2, 2)),
            dma((2, 2, 8)),
            dma((2, 2, 8)),
            dma((2,)),
            dma((STEPS, 2)),
            dma((STEPS, 2)),
            dma((STEPS, 2)),
            dma((STEPS, 2, 2)),
            dma((2, 2, 8)),
            dma((2, 2, 8)),
            dma((2,)),
        ],
        compiler_params=pltpu.CompilerParams(
            collective_id=0, has_side_effects=True, vmem_limit_bytes=56 * 2**20
        ),
        cost_estimate=pl.CostEstimate(
            flops=5 * 10**9, bytes_accessed=25 * 2**20, transcendentals=10**6
        ),
    )(
        hidden_in,
        norm_gain.reshape(T, 1, CHUNK),
        query_weight_base.reshape(32, 256, CHUNK),
        w_key.T,
        w_value.T,
        output_weight_base,
        kv_cache,
        cache_lengths,
        freq,
        adapter_shards,
        shard_order.reshape(1, 128),
    )


def solution(mesh):
    return jax.shard_map(
        body,
        mesh=mesh,
        in_specs=(
            P("rollout", None),
            P(),
            P(None, "tensor"),
            P(None, "tensor"),
            P(None, "tensor"),
            P("tensor", None),
            P(("rollout", "tensor"), None, None, None),
            P(("rollout", "tensor")),
            P(("rollout", "tensor"), None),
            P(),
        ),
        out_specs=P(None, "rollout", "tensor"),
        check_vma=False,
    )
```

```python
import jax
import jax.numpy as jnp
import numpy as np
from jax import lax
from jax.experimental import pallas as pl
from jax.experimental.pallas import tpu as pltpu
from jax.sharding import PartitionSpec as P

D = 8192
HEADS = 64
KV_HEADS = 8
HEAD_DIM = 128
RANK = 64
STEPS = 2
CAP = 256
T = 16
R = 8
CHUNK = D // T

low_rank_scale = 2.0
norm_epsilon = 1e-05
rope_theta = 500000.0
score_scale = 1.0 / np.sqrt(np.float32(HEAD_DIM))

f32 = jnp.float32
bf16 = jnp.bfloat16
MESH = pl.DeviceIdType.MESH


def mm(a, b):
    return jnp.dot(a, b, preferred_element_type=f32)


def mm_t(a, b):
    return lax.dot_general(a, b, (((1,), (1,)), ((), ())), preferred_element_type=f32)


def lanes(shape):
    return lax.broadcasted_iota(jnp.int32, shape, len(shape) - 1)


def swap_halves(x):
    return pltpu.roll(x, 64, len(x.shape) - 1)


def spread_pairs(x, ref):
    low = lanes(x.shape) < 64
    rows = x.shape[0]
    ref[pl.ds(0, rows, stride=2), :] = jnp.where(low, x, 0.0)
    ref[pl.ds(1, rows, stride=2), :] = jnp.where(low, swap_halves(x), 0.0)


def pack_rank(t):
    return t[0:32] + swap_halves(t[32:64])


def unpack_split(total):
    high = total.astype(bf16).astype(f32)
    rest = total - high
    low = lanes(total.shape) < 64
    top = jnp.where(low, high, swap_halves(rest))
    bottom = jnp.where(low, swap_halves(high), rest)
    return jnp.concatenate([top, bottom], axis=0).astype(bf16)


def kernel(
    hid, gain, wq, wk_t, wv_t, wo, kv, lens, freq, piece, order,
    out,
    WQ, WKV, WO, KV, HF, ST, SG, NB,
    PF, CP, A1R, A2S, A2R, XF, OF, AE, AQ, BQ, BO, AOS, AOR, AOE, AO,
    Q32, QS, QR, QX, KN, VN, AF, AM, AR, AT, TOS, TOR, RSS, RB, OUTF, SQS, SQR, DI, KEYS, VALS,
    lsem, wosem, a1sem, a2sem, a3dsem, a3fsem, aosem, qsem, asem, tosem, rssem, agdsem, agfsem, sqsem,
):
    me = lax.axis_index("tensor")
    ro = lax.axis_index("rollout")
    core = lax.rem(me, 2)
    chip = me // 2
    sib = me + 1 - 2 * core

    def wait(ref, sem):
        pltpu.make_async_copy(ref, ref, sem).wait()

    def tensor_copy(src, dst, send, recv, peer):
        return pltpu.make_async_remote_copy(
            src_ref=src, dst_ref=dst, send_sem=send, recv_sem=recv,
            device_id={"tensor": peer}, device_id_type=MESH,
        )

    def loop(lo, hi, body):
        def step(k, carry):
            body(k)
            return carry
        lax.fori_loop(lo, hi, step, 0)

    barrier = pltpu.get_barrier_semaphore()
    loop(1, T, lambda k: pl.semaphore_signal(
        barrier, inc=1, device_id={"tensor": lax.rem(me + k, T)}, device_id_type=MESH))
    loop(1, R, lambda k: pl.semaphore_signal(
        barrier, inc=1, device_id={"rollout": lax.rem(ro + k, R)}, device_id_type=MESH))

    for j in range(8):
        pltpu.make_async_copy(
            wq.at[pl.ds(4 * j, 4)], WQ.at[pl.ds(4 * j, 4)], lsem.at[0]).start()
    pltpu.make_async_copy(wk_t, WKV.at[pl.ds(0, 64), :], lsem.at[16]).start()
    pltpu.make_async_copy(wv_t, WKV.at[pl.ds(64, 64), :], lsem.at[17]).start()
    def wo_columns(q, parity):
        return wo.at[:, pl.ds(pl.multiple_of((2 * q + parity) * CHUNK, CHUNK), CHUNK)]

    wo_rows = pl.ds(pl.multiple_of(core * CHUNK, CHUNK), CHUNK)
    loop(0, 8, lambda q: pltpu.make_async_copy(
        wo_columns(q, core), WO.at[q, wo_rows, :], lsem.at[18]).start())

    order_row = order[...]
    mine = jnp.sum(
        jnp.where(lanes((1, 128)) == ro * T + me, order_row, 0), axis=1, keepdims=True)
    is_up = jnp.broadcast_to((mine >> 5) & 1, (128, 128))
    row = lax.broadcasted_iota(jnp.int32, (128, 128), 0)
    up_row = 64 * ((row >> 2) & 1) + 4 * (row >> 3) + (row & 3)
    wanted = jnp.where(is_up == 1, up_row, row)
    pick = jnp.where(lanes((128, 128)) == wanted, 1.0, 0.0).astype(bf16)
    flat = piece[...].astype(f32)
    for r in range(128):
        PF[r:r + 1, :] = flat[:, 128 * r:128 * r + 128]
    CP[...] = mm(pick, PF[...].astype(bf16)).astype(bf16)
    A1R[ro] = CP[...]
    place = jnp.where(row == jnp.broadcast_to(order_row, (128, 128)), 1.0, 0.0).astype(bf16)

    pl.semaphore_wait(barrier, T - 1 + R - 1)

    def send_piece(peer, sem):
        pltpu.make_async_remote_copy(
            src_ref=CP, dst_ref=A1R.at[ro], send_sem=a1sem.at[0, sem],
            recv_sem=a1sem.at[1, sem], device_id={"rollout": peer}, device_id_type=MESH).start()

    loop(1, 4, lambda k: send_piece(lax.rem(ro + 2 * k, R), 0))
    other = ro + 1 - 2 * lax.rem(ro, 2)
    loop(0, 4, lambda k: send_piece(lax.rem(other + 2 * k, R), 1))
    for i in range(4):
        for g in range(KV_HEADS):
            pltpu.make_async_copy(
                kv.at[i, :, :, pl.ds(HEAD_DIM * g, HEAD_DIM)], KV.at[i, g], lsem.at[19]).start()
    loop(0, 8, lambda q: tensor_copy(
        wo_columns(q, 1 - core), WO.at[q, wo_rows, :], wosem.at[0], wosem.at[1], sib).start())

    def permute_hidden(j):
        for c in range(4):
            at = pl.multiple_of(CHUNK * j + 128 * c, 128)
            HF[c] = hid[:, pl.ds(at, 128)].astype(f32)
        for c in range(4):
            for i in range(4):
                ST[j, 16 * i:16 * i + 16, 128 * c:128 * c + 128] = (
                    HF[c, pl.ds(i, 16, stride=4), :].astype(bf16))
    loop(0, T, permute_hidden)

    Q32[320:512, :] = jnp.zeros((192, 128), f32)

    def square_sum(j, total):
        x = ST[j].astype(f32)
        x = x * x
        return total + (x[:, 0:128] + x[:, 128:256]) + (x[:, 256:384] + x[:, 384:512])

    def normalize(total):
        inv = lax.rsqrt(jnp.sum(total, axis=1, keepdims=True) * (1.0 / D) + norm_epsilon)
        def body(j):
            NB[j] = (ST[j].astype(f32) * inv * gain[j]).astype(bf16)
        loop(0, T, body)

    zero_total = jnp.zeros((64, 128), f32)
    zero_query = jnp.zeros((64, CHUNK), f32)
    normalize(lax.fori_loop(0, T, square_sum, zero_total))

    def project_kv(j, new):
        columns = pl.ds(pl.multiple_of(CHUNK * j, CHUNK), CHUNK)
        return new + mm_t(NB[j], WKV[:, columns])

    for half in range(2):
        z = lax.rem(ro + half, 2)
        wait(A1R.at[pl.ds(0, 3 + half)], a1sem.at[1, half])
        for y in range(4):
            held = A1R[2 * y + z].astype(f32).reshape(T, 8, 128)
            OF[:, 8 * y:8 * y + 8, :] = held
        A2S[half] = OF[...].astype(bf16)
        loop(1, T, lambda k: tensor_copy(
            A2S.at[half, lax.rem(me + k, T)], A2R.at[z, me], a2sem.at[half, 0],
            a2sem.at[half, 1], lax.rem(me + k, T)).start())
        A2R[z, me] = A2S[half, me]

    wait(WKV.at[pl.ds(0, 64), :], lsem.at[16])
    wait(WKV.at[pl.ds(64, 64), :], lsem.at[17])
    new = lax.fori_loop(0, T, project_kv, zero_total, unroll=4)
    wait(WQ, lsem.at[0])
    for half in range(2):
        wait(A2R.at[0, pl.ds(0, T - 1)], a2sem.at[half, 1])

    for z in range(2):
        arrived = A2R[z].astype(f32).reshape(T, 4, 8, 128)
        for y in range(4):
            r = 2 * y + z
            XF[128 * r:128 * r + 128, :] = arrived[:, y].reshape(128, 128)
    FL = AOE
    for s in range(8):
        FL[pl.ds(s, 128, stride=8), :] = mm(place, XF[pl.ds(s, 128, stride=8), :].astype(bf16))
    spread_pairs(FL[0:256, :], AE)
    AQ[me] = (AE[0:256, :] + swap_halves(AE[256:512, :])).astype(bf16)
    loop(1, 8, lambda k: tensor_copy(
        AQ.at[me], AQ.at[me], a3dsem.at[0, k], a3dsem.at[1, k], lax.rem(me + 2 * k, T)).start())
    tensor_copy(AQ.at[me], AQ.at[me], a3fsem.at[0, 0], a3fsem.at[1, 0], sib).start()
    for c in range(4):
        up = (low_rank_scale * FL[pl.ds(256 + c, 64, stride=4), :]).astype(bf16)
        none = jnp.zeros_like(up)
        BQ[0, 0:64, 128 * c:128 * c + 128] = up
        BQ[0, 64:128, 128 * c:128 * c + 128] = none
        BQ[1, 0:64, 128 * c:128 * c + 128] = none
        BQ[1, 64:128, 128 * c:128 * c + 128] = up
        up = FL[pl.ds(768 + c, 64, stride=4), :].astype(bf16)
        BO[0:64, 128 * c:128 * c + 128] = up
        BO[64:128, 128 * c:128 * c + 128] = up
    AOS[...] = FL[512:768, :].astype(bf16).reshape(8, 32, 128)

    def merge(j):
        strip = pl.ds(pl.multiple_of(16 * j, 16), 16)
        for half in range(2):
            blocks = pl.ds(16 * half, 16)
            for n in range(2):
                columns = slice(256 * n, 256 * n + 256)
                change = mm(AQ[j], BQ[half, :, columns]).reshape(16, 16, 256)
                WQ[blocks, strip, columns] = (
                    WQ[blocks, strip, columns].astype(f32) + change).astype(bf16)

    def own_side(k):
        return lax.rem(me + T - 2 * k, T)

    def other_side(k):
        return lax.rem(sib + T - 2 * k, T)

    def pass_on_strips(k):
        j = own_side(k)
        wait(AQ.at[j], a3dsem.at[1, k])
        tensor_copy(AQ.at[j], AQ.at[j], a3fsem.at[0, k], a3fsem.at[1, k], sib).start()

    wait(KV, lsem.at[19])

    def part_cache(n):
        i, g = n // KV_HEADS, lax.rem(n, KV_HEADS)
        DI[...] = KV[i, g].reshape(2 * CAP, HEAD_DIM).astype(f32)
        KEYS[i, g] = DI[pl.ds(0, CAP, stride=2), :].astype(bf16)
        VALS[i, g] = DI[pl.ds(1, CAP, stride=2), :].astype(bf16)

    merge(me)
    loop(0, 4 * KV_HEADS, part_cache)
    loop(1, 8, pass_on_strips)
    loop(1, 8, lambda k: merge(own_side(k)))
    loop(0, 8, lambda k: wait(AQ.at[other_side(k)], a3fsem.at[1, k]))
    loop(0, 8, lambda k: merge(other_side(k)))

    low_half = lanes((8, 128)) < 64
    sub = lax.broadcasted_iota(jnp.int32, (8, 128), 0) & 3
    lengths = jnp.zeros((8, 128), jnp.int32)
    for i in range(4):
        lengths = jnp.where(sub == i, lens[i], lengths)
    wide = lanes((64, CAP))

    for s in range(STEPS):
        def project(j, q):
            return q + mm(NB[j], WQ[pl.ds(2 * j, 2)].reshape(CHUNK, CHUNK))

        if s == 0:
            q = lax.fori_loop(0, T, project, zero_query, unroll=4)
        for h in range(4):
            Q32[64 * h:64 * h + 64, :] = q[:, 128 * h:128 * h + 128]
        Q32[256:320, :] = new
        for t in range(T):
            QS[s, t] = Q32[pl.ds(t, 32, stride=16), :].astype(bf16)
        loop(1, T, lambda k: tensor_copy(
            QS.at[s, lax.rem(me + k, T)], QR.at[s, me], qsem.at[s, 0], qsem.at[s, 1],
            lax.rem(me + k, T)).start())
        QR[s, me] = QS[s, me]
        if s == 0:
            loop(1, T, lambda k: tensor_copy(
                AOS.at[lax.rem(me + k, T) // 2], AOR.at[me], aosem.at[0], aosem.at[1],
                lax.rem(me + k, T)).start())
            AOR[me] = AOS[chip]

        angles = (lengths + s).astype(f32) * freq[...]
        cosine = jnp.cos(angles)
        sine = jnp.where(low_half, -jnp.sin(angles), jnp.sin(angles))

        wait(QR.at[s, pl.ds(0, T - 1)], qsem.at[s, 1])
        got = QR[s].astype(f32)
        heads = got[:, 0:16].reshape(T, 2, 8, 128)
        heads = heads * cosine + swap_halves(heads) * sine
        QX[...] = heads.astype(bf16).astype(f32).reshape(256, 128)
        fresh = got[:, 16:24].reshape(8, 2, 8, 128)
        even, odd = fresh[:, 0], fresh[:, 1]
        low = lanes(even.shape) < 64
        key = jnp.where(low, even, swap_halves(odd))
        key = key * cosine + swap_halves(key) * sine
        KN[s] = key.astype(bf16).astype(f32).reshape(64, 128)
        VN[s] = jnp.where(low, swap_halves(even), odd).reshape(64, 128)


        def attend(i):
            queries = [QX[pl.ds(32 * g + i, 8, stride=4), :] for g in range(KV_HEADS)]
            scores = jnp.concatenate(
                [mm_t(queries[g].astype(bf16), KEYS[i, g])
                 for g in range(KV_HEADS)], axis=0) * score_scale
            scores = jnp.where(wide < lens[i], scores, -1e30)
            rows = jnp.concatenate(queries, axis=0)
            largest = jnp.max(scores, axis=1, keepdims=True)
            news, values = [], []
            for n in range(s + 1):
                k = KN[n, pl.ds(i, 8, stride=8), :]
                v = VN[n, pl.ds(i, 8, stride=8), :]
                k = jnp.broadcast_to(k[:, None, :], (8, 8, 128)).reshape(64, 128)
                values.append(jnp.broadcast_to(v[:, None, :], (8, 8, 128)).reshape(64, 128))
                news.append(jnp.sum(rows * k, axis=1, keepdims=True) * score_scale)
                largest = jnp.maximum(largest, news[-1])
            expo = jnp.exp(scores - largest)
            news = [jnp.exp(x - largest) for x in news]
            total = jnp.sum(expo, axis=1, keepdims=True)
            for x in news:
                total = total + x
            share = 1.0 / total
            weights = (expo * share).astype(bf16)
            result = jnp.concatenate(
                [mm(weights[8 * g:8 * g + 8], VALS[i, g])
                 for g in range(KV_HEADS)], axis=0)
            for x, v in zip(news, values):
                result = result + (x * share).astype(bf16).astype(f32) * v
            AF[pl.ds(i, 64, stride=4), :] = result

        for i in range(4):
            attend(i)
        AM[s] = AF[...].astype(bf16).reshape(8, 32, 128)
        loop(1, T, lambda k: tensor_copy(
            AM.at[s, lax.rem(me + k, T) // 2], AR.at[s, me], asem.at[s, 0], asem.at[s, 1],
            lax.rem(me + k, T)).start())
        AR[s, me] = AM[s, chip]
        if s == 0:
            wait(AOR.at[pl.ds(0, T - 1)], aosem.at[1])
            blocks = AOR[...].astype(f32).reshape(T, 4, 8, 128)
            for b in range(4):
                XF[128 * b:128 * b + 128, :] = blocks[:, b].reshape(128, 128)
            spread_pairs(XF[0:512, :], AOE)
            AO[...] = AOE[...].astype(bf16)
        wait(AR.at[s, pl.ds(0, T - 1)], asem.at[s, 1])
        XF[0:512, :] = AR[s].astype(f32).reshape(512, 128)
        for h in range(8):
            for i in range(4):
                AT[16 * i:16 * i + 16, 128 * h:128 * h + 128] = (
                    XF[pl.ds(4 * h + i, 16, stride=32), :].astype(bf16))

        attended = AT[...]
        if s == 0:
            wait(WO.at[:, pl.ds(0, CHUNK), :], lsem.at[18])
            wait(WO.at[:, pl.ds(0, CHUNK), :], wosem.at[1])

        halves = [slice(256 * half, 256 * half + 256) for half in range(2)]

        def send_parts(half):
            def part(k):
                q = lax.rem(chip + k, 8)
                RSS[s, half, q] = mm(AT[...], WO[q, :, halves[half]]).astype(bf16)
                tensor_copy(
                    RSS.at[s, half, q], RB.at[s, half, chip], rssem.at[s, half, 0],
                    rssem.at[s, half, 1], 2 * q + core).start()
            loop(1, 8, part)

        send_parts(0)
        t = mm(attended, AO[...])
        TOS[s] = pack_rank(t).astype(bf16)
        loop(1, 8, lambda k: tensor_copy(
            TOS.at[s], TOR.at[s, chip], tosem.at[s, 0], tosem.at[s, 1],
            lax.rem(me + 2 * k, T)).start())
        TOR[s, chip] = TOS[s]
        send_parts(1)
        bases = []
        for half in range(2):
            own = ST[me, :, halves[half]] if s == 0 else SG[me, half]
            bases.append(mm(attended, WO[chip, :, halves[half]]) + own.astype(f32))
        wait(TOR.at[s, pl.ds(0, 7)], tosem.at[s, 1])
        rank = unpack_split(jnp.sum(TOR[s].astype(f32), axis=0))
        parts = []
        for half in range(2):
            y = bases[half] + low_rank_scale * mm(rank, BO[:, halves[half]])
            RB[s, half, chip] = jnp.zeros((64, CHUNK // 2), bf16)
            wait(RB.at[s, half, pl.ds(0, 7)], rssem.at[s, half, 1])
            for q in range(8):
                y = y + RB[s, half, q].astype(f32)
            y = y.astype(bf16)
            parts.append(y)
            if s + 1 < STEPS:
                SG[me, half] = y
                if half == 1:
                    squares = [x.astype(f32) * x.astype(f32) for x in parts]
                    squares = (squares[0][:, 0:128] + squares[0][:, 128:256]) + (
                        squares[1][:, 0:128] + squares[1][:, 128:256])
                    SQS[...] = jnp.zeros_like(SQS)
                    SQS[0:1, 0:64] = jnp.sum(squares.T, axis=0, keepdims=True)
                    loop(1, T, lambda k: tensor_copy(
                        SQS, SQR.at[me], sqsem.at[0], sqsem.at[1], lax.rem(me + k, T)).start())
                loop(1, 8, lambda k: tensor_copy(
                    SG.at[me, half], SG.at[me, half], agdsem.at[0, half, k],
                    agdsem.at[1, half, k], lax.rem(me + 2 * k, T)).start())
                tensor_copy(
                    SG.at[me, half], SG.at[me, half], agfsem.at[0, half, 0],
                    agfsem.at[1, half, 0], sib).start()
        y = jnp.concatenate(parts, axis=1)
        yf = y.astype(f32)
        for c in range(4):
            for i in range(4):
                OUTF[c, pl.ds(i, 16, stride=4), :] = yf[16 * i:16 * i + 16, 128 * c:128 * c + 128]
        for c in range(4):
            out[s, :, 128 * c:128 * c + 128] = OUTF[c].astype(bf16)

        if s + 1 < STEPS:
            def pass_on_stream(half):
                def pass_on(k):
                    j = own_side(k)
                    wait(SG.at[j, half], agdsem.at[1, half, k])
                    tensor_copy(
                        SG.at[j, half], SG.at[j, half], agfsem.at[0, half, k],
                        agfsem.at[1, half, k], sib).start()
                loop(1, 8, pass_on)

            pass_on_stream(0)
            SQR[me] = SQS[...]
            wait(SQR.at[pl.ds(0, T - 1)], sqsem.at[1])
            total = jnp.sum(SQR[...], axis=0)[0:1]
            total = jnp.broadcast_to(total, (128, 128)).T[0:64, 0:1]
            inv = lax.rsqrt(total * (1.0 / D) + norm_epsilon)

            def take(j, half, carry):
                q, new = carry
                x = (SG[j, half].astype(f32) * inv * gain[j, :, halves[half]]).astype(bf16)
                columns = pl.ds(pl.multiple_of(CHUNK * j + 256 * half, 256), 256)
                return q + mm(x, WQ[2 * j + half]), new + mm_t(x, WKV[:, columns])

            carry = (zero_query, zero_total)
            for half in range(2):
                if half == 1:
                    pass_on_stream(1)
                carry = lax.fori_loop(
                    0, 8, lambda k, c: take(own_side(k), half, c), carry, unroll=4)
                loop(0, 8, lambda k: wait(SG.at[other_side(k), half], agfsem.at[1, half, k]))
                carry = lax.fori_loop(
                    0, 8, lambda k, c: take(other_side(k), half, c), carry, unroll=4)
            q, new = carry

    wait(A1R.at[pl.ds(0, 3)], a1sem.at[0, 0])
    wait(A1R.at[pl.ds(0, 4)], a1sem.at[0, 1])
    wait(WO.at[:, pl.ds(0, CHUNK), :], wosem.at[0])
    for half in range(2):
        wait(A2R.at[0, pl.ds(0, T - 1)], a2sem.at[half, 0])
    loop(1, 8, lambda k: wait(AQ.at[me], a3dsem.at[0, k]))
    loop(0, 8, lambda k: wait(AQ.at[me], a3fsem.at[0, k]))
    wait(AOR.at[pl.ds(0, T - 1)], aosem.at[0])
    for s in range(STEPS):
        wait(QR.at[s, pl.ds(0, T - 1)], qsem.at[s, 0])
        wait(AR.at[s, pl.ds(0, T - 1)], asem.at[s, 0])
        wait(TOR.at[s, pl.ds(0, 7)], tosem.at[s, 0])
        for half in range(2):
            wait(RB.at[s, half, pl.ds(0, 7)], rssem.at[s, half, 0])
    for half in range(2):
        loop(1, 8, lambda k: wait(SG.at[me, half], agdsem.at[0, half, k]))
        loop(0, 8, lambda k: wait(SG.at[me, half], agfsem.at[0, half, k]))
    wait(SQR.at[pl.ds(0, T - 1)], sqsem.at[0])


def body(
    hidden_in,
    norm_gain,
    query_weight_base,
    w_key,
    w_value,
    output_weight_base,
    kv_cache,
    cache_lengths,
    adapter_shards,
    shard_order,
):
    half_dim = HEAD_DIM // 2
    exponent = np.arange(half_dim, dtype=np.float32) * np.float32(2.0 / HEAD_DIM)
    frequency = np.float32(rope_theta) ** (-exponent)
    freq = jnp.asarray(np.concatenate([frequency, frequency]).reshape(1, HEAD_DIM))
    vmem = pl.BlockSpec(memory_space=pltpu.VMEM)
    smem = pl.BlockSpec(memory_space=pltpu.SMEM)
    hbm = pl.BlockSpec(memory_space=pl.ANY)
    V = pltpu.VMEM
    dma = pltpu.SemaphoreType.DMA
    return pl.pallas_call(
        kernel,
        out_shape=jax.ShapeDtypeStruct((STEPS, 64, CHUNK), bf16),
        in_specs=[vmem, vmem, hbm, hbm, hbm, hbm, hbm, smem, vmem, vmem, vmem],
        out_specs=vmem,
        scratch_shapes=[
            V((32, 256, CHUNK), bf16),
            V((128, D), bf16),
            V((8, 2 * CHUNK, CHUNK), bf16),
            V((4, KV_HEADS, CAP, 2, HEAD_DIM), bf16),
            V((4, 64, 128), f32),
            V((T, 64, CHUNK), bf16),
            V((T, 2, 64, CHUNK // 2), bf16),
            V((T, 64, CHUNK), bf16),
            V((128, 128), f32),
            V((128, 128), bf16),
            V((R, 128, 128), bf16),
            V((2, T, 32, 128), bf16),
            V((2, T, 32, 128), bf16),
            V((1024, 128), f32),
            V((T, 32, 128), f32),
            V((512, 128), f32),
            V((T, 256, 128), bf16),
            V((2, 128, CHUNK), bf16),
            V((128, CHUNK), bf16),
            V((8, 32, 128), bf16),
            V((T, 32, 128), bf16),
            V((1024, 128), f32),
            V((1024, 128), bf16),
            V((512, 128), f32),
            V((STEPS, T, 32, 128), bf16),
            V((STEPS, T, 32, 128), bf16),
            V((256, 128), f32),
            V((STEPS, 64, 128), f32),
            V((STEPS, 64, 128), f32),
            V((256, 128), f32),
            V((STEPS, 8, 32, 128), bf16),
            V((STEPS, T, 32, 128), bf16),
            V((64, 2 * CHUNK), bf16),
            V((STEPS, 32, 128), bf16),
            V((STEPS, 8, 32, 128), bf16),
            V((STEPS, 2, 8, 64, CHUNK // 2), bf16),
            V((STEPS, 2, 8, 64, CHUNK // 2), bf16),
            V((4, 64, 128), f32),
            V((8, 128), f32),
            V((T, 8, 128), f32),
            V((2 * CAP, HEAD_DIM), f32),
            V((4, KV_HEADS, CAP, HEAD_DIM), bf16),
            V((4, KV_HEADS, CAP, HEAD_DIM), bf16),
            dma((20,)),
            dma((2,)),
            dma((2, 2)),
            dma((2, 2)),
            dma((2, 8)),
            dma((2, 8)),
            dma((2,)),
            dma((STEPS, 2)),
            dma((STEPS, 2)),
            dma((STEPS, 2)),
            dma((STEPS, 2, 2)),
            dma((2, 2, 8)),
            dma((2, 2, 8)),
            dma((2,)),
        ],
        compiler_params=pltpu.CompilerParams(
            collective_id=0, has_side_effects=True, vmem_limit_bytes=56 * 2**20
        ),
        cost_estimate=pl.CostEstimate(
            flops=5 * 10**9, bytes_accessed=25 * 2**20, transcendentals=10**6
        ),
    )(
        hidden_in,
        norm_gain.reshape(T, 1, CHUNK),
        query_weight_base.reshape(32, 256, CHUNK),
        w_key.T,
        w_value.T,
        output_weight_base,
        kv_cache,
        cache_lengths,
        freq,
        adapter_shards,
        shard_order.reshape(1, 128),
    )


def solution(mesh):
    return jax.shard_map(
        body,
        mesh=mesh,
        in_specs=(
            P("rollout", None),
            P(),
            P(None, "tensor"),
            P(None, "tensor"),
            P(None, "tensor"),
            P("tensor", None),
            P(("rollout", "tensor"), None, None, None),
            P(("rollout", "tensor")),
            P(("rollout", "tensor"), None),
            P(),
        ),
        out_specs=P(None, "rollout", "tensor"),
        check_vma=False,
    )
```

```python
import jax
import jax.numpy as jnp
import numpy as np
from jax import lax
from jax.experimental import pallas as pl
from jax.experimental.pallas import tpu as pltpu
from jax.sharding import PartitionSpec as P

D = 8192
HEADS = 64
KV_HEADS = 8
HEAD_DIM = 128
RANK = 64
STEPS = 2
CAP = 256
T = 16
R = 8
CHUNK = D // T

low_rank_scale = 2.0
norm_epsilon = 1e-05
rope_theta = 500000.0
score_scale = 1.0 / np.sqrt(np.float32(HEAD_DIM))

f32 = jnp.float32
bf16 = jnp.bfloat16
MESH = pl.DeviceIdType.MESH


def mm(a, b):
    return jnp.dot(a, b, preferred_element_type=f32)


def mm_t(a, b):
    return lax.dot_general(a, b, (((1,), (1,)), ((), ())), preferred_element_type=f32)


def lanes(shape):
    return lax.broadcasted_iota(jnp.int32, shape, len(shape) - 1)


def swap_halves(x):
    return pltpu.roll(x, 64, len(x.shape) - 1)


def spread_pairs(x, ref):
    low = lanes(x.shape) < 64
    rows = x.shape[0]
    ref[pl.ds(0, rows, stride=2), :] = jnp.where(low, x, 0.0)
    ref[pl.ds(1, rows, stride=2), :] = jnp.where(low, swap_halves(x), 0.0)


def pack_rank(t):
    return t[0:32] + swap_halves(t[32:64])


def unpack_split(total):
    high = total.astype(bf16).astype(f32)
    rest = total - high
    low = lanes(total.shape) < 64
    top = jnp.where(low, high, swap_halves(rest))
    bottom = jnp.where(low, swap_halves(high), rest)
    return jnp.concatenate([top, bottom], axis=0).astype(bf16)


def kernel(
    hid, gain, wq, wk_t, wv_t, wo, kv, lens, freq, piece, order,
    out,
    WQ, WKV, WO, KV, HF, ST, SG, NB,
    PF, CP, A1R, A2S, A2R, XF, OF, AE, AQ, BQ, BO, AOS, AOR, AOE, AO,
    Q32, QS, QR, QX, KN, VN, AF, AM, AR, AT, TOS, TOR, RSS, RB, OUTF, SQS, SQR, DI, KEYS, VALS,
    lsem, wosem, a1sem, a2sem, a3dsem, a3fsem, aosem, qsem, asem, tosem, rssem, agdsem, agfsem, sqsem,
):
    me = lax.axis_index("tensor")
    ro = lax.axis_index("rollout")
    core = lax.rem(me, 2)
    chip = me // 2
    sib = me + 1 - 2 * core

    def wait(ref, sem):
        pltpu.make_async_copy(ref, ref, sem).wait()

    def tensor_copy(src, dst, send, recv, peer):
        return pltpu.make_async_remote_copy(
            src_ref=src, dst_ref=dst, send_sem=send, recv_sem=recv,
            device_id={"tensor": peer}, device_id_type=MESH,
        )

    def loop(lo, hi, body):
        def step(k, carry):
            body(k)
            return carry
        lax.fori_loop(lo, hi, step, 0)

    barrier = pltpu.get_barrier_semaphore()
    loop(1, T, lambda k: pl.semaphore_signal(
        barrier, inc=1, device_id={"tensor": lax.rem(me + k, T)}, device_id_type=MESH))
    loop(1, R, lambda k: pl.semaphore_signal(
        barrier, inc=1, device_id={"rollout": lax.rem(ro + k, R)}, device_id_type=MESH))

    for j in range(8):
        pltpu.make_async_copy(
            wq.at[pl.ds(4 * j, 4)], WQ.at[pl.ds(4 * j, 4)], lsem.at[0]).start()
    pltpu.make_async_copy(wk_t, WKV.at[pl.ds(0, 64), :], lsem.at[16]).start()
    pltpu.make_async_copy(wv_t, WKV.at[pl.ds(64, 64), :], lsem.at[17]).start()
    for i in range(4):
        for g in range(KV_HEADS):
            pltpu.make_async_copy(
                kv.at[i, :, :, pl.ds(HEAD_DIM * g, HEAD_DIM)], KV.at[i, g], lsem.at[19]).start()

    def wo_columns(q, parity):
        return wo.at[:, pl.ds(pl.multiple_of((2 * q + parity) * CHUNK, CHUNK), CHUNK)]

    wo_rows = pl.ds(pl.multiple_of(core * CHUNK, CHUNK), CHUNK)
    loop(0, 8, lambda q: pltpu.make_async_copy(
        wo_columns(q, core), WO.at[q, wo_rows, :], lsem.at[18]).start())

    order_row = order[...]
    mine = jnp.sum(
        jnp.where(lanes((1, 128)) == ro * T + me, order_row, 0), axis=1, keepdims=True)
    is_up = jnp.broadcast_to((mine >> 5) & 1, (128, 128))
    row = lax.broadcasted_iota(jnp.int32, (128, 128), 0)
    up_row = 64 * ((row >> 2) & 1) + 4 * (row >> 3) + (row & 3)
    wanted = jnp.where(is_up == 1, up_row, row)
    pick = jnp.where(lanes((128, 128)) == wanted, 1.0, 0.0).astype(bf16)
    flat = piece[...].astype(f32)
    for r in range(128):
        PF[r:r + 1, :] = flat[:, 128 * r:128 * r + 128]
    CP[...] = mm(pick, PF[...].astype(bf16)).astype(bf16)
    A1R[ro] = CP[...]
    place = jnp.where(row == jnp.broadcast_to(order_row, (128, 128)), 1.0, 0.0).astype(bf16)

    pl.semaphore_wait(barrier, T - 1 + R - 1)

    def send_piece(peer, sem):
        pltpu.make_async_remote_copy(
            src_ref=CP, dst_ref=A1R.at[ro], send_sem=a1sem.at[0, sem],
            recv_sem=a1sem.at[1, sem], device_id={"rollout": peer}, device_id_type=MESH).start()

    loop(1, 4, lambda k: send_piece(lax.rem(ro + 2 * k, R), 0))
    other = ro + 1 - 2 * lax.rem(ro, 2)
    loop(0, 4, lambda k: send_piece(lax.rem(other + 2 * k, R), 1))
    loop(0, 8, lambda q: tensor_copy(
        wo_columns(q, 1 - core), WO.at[q, wo_rows, :], wosem.at[0], wosem.at[1], sib).start())

    def permute_hidden(j):
        for c in range(4):
            at = pl.multiple_of(CHUNK * j + 128 * c, 128)
            HF[c] = hid[:, pl.ds(at, 128)].astype(f32)
        for c in range(4):
            for i in range(4):
                ST[j, 16 * i:16 * i + 16, 128 * c:128 * c + 128] = (
                    HF[c, pl.ds(i, 16, stride=4), :].astype(bf16))
    loop(0, T, permute_hidden)

    Q32[320:512, :] = jnp.zeros((192, 128), f32)

    def square_sum(j, total):
        x = ST[j].astype(f32)
        x = x * x
        return total + (x[:, 0:128] + x[:, 128:256]) + (x[:, 256:384] + x[:, 384:512])

    def normalize(total):
        inv = lax.rsqrt(jnp.sum(total, axis=1, keepdims=True) * (1.0 / D) + norm_epsilon)
        def body(j):
            NB[j] = (ST[j].astype(f32) * inv * gain[j]).astype(bf16)
        loop(0, T, body)

    zero_total = jnp.zeros((64, 128), f32)
    zero_query = jnp.zeros((64, CHUNK), f32)
    normalize(lax.fori_loop(0, T, square_sum, zero_total))

    def project_kv(j, new):
        columns = pl.ds(pl.multiple_of(CHUNK * j, CHUNK), CHUNK)
        return new + mm_t(NB[j], WKV[:, columns])

    for half in range(2):
        z = lax.rem(ro + half, 2)
        wait(A1R.at[pl.ds(0, 3 + half)], a1sem.at[1, half])
        for y in range(4):
            held = A1R[2 * y + z].astype(f32).reshape(T, 8, 128)
            OF[:, 8 * y:8 * y + 8, :] = held
        A2S[half] = OF[...].astype(bf16)
        loop(1, T, lambda k: tensor_copy(
            A2S.at[half, lax.rem(me + k, T)], A2R.at[z, me], a2sem.at[half, 0],
            a2sem.at[half, 1], lax.rem(me + k, T)).start())
        A2R[z, me] = A2S[half, me]

    wait(WKV.at[pl.ds(0, 64), :], lsem.at[16])
    wait(WKV.at[pl.ds(64, 64), :], lsem.at[17])
    new = lax.fori_loop(0, T, project_kv, zero_total, unroll=4)
    wait(WQ, lsem.at[0])
    for half in range(2):
        wait(A2R.at[0, pl.ds(0, T - 1)], a2sem.at[half, 1])

    for z in range(2):
        arrived = A2R[z].astype(f32).reshape(T, 4, 8, 128)
        for y in range(4):
            r = 2 * y + z
            XF[128 * r:128 * r + 128, :] = arrived[:, y].reshape(128, 128)
    FL = AOE
    for s in range(8):
        FL[pl.ds(s, 128, stride=8), :] = mm(place, XF[pl.ds(s, 128, stride=8), :].astype(bf16))
    spread_pairs(FL[0:256, :], AE)
    AQ[me] = (AE[0:256, :] + swap_halves(AE[256:512, :])).astype(bf16)
    loop(1, 8, lambda k: tensor_copy(
        AQ.at[me], AQ.at[me], a3dsem.at[0, k], a3dsem.at[1, k], lax.rem(me + 2 * k, T)).start())
    tensor_copy(AQ.at[me], AQ.at[me], a3fsem.at[0, 0], a3fsem.at[1, 0], sib).start()
    for c in range(4):
        up = (low_rank_scale * FL[pl.ds(256 + c, 64, stride=4), :]).astype(bf16)
        none = jnp.zeros_like(up)
        BQ[0, 0:64, 128 * c:128 * c + 128] = up
        BQ[0, 64:128, 128 * c:128 * c + 128] = none
        BQ[1, 0:64, 128 * c:128 * c + 128] = none
        BQ[1, 64:128, 128 * c:128 * c + 128] = up
        up = FL[pl.ds(768 + c, 64, stride=4), :].astype(bf16)
        BO[0:64, 128 * c:128 * c + 128] = up
        BO[64:128, 128 * c:128 * c + 128] = up
    AOS[...] = FL[512:768, :].astype(bf16).reshape(8, 32, 128)

    def merge(j):
        strip = pl.ds(pl.multiple_of(16 * j, 16), 16)
        for half in range(2):
            blocks = pl.ds(16 * half, 16)
            for n in range(2):
                columns = slice(256 * n, 256 * n + 256)
                change = mm(AQ[j], BQ[half, :, columns]).reshape(16, 16, 256)
                WQ[blocks, strip, columns] = (
                    WQ[blocks, strip, columns].astype(f32) + change).astype(bf16)

    def own_side(k):
        return lax.rem(me + T - 2 * k, T)

    def other_side(k):
        return lax.rem(sib + T - 2 * k, T)

    def pass_on_strips(k):
        j = own_side(k)
        wait(AQ.at[j], a3dsem.at[1, k])
        tensor_copy(AQ.at[j], AQ.at[j], a3fsem.at[0, k], a3fsem.at[1, k], sib).start()

    wait(KV, lsem.at[19])

    def part_cache(n):
        i, g = n // KV_HEADS, lax.rem(n, KV_HEADS)
        DI[...] = KV[i, g].reshape(2 * CAP, HEAD_DIM).astype(f32)
        KEYS[i, g] = DI[pl.ds(0, CAP, stride=2), :].astype(bf16)
        VALS[i, g] = DI[pl.ds(1, CAP, stride=2), :].astype(bf16)

    merge(me)
    loop(0, 4 * KV_HEADS, part_cache)
    loop(1, 8, pass_on_strips)
    loop(1, 8, lambda k: merge(own_side(k)))
    loop(0, 8, lambda k: wait(AQ.at[other_side(k)], a3fsem.at[1, k]))
    loop(0, 8, lambda k: merge(other_side(k)))

    low_half = lanes((8, 128)) < 64
    sub = lax.broadcasted_iota(jnp.int32, (8, 128), 0) & 3
    lengths = jnp.zeros((8, 128), jnp.int32)
    for i in range(4):
        lengths = jnp.where(sub == i, lens[i], lengths)
    wide = lanes((64, CAP))

    for s in range(STEPS):
        def project(j, q):
            return q + mm(NB[j], WQ[pl.ds(2 * j, 2)].reshape(CHUNK, CHUNK))

        if s == 0:
            q = lax.fori_loop(0, T, project, zero_query, unroll=8)
        for h in range(4):
            Q32[64 * h:64 * h + 64, :] = q[:, 128 * h:128 * h + 128]
        Q32[256:320, :] = new
        for t in range(T):
            QS[s, t] = Q32[pl.ds(t, 32, stride=16), :].astype(bf16)
        loop(1, T, lambda k: tensor_copy(
            QS.at[s, lax.rem(me + k, T)], QR.at[s, me], qsem.at[s, 0], qsem.at[s, 1],
            lax.rem(me + k, T)).start())
        QR[s, me] = QS[s, me]
        if s == 0:
            loop(1, T, lambda k: tensor_copy(
                AOS.at[lax.rem(me + k, T) // 2], AOR.at[me], aosem.at[0], aosem.at[1],
                lax.rem(me + k, T)).start())
            AOR[me] = AOS[chip]

        angles = (lengths + s).astype(f32) * freq[...]
        cosine = jnp.cos(angles)
        sine = jnp.where(low_half, -jnp.sin(angles), jnp.sin(angles))

        wait(QR.at[s, pl.ds(0, T - 1)], qsem.at[s, 1])
        got = QR[s].astype(f32)
        heads = got[:, 0:16].reshape(T, 2, 8, 128)
        heads = heads * cosine + swap_halves(heads) * sine
        QX[...] = heads.astype(bf16).astype(f32).reshape(256, 128)
        fresh = got[:, 16:24].reshape(8, 2, 8, 128)
        even, odd = fresh[:, 0], fresh[:, 1]
        low = lanes(even.shape) < 64
        key = jnp.where(low, even, swap_halves(odd))
        key = key * cosine + swap_halves(key) * sine
        KN[s] = key.astype(bf16).astype(f32).reshape(64, 128)
        VN[s] = jnp.where(low, swap_halves(even), odd).reshape(64, 128)


        def attend(i):
            queries = [QX[pl.ds(32 * g + i, 8, stride=4), :] for g in range(KV_HEADS)]
            scores = jnp.concatenate(
                [mm_t(queries[g].astype(bf16), KEYS[i, g])
                 for g in range(KV_HEADS)], axis=0) * score_scale
            scores = jnp.where(wide < lens[i], scores, -1e30)
            rows = jnp.concatenate(queries, axis=0)
            largest = jnp.max(scores, axis=1, keepdims=True)
            news, values = [], []
            for n in range(s + 1):
                k = KN[n, pl.ds(i, 8, stride=8), :]
                v = VN[n, pl.ds(i, 8, stride=8), :]
                k = jnp.broadcast_to(k[:, None, :], (8, 8, 128)).reshape(64, 128)
                values.append(jnp.broadcast_to(v[:, None, :], (8, 8, 128)).reshape(64, 128))
                news.append(jnp.sum(rows * k, axis=1, keepdims=True) * score_scale)
                largest = jnp.maximum(largest, news[-1])
            expo = jnp.exp(scores - largest)
            news = [jnp.exp(x - largest) for x in news]
            total = jnp.sum(expo, axis=1, keepdims=True)
            for x in news:
                total = total + x
            share = 1.0 / total
            weights = (expo * share).astype(bf16)
            result = jnp.concatenate(
                [mm(weights[8 * g:8 * g + 8], VALS[i, g])
                 for g in range(KV_HEADS)], axis=0)
            for x, v in zip(news, values):
                result = result + (x * share).astype(bf16).astype(f32) * v
            AF[pl.ds(i, 64, stride=4), :] = result

        for i in range(4):
            attend(i)
        AM[s] = AF[...].astype(bf16).reshape(8, 32, 128)
        loop(1, T, lambda k: tensor_copy(
            AM.at[s, lax.rem(me + k, T) // 2], AR.at[s, me], asem.at[s, 0], asem.at[s, 1],
            lax.rem(me + k, T)).start())
        AR[s, me] = AM[s, chip]
        if s == 0:
            wait(AOR.at[pl.ds(0, T - 1)], aosem.at[1])
            blocks = AOR[...].astype(f32).reshape(T, 4, 8, 128)
            for b in range(4):
                XF[128 * b:128 * b + 128, :] = blocks[:, b].reshape(128, 128)
            spread_pairs(XF[0:512, :], AOE)
            AO[...] = AOE[...].astype(bf16)
        wait(AR.at[s, pl.ds(0, T - 1)], asem.at[s, 1])
        XF[0:512, :] = AR[s].astype(f32).reshape(512, 128)
        for h in range(8):
            for i in range(4):
                AT[16 * i:16 * i + 16, 128 * h:128 * h + 128] = (
                    XF[pl.ds(4 * h + i, 16, stride=32), :].astype(bf16))

        attended = AT[...]
        if s == 0:
            wait(WO.at[:, pl.ds(0, CHUNK), :], lsem.at[18])
            wait(WO.at[:, pl.ds(0, CHUNK), :], wosem.at[1])

        halves = [slice(256 * half, 256 * half + 256) for half in range(2)]

        def send_parts(half):
            def part(k):
                q = lax.rem(chip + k, 8)
                RSS[s, half, q] = mm(AT[...], WO[q, :, halves[half]]).astype(bf16)
                tensor_copy(
                    RSS.at[s, half, q], RB.at[s, half, chip], rssem.at[s, half, 0],
                    rssem.at[s, half, 1], 2 * q + core).start()
            loop(1, 8, part)

        send_parts(0)
        t = mm(attended, AO[...])
        TOS[s] = pack_rank(t).astype(bf16)
        loop(1, 8, lambda k: tensor_copy(
            TOS.at[s], TOR.at[s, chip], tosem.at[s, 0], tosem.at[s, 1],
            lax.rem(me + 2 * k, T)).start())
        TOR[s, chip] = TOS[s]
        send_parts(1)
        bases = []
        for half in range(2):
            own = ST[me, :, halves[half]] if s == 0 else SG[me, half]
            bases.append(mm(attended, WO[chip, :, halves[half]]) + own.astype(f32))
        wait(TOR.at[s, pl.ds(0, 7)], tosem.at[s, 1])
        rank = unpack_split(jnp.sum(TOR[s].astype(f32), axis=0))
        parts = []
        for half in range(2):
            y = bases[half] + low_rank_scale * mm(rank, BO[:, halves[half]])
            RB[s, half, chip] = jnp.zeros((64, CHUNK // 2), bf16)
            wait(RB.at[s, half, pl.ds(0, 7)], rssem.at[s, half, 1])
            for q in range(8):
                y = y + RB[s, half, q].astype(f32)
            y = y.astype(bf16)
            parts.append(y)
            if s + 1 < STEPS:
                SG[me, half] = y
                if half == 1:
                    squares = [x.astype(f32) * x.astype(f32) for x in parts]
                    squares = (squares[0][:, 0:128] + squares[0][:, 128:256]) + (
                        squares[1][:, 0:128] + squares[1][:, 128:256])
                    SQS[...] = jnp.zeros_like(SQS)
                    SQS[0:1, 0:64] = jnp.sum(squares.T, axis=0, keepdims=True)
                    loop(1, T, lambda k: tensor_copy(
                        SQS, SQR.at[me], sqsem.at[0], sqsem.at[1], lax.rem(me + k, T)).start())
                loop(1, 8, lambda k: tensor_copy(
                    SG.at[me, half], SG.at[me, half], agdsem.at[0, half, k],
                    agdsem.at[1, half, k], lax.rem(me + 2 * k, T)).start())
                tensor_copy(
                    SG.at[me, half], SG.at[me, half], agfsem.at[0, half, 0],
                    agfsem.at[1, half, 0], sib).start()
        y = jnp.concatenate(parts, axis=1)
        yf = y.astype(f32)
        for c in range(4):
            for i in range(4):
                OUTF[c, pl.ds(i, 16, stride=4), :] = yf[16 * i:16 * i + 16, 128 * c:128 * c + 128]
        for c in range(4):
            out[s, :, 128 * c:128 * c + 128] = OUTF[c].astype(bf16)

        if s + 1 < STEPS:
            def pass_on_stream(half):
                def pass_on(k):
                    j = own_side(k)
                    wait(SG.at[j, half], agdsem.at[1, half, k])
                    tensor_copy(
                        SG.at[j, half], SG.at[j, half], agfsem.at[0, half, k],
                        agfsem.at[1, half, k], sib).start()
                loop(1, 8, pass_on)

            pass_on_stream(0)
            SQR[me] = SQS[...]
            wait(SQR.at[pl.ds(0, T - 1)], sqsem.at[1])
            total = jnp.sum(SQR[...], axis=0)[0:1]
            total = jnp.broadcast_to(total, (128, 128)).T[0:64, 0:1]
            inv = lax.rsqrt(total * (1.0 / D) + norm_epsilon)

            def take(j, half, carry):
                q, new = carry
                x = (SG[j, half].astype(f32) * inv * gain[j, :, halves[half]]).astype(bf16)
                columns = pl.ds(pl.multiple_of(CHUNK * j + 256 * half, 256), 256)
                return q + mm(x, WQ[2 * j + half]), new + mm_t(x, WKV[:, columns])

            carry = (zero_query, zero_total)
            for half in range(2):
                if half == 1:
                    pass_on_stream(1)
                carry = lax.fori_loop(
                    0, 8, lambda k, c: take(own_side(k), half, c), carry, unroll=4)
                loop(0, 8, lambda k: wait(SG.at[other_side(k), half], agfsem.at[1, half, k]))
                carry = lax.fori_loop(
                    0, 8, lambda k, c: take(other_side(k), half, c), carry, unroll=4)
            q, new = carry

    wait(A1R.at[pl.ds(0, 3)], a1sem.at[0, 0])
    wait(A1R.at[pl.ds(0, 4)], a1sem.at[0, 1])
    wait(WO.at[:, pl.ds(0, CHUNK), :], wosem.at[0])
    for half in range(2):
        wait(A2R.at[0, pl.ds(0, T - 1)], a2sem.at[half, 0])
    loop(1, 8, lambda k: wait(AQ.at[me], a3dsem.at[0, k]))
    loop(0, 8, lambda k: wait(AQ.at[me], a3fsem.at[0, k]))
    wait(AOR.at[pl.ds(0, T - 1)], aosem.at[0])
    for s in range(STEPS):
        wait(QR.at[s, pl.ds(0, T - 1)], qsem.at[s, 0])
        wait(AR.at[s, pl.ds(0, T - 1)], asem.at[s, 0])
        wait(TOR.at[s, pl.ds(0, 7)], tosem.at[s, 0])
        for half in range(2):
            wait(RB.at[s, half, pl.ds(0, 7)], rssem.at[s, half, 0])
    for half in range(2):
        loop(1, 8, lambda k: wait(SG.at[me, half], agdsem.at[0, half, k]))
        loop(0, 8, lambda k: wait(SG.at[me, half], agfsem.at[0, half, k]))
    wait(SQR.at[pl.ds(0, T - 1)], sqsem.at[0])


def body(
    hidden_in,
    norm_gain,
    query_weight_base,
    w_key,
    w_value,
    output_weight_base,
    kv_cache,
    cache_lengths,
    adapter_shards,
    shard_order,
):
    half_dim = HEAD_DIM // 2
    exponent = np.arange(half_dim, dtype=np.float32) * np.float32(2.0 / HEAD_DIM)
    frequency = np.float32(rope_theta) ** (-exponent)
    freq = jnp.asarray(np.concatenate([frequency, frequency]).reshape(1, HEAD_DIM))
    vmem = pl.BlockSpec(memory_space=pltpu.VMEM)
    smem = pl.BlockSpec(memory_space=pltpu.SMEM)
    hbm = pl.BlockSpec(memory_space=pl.ANY)
    V = pltpu.VMEM
    dma = pltpu.SemaphoreType.DMA
    return pl.pallas_call(
        kernel,
        out_shape=jax.ShapeDtypeStruct((STEPS, 64, CHUNK), bf16),
        in_specs=[vmem, vmem, hbm, hbm, hbm, hbm, hbm, smem, vmem, vmem, vmem],
        out_specs=vmem,
        scratch_shapes=[
            V((32, 256, CHUNK), bf16),
            V((128, D), bf16),
            V((8, 2 * CHUNK, CHUNK), bf16),
            V((4, KV_HEADS, CAP, 2, HEAD_DIM), bf16),
            V((4, 64, 128), f32),
            V((T, 64, CHUNK), bf16),
            V((T, 2, 64, CHUNK // 2), bf16),
            V((T, 64, CHUNK), bf16),
            V((128, 128), f32),
            V((128, 128), bf16),
            V((R, 128, 128), bf16),
            V((2, T, 32, 128), bf16),
            V((2, T, 32, 128), bf16),
            V((1024, 128), f32),
            V((T, 32, 128), f32),
            V((512, 128), f32),
            V((T, 256, 128), bf16),
            V((2, 128, CHUNK), bf16),
            V((128, CHUNK), bf16),
            V((8, 32, 128), bf16),
            V((T, 32, 128), bf16),
            V((1024, 128), f32),
            V((1024, 128), bf16),
            V((512, 128), f32),
            V((STEPS, T, 32, 128), bf16),
            V((STEPS, T, 32, 128), bf16),
            V((256, 128), f32),
            V((STEPS, 64, 128), f32),
            V((STEPS, 64, 128), f32),
            V((256, 128), f32),
            V((STEPS, 8, 32, 128), bf16),
            V((STEPS, T, 32, 128), bf16),
            V((64, 2 * CHUNK), bf16),
            V((STEPS, 32, 128), bf16),
            V((STEPS, 8, 32, 128), bf16),
            V((STEPS, 2, 8, 64, CHUNK // 2), bf16),
            V((STEPS, 2, 8, 64, CHUNK // 2), bf16),
            V((4, 64, 128), f32),
            V((8, 128), f32),
            V((T, 8, 128), f32),
            V((2 * CAP, HEAD_DIM), f32),
            V((4, KV_HEADS, CAP, HEAD_DIM), bf16),
            V((4, KV_HEADS, CAP, HEAD_DIM), bf16),
            dma((20,)),
            dma((2,)),
            dma((2, 2)),
            dma((2, 2)),
            dma((2, 8)),
            dma((2, 8)),
            dma((2,)),
            dma((STEPS, 2)),
            dma((STEPS, 2)),
            dma((STEPS, 2)),
            dma((STEPS, 2, 2)),
            dma((2, 2, 8)),
            dma((2, 2, 8)),
            dma((2,)),
        ],
        compiler_params=pltpu.CompilerParams(
            collective_id=0, has_side_effects=True, vmem_limit_bytes=56 * 2**20
        ),
        cost_estimate=pl.CostEstimate(
            flops=5 * 10**9, bytes_accessed=25 * 2**20, transcendentals=10**6
        ),
    )(
        hidden_in,
        norm_gain.reshape(T, 1, CHUNK),
        query_weight_base.reshape(32, 256, CHUNK),
        w_key.T,
        w_value.T,
        output_weight_base,
        kv_cache,
        cache_lengths,
        freq,
        adapter_shards,
        shard_order.reshape(1, 128),
    )


def solution(mesh):
    return jax.shard_map(
        body,
        mesh=mesh,
        in_specs=(
            P("rollout", None),
            P(),
            P(None, "tensor"),
            P(None, "tensor"),
            P(None, "tensor"),
            P("tensor", None),
            P(("rollout", "tensor"), None, None, None),
            P(("rollout", "tensor")),
            P(("rollout", "tensor"), None),
            P(),
        ),
        out_specs=P(None, "rollout", "tensor"),
        check_vma=False,
    )
```
